32 devices in a mesh: wide: 8 (over z, x), narrow: 4 (over y, core).
Axes of the slice: x: 2, y: 2, z: 4, core: 2. Of those that a mesh axis runs over, the one named last changes fastest.
Arguments:
- tokens: bfloat16 [17408, 384], P('wide'), may hold values from -6 to 6
- w_qkv: bfloat16 [384, 3, 384], replicated, may hold values from -0.3125 to 0.3125
- w_proj: bfloat16 [384, 384], replicated, may hold values from -1.25 to 1.25
- norm1_gain: float32 [384], replicated, may hold values from 0.25 to 1.75
- norm2_gain: float32 [384], replicated, may hold values from 0.25 to 1.75
- w_route: bfloat16 [384, 8], replicated, may hold values from -0.21875 to 0.21875
- w_in: bfloat16 [8, 384, 1536], P(None, None, 'narrow'), may hold values from -0.3125 to 0.3125
- w_out: bfloat16 [8, 1536, 384], P(None, 'narrow'), may hold values from -0.625 to 0.625
- cotangent: bfloat16 [17408, 384], P('wide'), may hold values from -6 to 6
- routes: int32 [17408, 1], P('wide'), may hold values from 0 to 7; in each aligned block of 2176 rows (0 to 2175, 2176 to 4351, ...) at most 408 rows name the same one
- kept_mask: int32 [17408], P('wide'), may hold values 0 or 1
- lengths: int32 [8, 8], P('wide'), may hold values from 1 to 1024, 2176 in all within a row
Outputs:
- layer_out: bfloat16 [17408, 384], P('wide')
- grad_tokens: bfloat16 [17408, 384], P('wide')
- grad_qkv: float32 [384, 3, 384], replicated
- grad_proj: float32 [384, 384], replicated
- grad_norm1: float32 [384], replicated
- grad_norm2: float32 [384], replicated
- grad_route: float32 [384, 8], replicated
- grad_in: float32 [8, 384, 1536], P(None, None, 'narrow')
- grad_out: float32 [8, 1536, 384], P(None, 'narrow')
The draws below stay inside these ranges and needn't reach their ends.
Inputs may be any that keep to these rules, and one draw needn't show every extreme that they name: `routes`: in each aligned block of 2176 rows (the rows of one index of wide) no expert is named by more than 408 rows, a bound that some block reaches. `lengths`: each row sums to 2176, and its longest sequence has exactly 1024 tokens.
All inputs are finite; a program needn't handle non-finite values. No bound on the sum of `kept_mask` on one device may be relied on, other than what follows from the above.
Results may differ from the reference program's by a relative error of at most 0.019.
Values may be sent and summed in bfloat16 or wider, within the bound.
No kernel may reach another device: no remote copies, remote signals or barrier semaphores. Data moves between devices by JAX's collectives and lax.ppermute only.
A program may use at most 192 MiB of HBM per device.

```python
import math
import jax
import jax.numpy as jnp
import numpy as np
from jax import lax

D = 384
HEADS = 6
FF = 1536
EXPERTS = 8
TOK_DEV = 2176
SEQS_DEV = 8
LONGEST = 1024
CAP = 408
TOKENS = 17408
N_WIDE = 8


def place_ends(array, own_key, least, high):
    shape = array.shape
    index_at = [jax.random.randint(jax.random.fold_in(own_key, axis), (), 0, shape[axis]) for axis in range(len(shape))]
    array = array.at[tuple(index_at)].set(least)
    longest = shape.index(max(shape))
    index_at[longest] = (index_at[longest] + 1) % shape[longest]
    return array.at[tuple(index_at)].set(high)


def levels(key, shape, pieces, least, high):
    loudness, own = 1.0, jax.random.fold_in(key, 6)
    for axis_at, shards_of in pieces:
        heights = jnp.exp(jax.random.uniform(jax.random.fold_in(own, axis_at), (shards_of,), jnp.float32, least / len(pieces), high / len(pieces)))
        loudness = loudness * jnp.repeat(heights, shape[axis_at] // shards_of).reshape([-1 if axis == axis_at else 1 for axis in range(len(shape))])
    return loudness


def profile(count, total, bound, skew):
    weights = [(1 << 20) // math.isqrt(standing ** skew) + 1 for standing in range(2, count + 1)]
    spare, counts = total - bound - (count - 1), [1] * (count - 1)
    while spare > 0:
        movable = [i for i in range(count - 1) if counts[i] < bound]
        whole, remaining = sum([weights[i] for i in movable]), spare
        for i in movable:
            addition = min(bound - counts[i], max(1, remaining * weights[i] // whole), spare)
            counts[i] = counts[i] + addition
            spare = spare - addition
    return np.array([bound] + counts)


def ragged_sizes(own_key, number_of, total, most, slope):
    if number_of == 2:
        one = jax.random.randint(own_key, (), max(1, total - most), min(most, total - 1) + 1)
        return jnp.stack([one, total - one])
    sizes = jnp.asarray(profile(number_of, total, most, slope), jnp.int32)
    couples = (number_of - 1) // 2
    source_of, taker = sizes[1:1 + 2 * couples:2], sizes[2:2 + 2 * couples:2]
    margin = jnp.minimum(source_of - 1, most - taker)
    passed = jax.random.randint(jax.random.fold_in(own_key, 1), (couples,), 0, 1 << 20) % (margin + 1)
    sizes = sizes.at[1:1 + 2 * couples:2].set(source_of - passed).at[2:2 + 2 * couples:2].set(taker + passed)
    return sizes[jax.random.permutation(jax.random.fold_in(own_key, 2), number_of)]


def routed_block(rng, own, number, rows, amount, top, limit, lean):
    order = jax.random.permutation(rng, amount)
    crowded, ordinary = load_shares(amount, rows * top, limit, lean, True), load_shares(amount, rows * top, limit, lean, False)
    places = jnp.arange(amount)

    def named(sizes, turn):
        used = int((sizes > 0).sum())
        fixed = max(1, used // 4)
        moved = fixed + (places - fixed + turn * (used - fixed)) % max(1, amount - fixed)
        return jnp.zeros((amount,), jnp.int32).at[order[jnp.where(places < fixed, places, moved)]].set(jnp.asarray(sizes, jnp.int32))

    sizes = jnp.where(number % 4 == 0, named(crowded, number // 4), named(ordinary, number - number // 4 - 1))
    mixed = jax.random.permutation(jax.random.fold_in(own, 3), amount)
    source_of, sink = mixed[0:amount // 2 * 2:2], mixed[1:amount // 2 * 2:2]
    margin = jnp.minimum(sizes[source_of] - 1, limit - sizes[sink]) // 2
    margin = jnp.where((source_of == order[0]) | (sink == order[0]) | (sizes[sink] == 0), 0, jnp.maximum(margin, 0))
    moved = jax.random.randint(jax.random.fold_in(own, 4), (amount // 2,), 0, 1 << 20) % (margin + 1)
    sizes = sizes.at[source_of].add(-moved).at[sink].add(moved)
    labels = jnp.searchsorted(jnp.cumsum(sizes), jnp.arange(rows * top), side="right").astype(jnp.int32)
    table = labels.reshape(top, rows).T
    table = table[jax.random.permutation(jax.random.fold_in(own, 1), rows)]
    turn = jax.random.randint(jax.random.fold_in(own, 2), (rows, 1), 0, top)
    return jnp.take_along_axis(table, (jnp.arange(top)[None, :] + turn) % top, axis=1)


def load_shares(number_of, total, reach, skew, full):
    loads = [(1 << 20) // math.isqrt(rank ** skew) + 1 for rank in range(1, number_of + 1)]
    largest = reach if full else min(reach, max(-(-total // number_of), total * loads[0] // sum(loads)))
    least = 1 if total - largest >= number_of - 1 else 0
    holding, surplus = [largest] + [least] * (number_of - 1), total - largest - least * (number_of - 1)
    while surplus > 0:
        candidates = [i for i in range(1, number_of) if holding[i] < largest] or [i for i in range(1, number_of) if holding[i] < reach]
        pool, left = sum([loads[i] for i in candidates]), surplus
        for i in candidates:
            addition = min(reach - holding[i], max(1, left * loads[i] // pool), surplus)
            holding[i] = holding[i] + addition
            surplus = surplus - addition
    return np.array(holding)


def bell_draw(own_key, dims, scale, bound, cuts=(), held_as=jnp.bfloat16):
    gain = levels(own_key, dims, cuts, -0.22, 0.18) if cuts else 1.0
    entries = jax.random.normal(own_key, dims, jnp.float32) * scale * gain
    return jnp.minimum(jnp.maximum(entries, -bound), bound).astype(held_as)


def setup_inputs(seed: int = 0) -> dict:
    streams_of = jax.random.split(jax.random.key(seed), 13)
    tokens = bell_draw(streams_of[0], (TOKENS, D), 1.0, 6.0, ((0, 8),))
    w_qkv = bell_draw(streams_of[1], (D, 3, D), D ** -0.5, 0.3125)
    w_proj = bell_draw(streams_of[2], (D, D), (D // 16) ** -0.5, 1.25)
    norm1_gain = jnp.clip(1.0 + 0.15 * jax.random.normal(streams_of[3], (D,), jnp.float32), 0.25, 1.75)
    norm2_gain = jnp.clip(1.0 + 0.15 * jax.random.normal(streams_of[4], (D,), jnp.float32), 0.25, 1.75)
    w_route = bell_draw(streams_of[5], (D, EXPERTS), (2 * D) ** -0.5, 0.21875)
    w_in = bell_draw(streams_of[6], (EXPERTS, D, FF), D ** -0.5, 0.3125, ((2, 4),))
    w_out = bell_draw(streams_of[7], (EXPERTS, FF, D), (FF // 16) ** -0.5, 0.625, ((1, 4),))
    cotangent = bell_draw(streams_of[8], (TOKENS, D), 1.0, 6.0, ((0, 8),))
    routes_keys = jax.random.split(jax.random.fold_in(streams_of[9], 1), TOKENS // TOK_DEV)
    routes_turns = jax.random.permutation(jax.random.fold_in(streams_of[9], 3), TOKENS // TOK_DEV)
    routes = jax.vmap(lambda own, number: routed_block(jax.random.fold_in(streams_of[9], 2), own, number, TOK_DEV, EXPERTS, 1, CAP, 2))(routes_keys, routes_turns).reshape((TOKENS, 1))
    kept_mask = place_ends((jax.random.randint(streams_of[10], (TOKENS,), 0, 8) < 7).astype(jnp.int32), jax.random.fold_in(streams_of[10], 1), 0, 1)
    lengths = jax.vmap(lambda own: ragged_sizes(own, SEQS_DEV, TOK_DEV, LONGEST, 2))(jax.random.split(streams_of[11], N_WIDE)).reshape((N_WIDE, SEQS_DEV)).astype(jnp.int32)
    return dict(tokens=tokens, w_qkv=w_qkv, w_proj=w_proj, norm1_gain=norm1_gain, norm2_gain=norm2_gain, w_route=w_route, w_in=w_in, w_out=w_out, cotangent=cotangent, routes=routes, kept_mask=kept_mask, lengths=lengths)


EPS = 1e-06
HIGHEST = lax.Precision.HIGHEST

@jax.custom_vjp
def low(v):
    return lax.optimization_barrier(v.astype(jnp.bfloat16)).astype(jnp.float32)

@jax.custom_vjp
def low_back(v):
    return v

def low_keep(v):
    return (low(v), None)

def low_pass(kept, grad):
    return (grad,)

def back_keep(v):
    return (v, None)

def back_low(kept, grad):
    return (low(grad),)
low.defvjp(low_keep, low_pass)
low_back.defvjp(back_keep, back_low)

def normalize(values, gain_row):
    centre = values - lax.optimization_barrier(jnp.mean(values, -1, keepdims=True))
    return centre * lax.rsqrt(lax.optimization_barrier(jnp.mean(centre * centre, -1, keepdims=True)) + EPS) * gain_row

def segment_ids(lengths_row, row_count):
    seq_ends = jnp.cumsum(lengths_row)
    places = jnp.arange(row_count, dtype=jnp.int32)
    return lax.optimization_barrier(jnp.sum((places[:, None] >= seq_ends[None, :]).astype(jnp.int32), -1))

def dispatch_plan(route_ids, keep_ids, experts_all, capacity):
    row_count = route_ids.shape[0]
    places = jnp.arange(row_count, dtype=jnp.int32)
    member = (route_ids[:, None] == jnp.arange(experts_all, dtype=jnp.int32)[None, :]).astype(jnp.int32) * keep_ids[:, None]
    before = jnp.cumsum(member, 0) - 1
    within = lax.optimization_barrier(jnp.sum(member * before, -1))
    slots_all = experts_all * capacity
    target = jnp.where(keep_ids == 1, route_ids * capacity + within, slots_all).astype(jnp.int32)
    source = jnp.zeros((slots_all,), jnp.int32).at[target].set(places, mode='drop')
    filled = jnp.zeros((slots_all,), jnp.float32).at[target].set(1.0, mode='drop')
    clamped = jnp.minimum(target, slots_all - 1).astype(jnp.int32)
    return (clamped, source, filled)

def layer_block(params, block_data):
    w_qkv, w_proj, norm1_gain, norm2_gain, w_route, w_in, w_out = params
    inputs, route_ids, keep_ids, lengths_row = block_data
    row_count = inputs.shape[0]
    head_width = D // HEADS
    score_scale = 1.0 / math.sqrt(head_width)
    hidden1 = low(normalize(inputs, norm1_gain))
    qkv_rows = low_back(low(jnp.dot(hidden1, w_qkv.reshape(D, 3 * D), precision=HIGHEST)))
    qkv_rows = qkv_rows.reshape(row_count, 3, HEADS, head_width)
    queries = qkv_rows[:, 0]
    key_rows = qkv_rows[:, 1]
    val_rows = qkv_rows[:, 2]
    segment = segment_ids(lengths_row, row_count)
    blocks = max(1, row_count // 512)
    rows_block = row_count // blocks

    def attend(block_part):
        query_block, segment_block = block_part
        scores = jnp.einsum('bhk,thk->hbt', query_block, key_rows, precision=HIGHEST) * score_scale
        scores = low_back(scores)
        same_seq = segment_block[:, None] == segment[None, :]
        scores = jnp.where(same_seq[None], scores, -jnp.inf)
        row_max = lax.optimization_barrier(jnp.max(scores, -1, keepdims=True))
        log_total = row_max + jnp.log(lax.optimization_barrier(jnp.sum(jnp.exp(scores - row_max), -1, keepdims=True)))
        prob_rows = low(jnp.exp(scores - log_total))
        return jnp.einsum('hbt,thk->bhk', prob_rows, val_rows, precision=HIGHEST)
    attended = lax.map(jax.checkpoint(attend), (queries.reshape(blocks, rows_block, HEADS, head_width), segment.reshape(blocks, rows_block)))
    attended = low_back(low(attended.reshape(row_count, D)))
    attn_sum = low_back(jnp.dot(attended, w_proj, precision=HIGHEST))
    mid_rows = inputs + attn_sum
    hidden2 = low(normalize(mid_rows, norm2_gain))
    logits = jnp.dot(hidden2, w_route, precision=HIGHEST)
    gate_all = jax.nn.softmax(logits, -1)
    chosen = (route_ids[:, None] == jnp.arange(EXPERTS, dtype=jnp.int32)[None, :]).astype(jnp.float32)
    gate_prob = lax.optimization_barrier(jnp.sum(gate_all * chosen, -1))
    clamped, source, filled = dispatch_plan(route_ids, keep_ids, EXPERTS, CAP)
    sent_rows = (hidden2[source] * filled[:, None]).reshape(EXPERTS, CAP, D)
    pre_act = low_back(jnp.einsum('ecd,edf->ecf', sent_rows, w_in, precision=HIGHEST))
    active = low(jax.nn.gelu(pre_act, approximate=True))
    back_rows = jnp.einsum('ecf,efd->ecd', active, w_out, precision=HIGHEST).reshape(EXPERTS * CAP, D)
    keep_float = keep_ids.astype(jnp.float32)
    expert = low_back(back_rows[clamped] * keep_float[:, None])
    return mid_rows + (gate_prob * keep_float)[:, None] * expert

def reference(tokens, w_qkv, w_proj, norm1_gain, norm2_gain, w_route, w_in, w_out, cotangent, routes, kept_mask, lengths):
    params = (w_qkv.astype(jnp.float32), w_proj.astype(jnp.float32), norm1_gain.astype(jnp.float32), norm2_gain.astype(jnp.float32), w_route.astype(jnp.float32), w_in.astype(jnp.float32), w_out.astype(jnp.float32))
    inputs = tokens.astype(jnp.float32).reshape(N_WIDE, TOK_DEV, D)
    routed = routes[:, 0].reshape(N_WIDE, TOK_DEV)
    kept_rows = kept_mask.reshape(N_WIDE, TOK_DEV)

    def forward(block_inputs, weights):

        def scan_step(carried, block_data):
            return (carried, layer_block(weights, block_data))
        unused, outputs = lax.scan(jax.checkpoint(scan_step), jnp.zeros((), jnp.float32), (block_inputs, routed, kept_rows, lengths))
        return outputs
    outputs, pullback = jax.vjp(forward, inputs, params)
    grad_inputs, grads = pullback(cotangent.astype(jnp.float32).reshape(N_WIDE, TOK_DEV, D))
    return (outputs.reshape(TOKENS, D).astype(jnp.bfloat16), grad_inputs.reshape(TOKENS, D).astype(jnp.bfloat16), grads[0], grads[1], grads[2], grads[3], grads[4], grads[5], grads[6])
```

```python
import math

import jax
import jax.numpy as jnp
from jax import lax
from jax.experimental import pallas as pl
from jax.experimental.pallas import tpu as pltpu
from jax.sharding import PartitionSpec as P

HEADS = 6
CAP = 408
EPS = 1e-06
NEG = -1e30
F32 = jnp.float32
BF16 = jnp.bfloat16
LANES = 128
KB = 256
GRAIN = 16
VMEM_LIMIT = 60 * 1024 * 1024
GELU_A = math.sqrt(2.0 / math.pi)
GELU_B = 0.044715

ROWS_COLS = (((1,), (0,)), ((), ()))
COLS_COLS = (((1,), (1,)), ((), ()))
ROWS_ROWS = (((0,), (0,)), ((), ()))


def up(value, grain):
    return -(-value // grain) * grain


def mm(a, b, dims=ROWS_COLS):
    return lax.dot_general(a, b, dims, preferred_element_type=F32)


def normalize_rows(values):
    centre = values - jnp.mean(values, -1, keepdims=True)
    row_scale = lax.rsqrt(jnp.mean(centre * centre, -1, keepdims=True) + EPS)
    return centre * row_scale, row_scale


def normal_back(grad_h, normed, row_scale, gain_row):
    g = grad_h * gain_row
    return row_scale * (
        g - jnp.mean(g, -1, keepdims=True) - normed * jnp.mean(g * normed, -1, keepdims=True)
    )


def q_blocks(half):
    blocks = []
    first = 0
    while first < half:
        left = half - first
        lanes = KB if left >= KB else up(left, LANES)
        blocks.append((first, lanes, min(lanes, left)))
        first += lanes
    return blocks


def load_rows(ref, base, first, lanes, valid):
    start = pl.multiple_of(base + first, GRAIN)
    rows = ref[pl.ds(start, valid), :]
    if valid < lanes:
        rows = jnp.concatenate([rows, jnp.zeros((lanes - valid, rows.shape[1]), rows.dtype)], 0)
    return rows


def seq_ends(len_ref, count):
    ends = []
    total = jnp.int32(0)
    for j in range(count):
        total = total + len_ref[0, j]
        ends.append(total)
    return ends


def seq_bounds(ends, first_row, last_row):
    low = jnp.int32(0)
    high = ends[-1]
    for end in ends:
        low = jnp.where(end <= first_row, end, low)
    for end in reversed(ends):
        high = jnp.where(end > last_row, end, high)
    return low, high


def segment_of(index, ends):
    seg = jnp.zeros(index.shape, jnp.int32)
    for end in ends:
        seg = seg + (index >= end).astype(jnp.int32)
    return seg


def key_segments(segk_ref, ends, kpad):
    def body(i, carry):
        start = pl.multiple_of(i * KB, KB)
        index = lax.broadcasted_iota(jnp.int32, (KB, LANES), 0) + start
        segk_ref[pl.ds(start, KB), :] = segment_of(index, ends)
        return carry

    lax.fori_loop(0, kpad // KB, body, 0)


def query_segments(base, first, lanes, valid, ends):
    lane = lax.broadcasted_iota(jnp.int32, (8, lanes), 1)
    seg = segment_of(lane + (base + first), ends)
    return jnp.where(lane < valid, seg, -1)[0:1]


def bias_block(segk_ref, kstart, segq, lanes):
    segk = segk_ref[pl.ds(kstart, KB), :]
    if lanes > LANES:
        segk = jnp.concatenate([segk] * (lanes // LANES), 1)
    return jnp.where(segk == segq, 0.0, NEG)


def head_mask(rows, odd):
    lane = lax.broadcasted_iota(jnp.int32, (rows, LANES), 1)
    return ((lane >= 64) if odd else (lane < 64)).astype(BF16)


def plan_of(code_row, experts):
    n = code_row.shape[1]
    sub = lax.broadcasted_iota(jnp.int32, (experts, n), 0)
    lane = lax.broadcasted_iota(jnp.int32, (experts, n), 1)
    member = (code_row == sub).astype(F32)
    rank = member
    shift = 1
    while shift < n:
        rank = rank + jnp.where(lane >= shift, pltpu.roll(rank, shift, 1), 0.0)
        shift *= 2
    counts = jnp.broadcast_to(rank[:, n - 1 : n], (experts, LANES))
    sizes = jnp.floor((counts + (GRAIN - 1)) * (1.0 / GRAIN)) * GRAIN
    row = lax.broadcasted_iota(jnp.int32, (experts, LANES), 0)
    total = sizes
    shift = 1
    while shift < experts:
        total = total + jnp.where(row >= shift, pltpu.roll(total, shift, 0), 0.0)
        shift *= 2
    offsets = total - sizes
    pos = jnp.sum(member * (rank + offsets[:, 0:1]), 0, keepdims=True) - 1.0
    return pos, offsets, sizes


def front_kernel(
    len_ref, where_ref, tok_ref, wqkv_ref, wproj_ref, gain1_ref, gain2_ref, wr_ref, cot_ref, code_ref,
    sorted_ref, hid_ref, k_ref, kt_ref, v_ref, q_ref, ho_ref, hot_ref, lse_ref, mid_ref, pos_ref, plan_ref,
    vt_s, segk_s, qm_s, acc_s, m_s, l_s, x_s,
):
    rows, width = tok_ref.shape
    own = rows // 2
    half = own // 2
    hpad = up(half, LANES)
    kpad = hid_ref.shape[0]
    experts = 8
    core = where_ref[0]
    ends = seq_ends(len_ref, len_ref.shape[1])
    scale = 1.0 / math.sqrt(width // HEADS)

    pos, offsets, sizes = plan_of(code_ref[core], experts)
    other_pos, other_offsets, other_sizes = plan_of(code_ref[1 - core], experts)
    pos_ref[...] = jnp.broadcast_to(pos, pos_ref.shape)
    plan_ref[0:8, :] = offsets.astype(jnp.int32)
    plan_ref[8:16, :] = sizes.astype(jnp.int32)
    plan_ref[16:24, :] = other_offsets.astype(jnp.int32)
    plan_ref[24:32, :] = other_sizes.astype(jnp.int32)

    key_segments(segk_s, ends, kpad)
    gain1 = gain1_ref[...]
    step = rows // 8
    wk = wqkv_ref[:, width : 2 * width]
    wv = wqkv_ref[:, 2 * width :]

    def norm_body(i, carry):
        start = pl.multiple_of(i * step, GRAIN)
        normed, unused = normalize_rows(tok_ref[pl.ds(start, step), :].astype(F32))
        hid = (normed * gain1).astype(BF16)
        hid_ref[pl.ds(start, step), :] = hid
        k_ref[pl.ds(start, step), :] = mm(hid, wk).astype(BF16)
        v_ref[pl.ds(start, step), :] = mm(hid, wv).astype(BF16)
        return carry

    lax.fori_loop(0, 8, norm_body, 0)
    if kpad > rows:
        for ref in (hid_ref, k_ref, v_ref):
            ref[rows:kpad, :] = jnp.zeros((kpad - rows, width), BF16)
    wkt = wk.T
    wvt = wv.T

    def key_body(i, carry):
        start = pl.multiple_of(i * KB, KB)
        hid = hid_ref[pl.ds(start, KB), :]
        kt_ref[:, pl.ds(start, KB)] = mm(wkt, hid, COLS_COLS).astype(BF16)
        vt_s[:, pl.ds(start, KB)] = mm(wvt, hid, COLS_COLS).astype(BF16)
        return carry

    lax.fori_loop(0, kpad // KB, key_body, 0)

    for part in range(2):
        base = core * own + part * half
        for first, lanes, valid in q_blocks(half):
            hid = load_rows(hid_ref, base, first, lanes, valid)
            q = (mm(hid, wqkv_ref[:, 0:width]).astype(BF16).astype(F32) * scale).astype(BF16)
            q_ref[part, first : first + lanes, :] = q
            for h in range(HEADS):
                pair = q[:, (h // 2) * LANES : (h // 2 + 1) * LANES]
                qm_s[h, 0:lanes, :] = pair * head_mask(lanes, h % 2)
            m_s[...] = jnp.full(m_s.shape, NEG, F32)
            l_s[...] = jnp.zeros(l_s.shape, F32)
            acc_s[...] = jnp.zeros(acc_s.shape, F32)
            low, high = seq_bounds(ends, base + first, base + first + valid - 1)
            segq = query_segments(base, first, lanes, valid, ends)

            def key_step(kb, carry, lanes=lanes, segq=segq):
                kstart = pl.multiple_of(kb * KB, KB)
                bias = bias_block(segk_s, kstart, segq, lanes)
                for h in range(HEADS):
                    kblk = k_ref[pl.ds(kstart, KB), (h // 2) * LANES : (h // 2 + 1) * LANES]
                    s = mm(kblk, qm_s[h, 0:lanes, :], COLS_COLS) + bias
                    m_old = m_s[h : h + 1, 0:lanes]
                    m_new = jnp.maximum(m_old, jnp.max(s, 0, keepdims=True))
                    p = jnp.exp(s - m_new)
                    alpha = jnp.exp(m_old - m_new)
                    m_s[h : h + 1, 0:lanes] = m_new
                    l_s[h : h + 1, 0:lanes] = l_s[h : h + 1, 0:lanes] * alpha + jnp.sum(p, 0, keepdims=True)
                    vblk = vt_s[h * 64 : (h + 1) * 64, pl.ds(kstart, KB)]
                    acc_s[h * 64 : (h + 1) * 64, 0:lanes] = acc_s[
                        h * 64 : (h + 1) * 64, 0:lanes
                    ] * alpha + mm(vblk, p.astype(BF16))
                return carry

            lax.fori_loop(low // KB, (high + KB - 1) // KB, key_step, 0)
            lse_ref[part, :, first : first + lanes] = m_s[:, 0:lanes] + jnp.log(
                jnp.maximum(l_s[:, 0:lanes], 1e-30)
            )
            for h in range(HEADS):
                inv = 1.0 / l_s[h : h + 1, 0:lanes]
                acc_s[h * 64 : (h + 1) * 64, 0:lanes] = acc_s[h * 64 : (h + 1) * 64, 0:lanes] * inv
            heads_t = acc_s[:, 0:lanes]
            hot_ref[part, :, first : first + lanes] = heads_t.astype(BF16)
            heads = heads_t.T.astype(BF16)
            ho_ref[part, first : first + lanes, :] = heads
            mid = load_rows(tok_ref, base, first, lanes, valid).astype(F32) + mm(heads, wproj_ref[...])
            mid_ref[part, first : first + lanes, :] = mid
            normed2, unused = normalize_rows(mid)
            hidden2 = (normed2 * gain2_ref[...]).astype(BF16)
            lane = lax.broadcasted_iota(jnp.int32, (lanes, LANES), 1)
            gates = router_gates(hidden2, wr_ref[...], lane, experts)
            at = part * hpad + first
            code_col = jnp.broadcast_to(code_ref[core][:, at : at + lanes].astype(F32), (LANES, lanes)).T
            gate = jnp.sum(jnp.where(code_col == lane.astype(F32), gates, 0.0), -1, keepdims=True)
            grad_final = load_rows(cot_ref, base, first, lanes, valid).astype(F32)
            x_s[at : at + lanes, 0:width] = hidden2
            x_s[at : at + lanes, width:] = (gate * grad_final).astype(BF16)

    count = sorted_ref.shape[0]
    piece = count // 4
    for i in range(4):
        sub = lax.broadcasted_iota(jnp.int32, (piece, 2 * hpad), 0) + i * piece
        pick = jnp.where(sub.astype(F32) == pos, 1.0, 0.0).astype(BF16)
        sorted_ref[i * piece : (i + 1) * piece, :] = mm(pick, x_s[...]).astype(BF16)


def router_gates(hidden2, wr, lane, experts):
    logits = jnp.where(lane < experts, mm(hidden2, wr), NEG)
    top = jnp.max(logits, -1, keepdims=True)
    e = jnp.exp(logits - top)
    return e / jnp.sum(e, -1, keepdims=True)


def call(kernel, outs, scratch, name, flops, **more):
    return pl.pallas_call(
        kernel,
        out_shape=outs,
        scratch_shapes=scratch,
        name=name,
        compiler_params=pltpu.CompilerParams(vmem_limit_bytes=VMEM_LIMIT),
        cost_estimate=pl.CostEstimate(flops=flops, bytes_accessed=flops // 300, transcendentals=0),
        **more,
    )


SMEM_SPEC = pl.BlockSpec(memory_space=pltpu.SMEM)
VMEM_SPEC = pl.BlockSpec(memory_space=pltpu.VMEM)


def sds(shape, dtype):
    return jax.ShapeDtypeStruct(shape, dtype)


def run_front(lengths, where, tokens, wqkv, wproj, gain1, gain2, wr, cot, code):
    rows, width = tokens.shape
    own, half = rows // 2, rows // 4
    hpad = up(half, LANES)
    kpad = up(rows, KB)
    count = up(own + 8 * (GRAIN - 1), 4 * GRAIN)
    outs = (
        sds((count, 2 * width), BF16),
        sds((kpad, width), BF16),
        sds((kpad, width), BF16),
        sds((width, kpad), BF16),
        sds((kpad, width), BF16),
        sds((2, hpad, width), BF16),
        sds((2, hpad, width), BF16),
        sds((2, width, hpad), BF16),
        sds((2, 8, hpad), F32),
        sds((2, hpad, width), F32),
        sds((8, 2 * hpad), F32),
        sds((32, LANES), jnp.int32),
    )
    scratch = [
        pltpu.VMEM((width, kpad), BF16),
        pltpu.VMEM((kpad, LANES), jnp.int32),
        pltpu.VMEM((HEADS, KB, LANES), BF16),
        pltpu.VMEM((width, KB), F32),
        pltpu.VMEM((8, KB), F32),
        pltpu.VMEM((8, KB), F32),
        pltpu.VMEM((2 * hpad, 2 * width), BF16),
    ]
    return call(
        front_kernel, outs, scratch, "front", 12 * 10**9,
        in_specs=[SMEM_SPEC, SMEM_SPEC] + [VMEM_SPEC] * 8,
    )(lengths, where, tokens, wqkv, wproj, gain1, gain2, wr, cot, code)


def expert_kernel(
    plan_ref, where_ref, own_ref, oth_ref, win_ref, wout_ref, wr_ref,
    yown_ref, yoth_ref, ka_ref, sa_ref, kb_ref, sb_ref, kc_ref, sc_ref, groute_ref,
    x_s, y_s,
):
    e = pl.program_id(0)
    width = win_ref.shape[1]
    most = x_s.shape[0]

    @pl.when(e == 0)
    def _():
        yown_ref[...] = jnp.zeros(yown_ref.shape, BF16)
        yoth_ref[...] = jnp.zeros(yoth_ref.shape, BF16)
        groute_ref[...] = jnp.zeros(groute_ref.shape, F32)

    own_at, own_size = plan_ref[e, 0], plan_ref[8 + e, 0]
    oth_at, oth_size = plan_ref[16 + e, 0], plan_ref[24 + e, 0]
    total = own_size + oth_size

    def move(dst, dst_at, src, src_at, size):
        def body(i, carry):
            a = pl.multiple_of(dst_at + i * GRAIN, GRAIN)
            b = pl.multiple_of(src_at + i * GRAIN, GRAIN)
            dst[pl.ds(a, GRAIN), :] = src[pl.ds(b, GRAIN), :]
            return carry

        lax.fori_loop(0, size // GRAIN, body, 0)

    move(x_s, 0, own_ref, own_at, own_size)
    move(x_s, own_size, oth_ref, oth_at, oth_size)

    def work(m):
        def zero_body(i, carry):
            x_s[pl.ds(pl.multiple_of(i * GRAIN, GRAIN), GRAIN), :] = jnp.zeros((GRAIN, 2 * width), BF16)
            return carry

        lax.fori_loop(total // GRAIN, m // GRAIN, zero_body, 0)
        h = x_s[0:m, 0:width]
        g = x_s[0:m, width:]
        w_in = win_ref[0]
        w_out = wout_ref[0]
        lane = lax.broadcasted_iota(jnp.int32, (m, LANES), 1)
        gates = router_gates(h, wr_ref[...], lane, 8)
        here = (lane == e).astype(F32)
        pre = mm(h, w_in)
        t = jnp.tanh(GELU_A * (pre + GELU_B * (pre * pre * pre)))
        act = (0.5 * pre * (1.0 + t)).astype(BF16)
        slope = 0.5 * (1.0 + t) + 0.5 * pre * (1.0 - t * t) * (GELU_A * (1.0 + 3.0 * GELU_B * (pre * pre)))
        out = mm(act, w_out)
        grad_pre = (mm(g, w_out, COLS_COLS) * slope).astype(BF16)
        dot = jnp.sum(g.astype(F32) * out, -1, keepdims=True)
        grad_logits = (dot * (here - gates)).astype(BF16)
        gate = jnp.sum(gates * here, -1, keepdims=True)
        y_s[0:m, 0:width] = (mm(grad_pre, w_in, COLS_COLS) + mm(grad_logits, wr_ref[...], COLS_COLS)).astype(BF16)
        y_s[0:m, width:] = (gate * out).astype(BF16)
        ht = h.T
        groute_ref[...] += mm(ht, grad_logits)
        grad_in = mm(ht, grad_pre).astype(BF16)
        grad_out = mm(act.T, g).astype(BF16)

        def put(keep_ref, send_ref, side):
            @pl.when(side == 0)
            def _():
                keep_ref[0] = grad_in
                send_ref[0] = grad_out

            @pl.when(side != 0)
            def _():
                keep_ref[0] = grad_out
                send_ref[0] = grad_in

        @pl.when(e < 3)
        def _():
            put(ka_ref, sa_ref, where_ref[2])

        @pl.when((e >= 3) & (e < 6))
        def _():
            put(kb_ref, sb_ref, where_ref[3])

        @pl.when(e >= 6)
        def _():
            put(kc_ref, sc_ref, where_ref[4])

    small = up(CAP * 2 // 3, GRAIN)

    @pl.when(total <= small)
    def _():
        work(small)

    @pl.when(total > small)
    def _():
        work(most)

    move(yown_ref, own_at, y_s, 0, own_size)
    move(yoth_ref, oth_at, y_s, own_size, oth_size)


def run_experts(plan, where, own, oth, w_in, w_out, wr):
    experts, width, hidden = w_in.shape
    count = own.shape[0]
    most = (CAP + 2 * (GRAIN - 1)) // GRAIN * GRAIN
    whole = lambda shape: pl.BlockSpec(shape, lambda e: (0,) * len(shape))
    part = lambda first, size: pl.BlockSpec(
        (1, width, hidden), lambda e: (jnp.clip(e - first, 0, size - 1), 0, 0)
    )
    parts = ((0, 3), (3, 3), (6, 2))
    outs = [sds((count, 2 * width), BF16)] * 2
    out_specs = [whole((count, 2 * width))] * 2
    for first, size in parts:
        outs += [sds((size, width, hidden), BF16)] * 2
        out_specs += [part(first, size)] * 2
    outs.append(sds((width, LANES), F32))
    out_specs.append(whole((width, LANES)))
    return call(
        expert_kernel,
        tuple(outs),
        [pltpu.VMEM((most, 2 * width), BF16), pltpu.VMEM((most, 2 * width), BF16)],
        "experts",
        10 * 10**9,
        grid=(experts,),
        in_specs=[
            SMEM_SPEC,
            SMEM_SPEC,
            whole(own.shape),
            whole(oth.shape),
            pl.BlockSpec((1, width, hidden), lambda e: (e, 0, 0)),
            pl.BlockSpec((1, hidden, width), lambda e: (e, 0, 0)),
            whole(wr.shape),
        ],
        out_specs=tuple(out_specs),
    )(plan, where, own, oth, w_in, w_out, wr)


def unsort_kernel(where_ref, mine_ref, got_ref, pos_ref, keep_ref, send_ref, ex_ref, y_s):
    count, wide = mine_ref.shape
    width = wide // 2
    half = keep_ref.shape[0]
    hpad = up(half, LANES)
    cpad = y_s.shape[0]
    y_s[0:count, :] = (mine_ref[...].astype(F32) + got_ref[...].astype(F32)).astype(BF16)
    if cpad > count:
        y_s[count:cpad, :] = jnp.zeros((cpad - count, wide), BF16)
    side = where_ref[1]
    for part in range(2):
        pos = jnp.broadcast_to(pos_ref[0:1, part * hpad : (part + 1) * hpad], (LANES, hpad)).T
        pos = pos[0:half]
        lane = lax.broadcasted_iota(jnp.int32, (half, LANES), 1).astype(F32)
        pick = jnp.concatenate(
            [jnp.where(pos == lane + float(j * LANES), 1.0, 0.0).astype(BF16) for j in range(cpad // LANES)], 1
        )
        ex_ref[part] = mm(pick, y_s[:, width:]).astype(BF16)
        rows = mm(pick, y_s[:, 0:width]).astype(BF16)

        @pl.when(side == part)
        def _():
            keep_ref[...] = rows

        @pl.when(side != part)
        def _():
            send_ref[...] = rows


def run_unsort(where, mine, got, pos, half):
    count, wide = mine.shape
    width = wide // 2
    outs = (sds((half, width), BF16), sds((half, width), BF16), sds((2, half, width), BF16))
    return call(
        unsort_kernel, outs, [pltpu.VMEM((up(count, LANES), wide), BF16)], "unsort", 4 * 10**9,
        in_specs=[SMEM_SPEC] + [VMEM_SPEC] * 3,
    )(where, mine, got, pos)


def out_kernel(mid_ref, mine_ref, got_ref, out_ref):
    half = out_ref.shape[1]
    for part in range(2):
        out_ref[part] = (
            mid_ref[part, 0:half, :] + (mine_ref[part].astype(F32) + got_ref[part].astype(F32))
        ).astype(BF16)


def run_out(mid, mine, got):
    return call(
        out_kernel, sds(mine.shape, BF16), [], "block_out", 10**9, in_specs=[VMEM_SPEC] * 3
    )(mid, mine, got)


def back_kernel(
    len_ref, where_ref, keep_ref, got_ref, mid_ref, cot_ref, ho_ref, hot_ref, q_ref, lse_ref, k_ref, kt_ref, v_ref,
    hid_ref, wqkv_ref, wproj_ref, gain2_ref, groute_ref,
    gmid_ref, hkeep_ref, hsend_ref, wkeep_ref, wsend_ref,
    segk_s, qm_s, dm_s, dq_s, dk_s, dv_s, ga_s, do_s, d_s, dqr_s,
):
    half, width = keep_ref.shape
    hpad = ho_ref.shape[1]
    kpad = k_ref.shape[0]
    rows = cot_ref.shape[0]
    own = rows // 2
    core, side = where_ref[0], where_ref[1]
    base = core * own + side * half
    ends = seq_ends(len_ref, len_ref.shape[1])
    scale = 1.0 / math.sqrt(width // HEADS)
    key_segments(segk_s, ends, kpad)

    grad_h2 = keep_ref[...].astype(F32) + got_ref[...].astype(F32)
    normed2, scale2 = normalize_rows(mid_ref[0, 0:half, :])
    gain2_part = jnp.sum(grad_h2 * normed2, 0, keepdims=True)
    grad_final = cot_ref[pl.ds(pl.multiple_of(base, GRAIN), half), :].astype(F32)
    grad_mid = grad_final + normal_back(grad_h2, normed2, scale2, gain2_ref[...])
    gmid_ref[...] = grad_mid
    ga_s[0:half, :] = grad_mid.astype(BF16)
    ga_s[half:hpad, :] = jnp.zeros((hpad - half, width), BF16)
    grad_attn = ga_s[...]
    grad_proj = mm(hot_ref[0], grad_attn)
    grad_heads = mm(grad_attn, wproj_ref[...], COLS_COLS).astype(BF16)
    do_s[...] = grad_heads
    sub = lax.broadcasted_iota(jnp.int32, (8, width), 0)
    lane = lax.broadcasted_iota(jnp.int32, (8, width), 1)
    pick = (lane // 64 == sub).astype(F32)
    product = grad_heads.astype(F32) * ho_ref[0].astype(F32)
    d_s[...] = lax.dot_general(pick, product, COLS_COLS, precision=lax.Precision.HIGHEST, preferred_element_type=F32)

    dk_s[...] = jnp.zeros(dk_s.shape, F32)
    dv_s[...] = jnp.zeros(dv_s.shape, F32)
    for first, lanes, valid in q_blocks(half):
        for h in range(HEADS):
            cols = slice((h // 2) * LANES, (h // 2 + 1) * LANES)
            mask = head_mask(lanes, h % 2)
            qm_s[h, 0:lanes, :] = q_ref[0, first : first + lanes, cols] * mask
            dm_s[h, 0:lanes, :] = do_s[first : first + lanes, cols] * mask
        dq_s[...] = jnp.zeros(dq_s.shape, F32)
        low, high = seq_bounds(ends, base + first, base + first + valid - 1)
        segq = query_segments(base, first, lanes, valid, ends)

        def key_step(kb, carry, first=first, lanes=lanes, segq=segq):
            kstart = pl.multiple_of(kb * KB, KB)
            bias = bias_block(segk_s, kstart, segq, lanes)
            for j in range(HEADS // 2):
                cols = slice(j * LANES, (j + 1) * LANES)
                kblk = k_ref[pl.ds(kstart, KB), cols]
                vblk = v_ref[pl.ds(kstart, KB), cols]
                dk = dk_s[pl.ds(kstart, KB), cols]
                dv = dv_s[pl.ds(kstart, KB), cols]
                for h in (2 * j, 2 * j + 1):
                    qm = qm_s[h, 0:lanes, :]
                    dm = dm_s[h, 0:lanes, :]
                    s = mm(kblk, qm, COLS_COLS) + bias
                    p = jnp.exp(s - lse_ref[0, h : h + 1, first : first + lanes])
                    dp = mm(vblk, dm, COLS_COLS)
                    ds = (p * (dp - d_s[h : h + 1, first : first + lanes])).astype(BF16)
                    dv = dv + mm(p.astype(BF16), dm)
                    dk = dk + mm(ds, qm)
                    dq_s[h * 64 : (h + 1) * 64, 0:lanes] += mm(
                        kt_ref[h * 64 : (h + 1) * 64, pl.ds(kstart, KB)], ds
                    )
                dk_s[pl.ds(kstart, KB), cols] = dk
                dv_s[pl.ds(kstart, KB), cols] = dv
            return carry

        lax.fori_loop(low // KB, (high + KB - 1) // KB, key_step, 0)
        dq = (dq_s[:, 0:lanes] * scale).T.astype(BF16)
        dqr_s[first : first + lanes, :] = dq

    wq = wqkv_ref[:, 0:width]
    wk = wqkv_ref[:, width : 2 * width]
    wv = wqkv_ref[:, 2 * width :]
    grad_q = dqr_s[0:half, :]
    hid_own = hid_ref[pl.ds(pl.multiple_of(base, GRAIN), half), :]
    gwq = mm(hid_own, grad_q, ROWS_ROWS)
    gwk = jnp.zeros((width, width), F32)
    gwv = jnp.zeros((width, width), F32)
    for part in range(2):
        target = hkeep_ref if part == 0 else hsend_ref
        start = pl.multiple_of((core if part == 0 else 1 - core) * own, GRAIN)
        dk = dk_s[pl.ds(start, own), :].astype(BF16)
        dv = dv_s[pl.ds(start, own), :].astype(BF16)
        hid = hid_ref[pl.ds(start, own), :].T
        gwk = gwk + mm(hid, dk)
        gwv = gwv + mm(hid, dv)
        target[...] = (mm(dk, wk, COLS_COLS) + mm(dv, wv, COLS_COLS)).astype(BF16)
    at = pl.multiple_of(side * half, GRAIN)
    dk = dk_s[pl.ds(pl.multiple_of(base, GRAIN), half), :].astype(BF16)
    dv = dv_s[pl.ds(pl.multiple_of(base, GRAIN), half), :].astype(BF16)
    hkeep_ref[pl.ds(at, half), :] = (
        mm(grad_q, wq, COLS_COLS) + mm(dk, wk, COLS_COLS) + mm(dv, wv, COLS_COLS)
    ).astype(BF16)

    route_t = groute_ref[...].T[0:8]
    extra = jnp.concatenate([route_t, jnp.broadcast_to(gain2_part, (8, width)), jnp.zeros((16, width), F32)], 0)

    def pack(ref, upper):
        a, b = (gwq, gwk) if upper else (gwv, grad_proj)
        ref[0:width, :] = a.astype(BF16)
        ref[width : 2 * width, :] = b.astype(BF16)
        ref[2 * width : 2 * width + 32, :] = (extra if upper else jnp.zeros_like(extra)).astype(BF16)

    @pl.when(core == 0)
    def _():
        pack(wkeep_ref, True)
        pack(wsend_ref, False)

    @pl.when(core != 0)
    def _():
        pack(wkeep_ref, False)
        pack(wsend_ref, True)


def run_back(lengths, where, side, keep, got, mid, cot, ho, hot, q, lse, k, kt, v, hid, wqkv, wproj, gain2, groute):
    half, width = keep.shape
    rows = cot.shape[0]
    own = rows // 2
    hpad = ho.shape[1]
    kpad = k.shape[0]

    def pick(shape):
        return pl.BlockSpec((1,) + shape[1:], lambda i, side_ref: (side_ref[0],) + (0,) * (len(shape) - 1))

    def whole(shape):
        return pl.BlockSpec(shape, lambda i, side_ref: (0,) * len(shape))

    outs = (
        sds((half, width), F32),
        sds((own, width), BF16),
        sds((own, width), BF16),
        sds((2 * width + 32, width), BF16),
        sds((2 * width + 32, width), BF16),
    )
    scratch = [
        pltpu.VMEM((kpad, LANES), jnp.int32),
        pltpu.VMEM((HEADS, KB, LANES), BF16),
        pltpu.VMEM((HEADS, KB, LANES), BF16),
        pltpu.VMEM((width, KB), F32),
        pltpu.VMEM((kpad, width), F32),
        pltpu.VMEM((kpad, width), F32),
        pltpu.VMEM((hpad, width), BF16),
        pltpu.VMEM((hpad, width), BF16),
        pltpu.VMEM((8, hpad), F32),
        pltpu.VMEM((hpad, width), BF16),
    ]

    def kernel(side_ref, *refs):
        back_kernel(*refs)

    args = (lengths, where, keep, got, mid, cot, ho, hot, q, lse, k, kt, v, hid, wqkv, wproj, gain2, groute)
    picked = {4, 6, 7, 8, 9}
    in_specs = [SMEM_SPEC, SMEM_SPEC]
    for i, a in enumerate(args):
        if i >= 2:
            in_specs.append(pick(a.shape) if i in picked else whole(a.shape))
    return call(
        kernel, outs, (), "back", 20 * 10**9,
        grid_spec=pltpu.PrefetchScalarGridSpec(
            num_scalar_prefetch=1,
            grid=(1,),
            in_specs=in_specs,
            out_specs=tuple(whole(o.shape) for o in outs),
            scratch_shapes=scratch,
        ),
    )(side, *args)


def token_kernel(where_ref, mine_ref, got_ref, gmid_ref, tok_ref, gain1_ref, out_ref):
    half = gmid_ref.shape[0]
    own = tok_ref.shape[0] // 2
    base = where_ref[0] * own + where_ref[1] * half
    grad_h1 = mine_ref[...].astype(F32) + got_ref[...].astype(F32)
    normed1, scale1 = normalize_rows(tok_ref[pl.ds(pl.multiple_of(base, GRAIN), half), :].astype(F32))
    out_ref[...] = (gmid_ref[...] + normal_back(grad_h1, normed1, scale1, gain1_ref[...])).astype(BF16)


def run_tokens(where, mine, got, gmid, tokens, gain1):
    return call(
        token_kernel, sds(gmid.shape, BF16), [], "token_grad", 10**9,
        in_specs=[SMEM_SPEC] + [VMEM_SPEC] * 5,
    )(where, mine, got, gmid, tokens, gain1)


def expert_end_kernel(where_ref, ma_ref, oa_ref, mb_ref, ob_ref, mc_ref, oc_ref, gin_ref, gout_ref):
    e = pl.program_id(0)

    def put(mine_ref, other_ref, side):
        mine = mine_ref[0].astype(F32)
        other = other_ref[0].astype(F32)
        first = side == 0
        gin_ref[0] = jnp.where(first, mine, other)
        gout_ref[0] = jnp.where(first, other, mine)

    @pl.when(e < 3)
    def _():
        put(ma_ref, oa_ref, where_ref[2])

    @pl.when((e >= 3) & (e < 6))
    def _():
        put(mb_ref, ob_ref, where_ref[3])

    @pl.when(e >= 6)
    def _():
        put(mc_ref, oc_ref, where_ref[4])


def run_expert_end(where, pieces, shape_in, shape_out):
    experts, width, hidden = shape_in
    part = lambda first, size: pl.BlockSpec(
        (1, width, hidden), lambda e: (jnp.clip(e - first, 0, size - 1), 0, 0)
    )
    in_specs = [SMEM_SPEC]
    for first, size in ((0, 3), (3, 3), (6, 2)):
        in_specs += [part(first, size)] * 2
    block = pl.BlockSpec((1, width, hidden), lambda e: (e, 0, 0))
    return call(
        expert_end_kernel,
        (sds(shape_in, F32), sds(shape_out, F32)),
        [],
        "expert_end",
        10**9,
        grid=(experts,),
        in_specs=in_specs,
        out_specs=(block, block),
    )(where, *pieces)


def attn_end_kernel(where_ref, mine_ref, other_ref, wqkv_ref, gain1_ref, gqkv_ref, gproj_ref, g1_ref, g2_ref, groute_ref):
    width = wqkv_ref.shape[0]
    first = where_ref[0] == 0
    mine = mine_ref[...].astype(F32)
    other = other_ref[...].astype(F32)
    low = jnp.where(first, mine, other)
    high = jnp.where(first, other, mine)
    gq, gk, gv = low[0:width], low[width : 2 * width], high[0:width]
    gqkv_ref[:, 0, :] = gq
    gqkv_ref[:, 1, :] = gk
    gqkv_ref[:, 2, :] = gv
    gproj_ref[...] = high[width : 2 * width]
    product = gq * wqkv_ref[:, 0:width].astype(F32)
    product = product + gk * wqkv_ref[:, width : 2 * width].astype(F32)
    product = product + gv * wqkv_ref[:, 2 * width :].astype(F32)
    total = jnp.sum(product.T, 0, keepdims=True)
    g1_ref[...] = total / gain1_ref[...]
    g2_ref[...] = low[2 * width + 8 : 2 * width + 9]
    groute_ref[...] = low[2 * width : 2 * width + 8]


def run_attn_end(where, mine, other, wqkv, gain1):
    width = wqkv.shape[0]
    outs = (
        sds((width, 3, width), F32),
        sds((width, width), F32),
        sds((1, width), F32),
        sds((1, width), F32),
        sds((8, width), F32),
    )
    return call(
        attn_end_kernel, outs, [], "attn_end", 10**9, in_specs=[SMEM_SPEC] + [VMEM_SPEC] * 4
    )(where, mine, other, wqkv, gain1)


def swap(value, axis, mask):
    size = lax.axis_size(axis)
    return lax.ppermute(value, axis, [(i, i ^ mask) for i in range(size)])


def added(a, b):
    return (a.astype(F32) + b.astype(F32)).astype(BF16)


def in_order(mine, other, bit):
    return jnp.where(bit == 0, jnp.stack([mine, other]), jnp.stack([other, mine]))


def wide_sum(keep, send, masks, bit2, rest):
    first, second, third = masks
    part = added(keep, swap(send, "wide", first)).reshape((2, -1) + keep.shape[1:])
    mine = lax.dynamic_index_in_dim(part, bit2, 0, False)
    give = lax.dynamic_index_in_dim(part, 1 - bit2, 0, False)
    mine = added(mine, swap(give, "wide", second))
    for mask in (third,) + rest:
        mine = added(mine, swap(mine, "wide", mask))
    mine = in_order(mine, swap(mine, "wide", second), bit2).reshape(keep.shape)
    return mine, swap(mine, "wide", first)


def on_device(
    tokens, w_qkv, w_proj, norm1_gain, norm2_gain, w_route, w_in, w_out, cotangent, routes, kept_mask, lengths
):
    rows, width = tokens.shape
    own, half = rows // 2, rows // 4
    hpad = up(half, LANES)
    experts = w_in.shape[0]
    n = lax.axis_index("narrow")
    w = lax.axis_index("wide")
    core, side = n % 2, n // 2
    bit_x = w % 2
    bit_m = (w // 4) % 2
    bit_p = (w // 2) % 2 ^ bit_m
    where = jnp.stack([core, side, bit_x, bit_p, bit_m, jnp.int32(0), jnp.int32(0), jnp.int32(0)]).astype(jnp.int32)
    rest = tuple(1 << i for i in range(3, lax.axis_size("wide").bit_length() - 1))

    wqkv = w_qkv.reshape(width, 3 * width)
    wr = jnp.pad(w_route, ((0, 0), (0, LANES - experts)))
    gain1 = norm1_gain.reshape(1, width)
    gain2 = norm2_gain.reshape(1, width)
    code = jnp.where(kept_mask == 1, routes[:, 0], experts).reshape(2, 2, half)
    code = jnp.pad(code, ((0, 0), (0, 0), (0, hpad - half)), constant_values=experts).reshape(2, 1, 2 * hpad)

    own_x, hid, k, kt, v, q, ho, hot, lse, mid, pos, plan = run_front(
        lengths, where, tokens, wqkv, w_proj, gain1, gain2, wr, cotangent, code
    )
    oth_x = swap(own_x, "narrow", 1)
    yown, yoth, ka, sa, kb, sb, kc, sc, groute = run_experts(plan, where, own_x, oth_x, w_in, w_out, wr)

    got = swap(yoth, "narrow", 1)
    keep, send, ex = run_unsort(where, yown, got, pos, half)
    got = swap(send, "narrow", 2)

    x, p, m = 1, 2, 6
    flat = lambda a: a.reshape(-1, a.shape[-1])
    pieces = []
    for (kk, ss), masks, bit2 in (
        ((ka, sa), (x, p, m), bit_p),
        ((kb, sb), (p, m, x), bit_m),
        ((kc, sc), (m, x, p), bit_x),
    ):
        mine, other = wide_sum(flat(kk), flat(ss), masks, bit2, rest)
        pieces += [mine.reshape(kk.shape), other.reshape(kk.shape)]
    grad_in, grad_out = run_expert_end(where, pieces, w_in.shape, w_out.shape)

    gmid, hkeep, hsend, wkeep, wsend = run_back(
        lengths, where, side.astype(jnp.int32).reshape(1), keep, got, mid, cotangent, ho, hot, q, lse, k, kt, v, hid,
        wqkv, w_proj, gain2, groute,
    )

    part = added(wkeep, swap(wsend, "narrow", 1)).reshape(2, -1, width)
    mine = lax.dynamic_index_in_dim(part, side, 0, False)
    give = lax.dynamic_index_in_dim(part, 1 - side, 0, False)
    mine = added(mine, swap(give, "narrow", 2))
    for mask in (x, p, m) + rest:
        mine = added(mine, swap(mine, "wide", mask))
    mine = in_order(mine, swap(mine, "narrow", 2), side).reshape(wkeep.shape)
    other = swap(mine, "narrow", 1)
    grad_qkv, grad_proj, grad_norm1, grad_norm2, route_t = run_attn_end(where, mine, other, wqkv, gain1)

    part = added(hkeep, swap(hsend, "narrow", 1)).reshape(2, half, width)
    mine = lax.dynamic_index_in_dim(part, side, 0, False)
    give = lax.dynamic_index_in_dim(part, 1 - side, 0, False)
    token_rows = run_tokens(where, mine, swap(give, "narrow", 2), gmid, tokens, gain1)
    mine = in_order(token_rows, swap(token_rows, "narrow", 2), side).reshape(own, width)
    grad_tokens = in_order(mine, swap(mine, "narrow", 1), core).reshape(rows, width)

    mine = run_out(mid, ex, swap(ex, "narrow", 2)).reshape(own, width)
    layer_out = in_order(mine, swap(mine, "narrow", 1), core).reshape(rows, width)

    return (
        layer_out,
        grad_tokens,
        grad_qkv,
        grad_proj,
        grad_norm1.reshape(width),
        grad_norm2.reshape(width),
        route_t.T,
        grad_in,
        grad_out,
    )


def solution(mesh):
    in_specs = (
        P("wide", None),
        P(),
        P(),
        P(),
        P(),
        P(),
        P(None, None, "narrow"),
        P(None, "narrow", None),
        P("wide", None),
        P("wide", None),
        P("wide"),
        P("wide", None),
    )
    out_specs = (
        P("wide", None),
        P("wide", None),
        P(),
        P(),
        P(),
        P(),
        P(),
        P(None, None, "narrow"),
        P(None, "narrow", None),
    )
    return jax.shard_map(on_device, mesh=mesh, in_specs=in_specs, out_specs=out_specs, check_vma=False)
```

```python
import math

import jax
import jax.numpy as jnp
from jax import lax
from jax.experimental import pallas as pl
from jax.experimental.pallas import tpu as pltpu
from jax.sharding import Mesh, PartitionSpec as P

HEADS = 6
CAP = 408
EPS = 1e-06
NEG = -1e30
F32 = jnp.float32
BF16 = jnp.bfloat16
LANES = 128
KB = 256
GRAIN = 16
STRIP = 32
FLOPS = 10**10
PARTS = (4, 2, 2)
GELU_A = math.sqrt(2.0 / math.pi)
GELU_B = 0.044715

ROWS_COLS = (((1,), (0,)), ((), ()))
COLS_COLS = (((1,), (1,)), ((), ()))
ROWS_ROWS = (((0,), (0,)), ((), ()))


def up(value, grain):
    return -(-value // grain) * grain


def mm(a, b, dims=ROWS_COLS):
    return lax.dot_general(a, b, dims, preferred_element_type=F32)


def normalize_rows(values):
    centre = values - jnp.mean(values, -1, keepdims=True)
    row_scale = lax.rsqrt(jnp.mean(centre * centre, -1, keepdims=True) + EPS)
    return centre * row_scale, row_scale


def normal_back(grad_h, normed, row_scale, gain_row):
    g = grad_h * gain_row
    return row_scale * (
        g - jnp.mean(g, -1, keepdims=True) - normed * jnp.mean(g * normed, -1, keepdims=True)
    )


def lane_head(h):
    return slice((h // 2) * LANES, (h // 2 + 1) * LANES)


def seq_ends(len_ref, count):
    ends = []
    total = jnp.int32(0)
    for j in range(count):
        total = total + len_ref[0, j]
        ends.append(total)
    return ends


def seq_bounds(ends, first_row, last_row):
    low = jnp.int32(0)
    high = ends[-1]
    for end in ends:
        low = jnp.where(end <= first_row, end, low)
    for end in reversed(ends):
        high = jnp.where(end > last_row, end, high)
    return low, high


def segment_of(index, ends):
    seg = jnp.zeros(index.shape, jnp.int32)
    for end in ends:
        seg = seg + (index >= end).astype(jnp.int32)
    return seg


def key_segments(segk_ref, ends, kpad):
    def body(i, carry):
        start = pl.multiple_of(i * LANES, LANES)
        index = lax.broadcasted_iota(jnp.int32, (LANES, LANES), 0) + start
        segk_ref[pl.ds(start, LANES), :] = segment_of(index, ends)
        return carry

    lax.fori_loop(0, kpad // LANES, body, 0)


def bias_block(segk_ref, kstart, segq):
    segk = segk_ref[pl.ds(kstart, KB), :]
    return jnp.where(jnp.concatenate([segk, segk], 1) == segq, 0.0, NEG)


def head_mask(rows, odd):
    lane = lax.broadcasted_iota(jnp.int32, (rows, LANES), 1)
    return ((lane >= 64) if odd else (lane < 64)).astype(BF16)


def plan_of(code_row, experts):
    n = code_row.shape[1]
    sub = lax.broadcasted_iota(jnp.int32, (experts, n), 0)
    lane = lax.broadcasted_iota(jnp.int32, (experts, n), 1)
    member = (code_row == sub).astype(F32)
    rank = member
    shift = 1
    while shift < n:
        rank = rank + jnp.where(lane >= shift, pltpu.roll(rank, shift, 1), 0.0)
        shift *= 2
    counts = jnp.broadcast_to(rank[:, n - 1 : n], (experts, LANES))
    sizes = jnp.floor((counts + (GRAIN - 1)) * (1.0 / GRAIN)) * GRAIN
    row = lax.broadcasted_iota(jnp.int32, (experts, LANES), 0)
    total = sizes
    shift = 1
    while shift < experts:
        total = total + jnp.where(row >= shift, pltpu.roll(total, shift, 0), 0.0)
        shift *= 2
    offsets = total - sizes
    pos = jnp.sum(member * (rank + offsets[:, 0:1]), 0, keepdims=True) - 1.0
    return pos, offsets, sizes


def key_steps(low, high):
    start = low // LANES * LANES
    return start, (high - start + KB - 1) // KB


def plan_kernel(where_ref, code_ref, plan_ref, pos_ref):
    experts = 8
    core = where_ref[0]
    pos, offsets, sizes = plan_of(code_ref[core], experts)
    unused, other_offsets, other_sizes = plan_of(code_ref[1 - core], experts)
    plan_ref[0:8, :] = offsets.astype(jnp.int32)
    plan_ref[8:16, :] = sizes.astype(jnp.int32)
    plan_ref[16:24, :] = other_offsets.astype(jnp.int32)
    plan_ref[24:32, :] = other_sizes.astype(jnp.int32)
    pos_ref[...] = jnp.broadcast_to(pos, pos_ref.shape)


def unpick_part(columns, part, half, cpad):
    lane = lax.broadcasted_iota(jnp.int32, (half, LANES), 1).astype(F32)
    column = strips(columns, part, half)
    return jnp.concatenate(
        [jnp.where(column == lane + float(j * LANES), 1.0, 0.0).astype(BF16) for j in range(cpad // LANES)], 1
    )


def unpick_kernel(pos_ref, unpick_ref):
    half, cpad = unpick_ref.shape[1:]
    columns = jnp.broadcast_to(pos_ref[0:1, :], (LANES, pos_ref.shape[1])).T
    for part in range(2):
        unpick_ref[part] = unpick_part(columns, part, half, cpad)


def run_unpick(pos, own, count, after):
    return call(
        unpick_kernel, sds((2, own // 2, up(count, LANES)), BF16), [], "unpick", 2, limit=12,
        in_specs=[VMEM_SPEC], after=after,
    )(pos)


def strips(value, part, half):
    return jnp.concatenate(
        [value[(2 * i + part) * STRIP : (2 * i + part + 1) * STRIP] for i in range(half // STRIP)], 0
    )


def strip_start(base, i, side):
    return pl.multiple_of(base + 2 * STRIP * i + STRIP * side, STRIP)


def in_strips(array):
    return array.reshape(-1, 2, STRIP, array.shape[-1])


def strip_copy(ref, first, side, dst, sem):
    return pltpu.make_async_copy(ref.at[pl.ds(first, dst.shape[0]), side], dst, sem)


def load_strips(ref, base, side, half):
    return jnp.concatenate([ref[pl.ds(strip_start(base, i, side), STRIP), :] for i in range(half // STRIP)], 0)


def front_kernel(
    len_ref, where_ref, tok_ref, w3_ref, wproj_ref, gain1_ref,
    hid_out, k_out, kt_out, v_out, q_out, ho_out, lse_out, keep_ref, send_ref,
    hid_ref, k_ref, kt_ref, v_ref, q_ref, ho_ref, lse_ref,
    vt_s, segk_s, qm_s, acc_s, m_s, l_s, s_s, st_s, sems,
):
    rows, width = tok_ref.shape
    own = rows // 2
    copies = [
        pltpu.make_async_copy(src, dst, sems.at[i])
        for i, (src, dst) in enumerate(
            (
                (hid_ref, hid_out), (k_ref, k_out), (kt_ref, kt_out), (v_ref, v_out), (q_ref, q_out),
                (ho_ref, ho_out), (lse_ref, lse_out),
            )
        )
    ]
    kpad = hid_ref.shape[0]
    qpad = q_ref.shape[0]
    mine = w3_ref.shape[2]
    heads = mine // 64
    core = where_ref[0]
    ends = seq_ends(len_ref, len_ref.shape[1])
    scale = 1.0 / math.sqrt(width // HEADS)
    key_segments(segk_s, ends, kpad)
    gain1 = gain1_ref[...]
    wq, wk, wv = w3_ref[0], w3_ref[1], w3_ref[2]
    step = rows // 4

    def norm_body(i, carry):
        at = pl.ds(pl.multiple_of(i * step, GRAIN), step)
        normed, unused = normalize_rows(tok_ref[at, :].astype(F32))
        hid = (normed * gain1).astype(BF16)
        hid_ref[at, :] = hid
        k_ref[at, 0:mine] = mm(hid, wk).astype(BF16)
        v_ref[at, 0:mine] = mm(hid, wv).astype(BF16)
        q_ref[at, 0:mine] = (mm(hid, wq).astype(BF16).astype(F32) * scale).astype(BF16)
        return carry

    lax.fori_loop(0, 4, norm_body, 0)
    hid_ref[rows:kpad, :] = jnp.zeros((kpad - rows, width), BF16)
    for ref in (k_ref, v_ref, q_ref):
        size = ref.shape[0]
        ref[rows:size, 0:mine] = jnp.zeros((size - rows, mine), BF16)
        ref[:, mine:] = jnp.zeros((size, ref.shape[1] - mine), BF16)
    wkt = wk.T
    wvt = wv.T

    def key_body(i, carry):
        at = pl.ds(pl.multiple_of(i * 2 * KB, 2 * KB), 2 * KB)
        hid = hid_ref[at, :]
        kt_ref[:, at] = mm(wkt, hid, COLS_COLS).astype(BF16)
        vt_s[:, at] = mm(wvt, hid, COLS_COLS).astype(BF16)
        return carry

    lax.fori_loop(0, kpad // (2 * KB), key_body, 0)
    for copy in copies[:5]:
        copy.start()
    st_s[...] = jnp.zeros(st_s.shape, F32)

    def q_step(qb, carry):
        first = pl.multiple_of(qb * KB, KB)
        last = jnp.minimum(first + KB, rows) - 1
        for h in range(heads):
            qm_s[h] = q_ref[pl.ds(first, KB), lane_head(h)] * head_mask(KB, h % 2)
        for h in range(heads):
            m_s[h : h + 1] = jnp.full((1, KB), NEG, F32)
            l_s[h : h + 1] = jnp.zeros((1, KB), F32)
        acc_s[...] = jnp.zeros(acc_s.shape, F32)
        low, high = seq_bounds(ends, first, last)
        start, steps = key_steps(low, high)
        segq = segment_of(lax.broadcasted_iota(jnp.int32, (8, KB), 1) + first, ends)[0:1]

        def scores(at):
            return [mm(k_ref[pl.ds(at, KB), lane_head(h)], qm_s[h], COLS_COLS) for h in range(heads)]

        for h, s in enumerate(scores(pl.multiple_of(start, LANES))):
            s_s[h] = s

        def k_step(kb, carry):
            at = pl.multiple_of(start + kb * KB, LANES)
            later = pl.multiple_of(start + jnp.minimum(kb + 1, steps - 1) * KB, LANES)
            bias = bias_block(segk_s, at, segq)
            now = [s_s[h] + bias for h in range(heads)]
            nexts = scores(later)
            m_old = [m_s[h : h + 1] for h in range(heads)]
            m_new = [jnp.maximum(m, jnp.max(s, 0, keepdims=True)) for m, s in zip(m_old, now)]
            p = [jnp.exp(s - m) for s, m in zip(now, m_new)]
            alpha = [jnp.exp(a - b) for a, b in zip(m_old, m_new)]
            for h in range(heads):
                m_s[h : h + 1] = m_new[h]
                l_s[h : h + 1] = l_s[h : h + 1] * alpha[h] + jnp.sum(p[h], 0, keepdims=True)
            out = [mm(vt_s[h * 64 : (h + 1) * 64, pl.ds(at, KB)], p[h].astype(BF16)) for h in range(heads)]
            for h in range(heads):
                acc_s[h * 64 : (h + 1) * 64] = acc_s[h * 64 : (h + 1) * 64] * alpha[h] + out[h]
                s_s[h] = nexts[h]
            return carry

        lax.fori_loop(0, steps, k_step, 0)
        parts = []
        for h in range(heads):
            total = l_s[h : h + 1]
            st_s[h : h + 1] = m_s[h : h + 1] + jnp.log(total)
            parts.append(acc_s[h * 64 : (h + 1) * 64] * (1.0 / total))
        lse_ref[pl.ds(first, KB), :] = st_s[...].T
        parts.append(jnp.zeros((ho_ref.shape[1] - mine, KB), F32))
        ho_ref[pl.ds(first, KB), :] = jnp.concatenate(parts, 0).T.astype(BF16)
        return carry

    lax.fori_loop(0, qpad // KB, q_step, 0)
    for copy in copies[5:]:
        copy.start()
    wproj = wproj_ref[pl.ds(pl.multiple_of(core * mine, GRAIN), mine), :]
    keep_ref[...] = mm(ho_ref[pl.ds(pl.multiple_of(core * own, GRAIN), own), 0:mine], wproj).astype(BF16)
    send_ref[...] = mm(ho_ref[pl.ds(pl.multiple_of((1 - core) * own, GRAIN), own), 0:mine], wproj).astype(BF16)
    for copy in copies:
        copy.wait()


def mid_kernel(
    where_ref, keep_ref, got_ref, tok_ref, cot_ref, gain2_ref, wr_ref, code_ref, pos_ref,
    mid_ref, sorted_ref, send_ref, x_s, tok_s, cot_s, mid_s, sems,
):
    own, width = keep_ref.shape
    npad = x_s.shape[0]
    core = where_ref[0]
    at = pl.ds(pl.multiple_of(core * own, GRAIN), own)
    tok_copy = pltpu.make_async_copy(tok_ref.at[at, :], tok_s, sems.at[0])
    cot_copy = pltpu.make_async_copy(cot_ref.at[at, :], cot_s, sems.at[1])
    tok_copy.start()
    cot_copy.start()
    tok_copy.wait()
    mid = tok_s[...].astype(F32) + (keep_ref[...].astype(F32) + got_ref[...].astype(F32))
    mid_s[...] = mid
    mid_copy = pltpu.make_async_copy(mid_s, mid_ref, sems.at[6])
    mid_copy.start()
    normed2, unused = normalize_rows(mid)
    hidden2 = (normed2 * gain2_ref[...]).astype(BF16)
    lane = lax.broadcasted_iota(jnp.int32, (own, LANES), 1)
    gates = router_gates(hidden2, wr_ref[...], lane, 8)
    code_col = jnp.broadcast_to(code_ref[core].astype(F32), (LANES, npad)).T[0:own]
    gate = jnp.sum(jnp.where(code_col == lane.astype(F32), gates, 0.0), -1, keepdims=True)
    x_s[0:own, 0:width] = hidden2
    cot_copy.wait()
    x_s[0:own, width:] = (gate * cot_s[...].astype(F32)).astype(BF16)
    x_s[own:npad, :] = jnp.zeros((npad - own, 2 * width), BF16)
    piece = sorted_ref.shape[0] // 4
    copies = []
    for i in range(4):
        rows = slice(i * piece, (i + 1) * piece)
        sub = lax.broadcasted_iota(jnp.int32, (piece, npad), 0) + i * piece
        pick = jnp.where(sub.astype(F32) == pos_ref[0:1, :], 1.0, 0.0).astype(BF16)
        sorted_ref[rows, :] = mm(pick, x_s[...]).astype(BF16)
        copies.append(pltpu.make_async_copy(sorted_ref.at[rows, :], send_ref.at[rows, :], sems.at[2 + i]))
        copies[-1].start()
    for copy in copies + [mid_copy]:
        copy.wait()


def router_gates(hidden2, wr, lane, experts):
    logits = jnp.where(lane < experts, mm(hidden2, wr), NEG)
    top = jnp.max(logits, -1, keepdims=True)
    e = jnp.exp(logits - top)
    return e / jnp.sum(e, -1, keepdims=True)


def call(kernel, outs, scratch, name, micros, in_specs, limit=24, after=None, **more):
    def out_of(shape, spec):
        if spec is VMEM_SPEC:
            return pltpu.VMEM(shape.shape, shape.dtype)
        return pltpu.HBM(shape.shape, shape.dtype) if is_far(spec) else shape

    out_specs = more.get("out_specs")
    if out_specs is None:
        out_specs = jax.tree.map(lambda o: VMEM_SPEC, outs)
    if isinstance(outs, tuple):
        outs = tuple(out_of(o, spec) for o, spec in zip(outs, out_specs))
    else:
        outs = out_of(outs, out_specs)
    more["out_specs"] = out_specs
    aliases = more.pop("input_output_aliases", {})
    body = kernel
    if after is not None:
        in_specs = [ANY_SPEC] + list(in_specs)
        aliases = {i + 1: o for i, o in aliases.items()}
        body = lambda after_ref, *refs: kernel(*refs)
    run = pl.pallas_call(
        body,
        out_shape=outs,
        in_specs=in_specs,
        scratch_shapes=scratch,
        name=name,
        input_output_aliases=aliases,
        compiler_params=pltpu.CompilerParams(vmem_limit_bytes=limit * 1024 * 1024),
        cost_estimate=pl.CostEstimate(flops=micros * FLOPS, bytes_accessed=10**4, transcendentals=0),
        **more,
    )

    def place(array, spec):
        if spec is VMEM_SPEC:
            return pltpu.with_memory_space_constraint(array, pltpu.VMEM)
        return pltpu.with_memory_space_constraint(array, pltpu.HBM) if is_far(spec) else array

    def run_on(*args):
        placed = [place(a, spec) for a, spec in zip(args, in_specs[len(in_specs) - len(args) :])]
        if after is not None:
            array, spec = after
            placed = [place(array, spec)] + placed
        return run(*placed)

    return run_on


def is_far(spec):
    return spec is FAR_SPEC or spec is FAR_ANY or spec.block_shape is not None


ANY_SPEC = pl.BlockSpec(memory_space=pl.ANY)
FAR_SPEC = pl.BlockSpec(memory_space=pltpu.VMEM)
FAR_ANY = pl.BlockSpec(memory_space=pl.ANY)
PLAIN_SPEC = pl.BlockSpec(memory_space=pltpu.VMEM)
SMEM_SPEC = pl.BlockSpec(memory_space=pltpu.SMEM)
VMEM_SPEC = pl.BlockSpec(memory_space=pltpu.VMEM)


def sds(shape, dtype):
    return jax.ShapeDtypeStruct(shape, dtype)


def run_plan(where, code, after=None):
    npad = code.shape[2]
    outs = (
        sds((32, LANES), jnp.int32),
        sds((8, npad), F32),
    )
    return call(plan_kernel, outs, [], "plan", 5, limit=12, in_specs=[SMEM_SPEC, VMEM_SPEC], after=after)(where, code)


def run_front(lengths, where, tokens, w3, wproj, gain1):
    rows, width = tokens.shape
    own = rows // 2
    mine = w3.shape[2]
    heads = mine // 64
    kpad = up(rows + KB, 2 * KB)
    qpad = up(rows, KB)
    lanes = up(mine, LANES)
    outs = (
        sds((kpad, width), BF16),
        sds((kpad, lanes), BF16),
        sds((mine, kpad), BF16),
        sds((kpad, lanes), BF16),
        sds((qpad, lanes), BF16),
        sds((qpad, lanes), BF16),
        sds((qpad, LANES), F32),
        sds((own, width), BF16),
        sds((own, width), BF16),
    )
    scratch = [pltpu.VMEM(o.shape, o.dtype) for o in outs[:7]] + [
        pltpu.VMEM((mine, kpad), BF16),
        pltpu.VMEM((kpad, LANES), jnp.int32),
        pltpu.VMEM((heads, KB, LANES), BF16),
        pltpu.VMEM((mine, KB), F32),
        pltpu.VMEM((8, KB), F32),
        pltpu.VMEM((8, KB), F32),
        pltpu.VMEM((heads, KB, KB), F32),
        pltpu.VMEM((LANES, KB), F32),
        pltpu.SemaphoreType.DMA((7,)),
    ]
    return call(
        front_kernel, outs, scratch, "front", 33, in_specs=[SMEM_SPEC, SMEM_SPEC] + [VMEM_SPEC] * 4, limit=32,
        out_specs=(FAR_ANY,) * 7 + (PLAIN_SPEC,) * 2,
    )(lengths, where, tokens, w3, wproj, gain1)


def run_mid(where, keep, got, tokens, cot, gain2, wr, code, pos):
    own, width = keep.shape
    count = up(own + 8 * (GRAIN - 1), 4 * GRAIN)
    outs = (sds((own, width), F32),) + (sds((count, 2 * width), BF16),) * 2
    scratch = [
        pltpu.VMEM((code.shape[2], 2 * width), BF16),
        pltpu.VMEM((own, width), BF16),
        pltpu.VMEM((own, width), BF16),
        pltpu.VMEM((own, width), F32),
        pltpu.SemaphoreType.DMA((7,)),
    ]
    return call(
        mid_kernel, outs, scratch, "mid", 9, limit=20,
        in_specs=[SMEM_SPEC, PLAIN_SPEC, PLAIN_SPEC, FAR_ANY, FAR_ANY] + [VMEM_SPEC] * 4,
        out_specs=(FAR_ANY, VMEM_SPEC, ANY_SPEC),
    )(where, keep, got, tokens, cot, gain2, wr, code, pos)


def expert_kernel(
    plan_ref, where_ref, own_ref, oth_ref, win_ref, wout_ref, wr_ref,
    yown_ref, yoth_ref, groute_ref, *refs,
):
    *grads, x_s, y_s = refs
    e = pl.program_id(0)
    width = win_ref.shape[1]
    most = x_s.shape[0]

    @pl.when(e == 0)
    def _():
        yown_ref[...] = jnp.zeros(yown_ref.shape, BF16)
        yoth_ref[...] = jnp.zeros(yoth_ref.shape, BF16)
        groute_ref[...] = jnp.zeros(groute_ref.shape, F32)

    own_at, own_size = plan_ref[e, 0], plan_ref[8 + e, 0]
    oth_at, oth_size = plan_ref[16 + e, 0], plan_ref[24 + e, 0]
    total = own_size + oth_size

    def move(dst, dst_at, src, src_at, size):
        def body(i, carry):
            a = pl.multiple_of(dst_at + i * GRAIN, GRAIN)
            b = pl.multiple_of(src_at + i * GRAIN, GRAIN)
            dst[pl.ds(a, GRAIN), :] = src[pl.ds(b, GRAIN), :]
            return carry

        lax.fori_loop(0, size // GRAIN, body, 0)

    move(x_s, 0, own_ref, own_at, own_size)
    move(x_s, own_size, oth_ref, oth_at, oth_size)

    def work(m):
        def zero_body(i, carry):
            x_s[pl.ds(pl.multiple_of(i * GRAIN, GRAIN), GRAIN), :] = jnp.zeros((GRAIN, 2 * width), BF16)
            return carry

        lax.fori_loop(total // GRAIN, m // GRAIN, zero_body, 0)
        h = x_s[0:m, 0:width]
        g = x_s[0:m, width:]
        w_in = win_ref[0]
        w_out = wout_ref[0]
        lane = lax.broadcasted_iota(jnp.int32, (m, LANES), 1)
        gates = router_gates(h, wr_ref[...], lane, 8)
        here = (lane == e).astype(F32)
        pre = mm(h, w_in)
        t = jnp.tanh(GELU_A * (pre + GELU_B * (pre * pre * pre)))
        act = (0.5 * pre * (1.0 + t)).astype(BF16)
        slope = 0.5 * (1.0 + t) + 0.5 * pre * (1.0 - t * t) * (GELU_A * (1.0 + 3.0 * GELU_B * (pre * pre)))
        out = mm(act, w_out)
        grad_pre = (mm(g, w_out, COLS_COLS) * slope).astype(BF16)
        dot = jnp.sum(g.astype(F32) * out, -1, keepdims=True)
        grad_logits = (dot * (here - gates)).astype(BF16)
        gate = jnp.sum(gates * here, -1, keepdims=True)
        y_s[0:m, 0:width] = (mm(grad_pre, w_in, COLS_COLS) + mm(grad_logits, wr_ref[...], COLS_COLS)).astype(BF16)
        y_s[0:m, width:] = (gate * out).astype(BF16)
        ht = h.T
        groute_ref[...] += mm(ht, grad_logits)
        grad_in = mm(ht, grad_pre).astype(BF16)
        grad_out = mm(act.T, g).astype(BF16)

        at = 0
        for i, size in enumerate(PARTS):
            here = (e >= at) & (e < at + size)
            if i == 0:
                put_both(grads[0], grad_in, grad_out, here)
            else:
                put(grads[2 * i - 1 : 2 * i + 1], grad_in, grad_out, here)
            at += size

    def put_both(ref, grad_in, grad_out, here):
        @pl.when(here)
        def _():
            ref[0, 0] = grad_in
            ref[0, 1] = grad_out

    def put(pair, grad_in, grad_out, here):
        keep_ref, send_ref = pair

        @pl.when(here & (where_ref[2] == 0))
        def _():
            keep_ref[0] = grad_in
            send_ref[0] = grad_out

        @pl.when(here & (where_ref[2] != 0))
        def _():
            keep_ref[0] = grad_out
            send_ref[0] = grad_in

    small = up(CAP * 2 // 3, GRAIN)

    @pl.when(total <= small)
    def _():
        work(small)

    @pl.when(total > small)
    def _():
        work(most)

    move(yown_ref, own_at, y_s, 0, own_size)
    move(yoth_ref, oth_at, y_s, own_size, oth_size)


def run_experts(plan, where, own, oth, w_in, w_out, wr):
    experts, width, hidden = w_in.shape
    count = own.shape[0]
    most = (CAP + 2 * (GRAIN - 1)) // GRAIN * GRAIN
    outs = [sds((count, 2 * width), BF16)] * 2 + [sds((width, LANES), F32)]
    out_specs = [VMEM_SPEC, PLAIN_SPEC, VMEM_SPEC]

    def part(at, size, tail):
        return pl.BlockSpec((1,) + tail, lambda e: (jnp.clip(e - at, 0, size - 1),) + (0,) * len(tail))

    at = 0
    for i, size in enumerate(PARTS):
        tail = (2, width, hidden) if i == 0 else (width, hidden)
        copies = 1 if i == 0 else 2
        outs += [sds((size,) + tail, BF16)] * copies
        out_specs += [part(at, size, tail)] * copies
        at += size
    return call(
        expert_kernel,
        tuple(outs),
        [pltpu.VMEM((most, 2 * width), BF16), pltpu.VMEM((most, 2 * width), BF16)],
        "experts",
        22, limit=28,
        grid=(experts,),
        in_specs=[
            SMEM_SPEC,
            SMEM_SPEC,
            VMEM_SPEC,
            PLAIN_SPEC,
            pl.BlockSpec((1, width, hidden), lambda e: (e, 0, 0)),
            pl.BlockSpec((1, hidden, width), lambda e: (e, 0, 0)),
            VMEM_SPEC,
        ],
        out_specs=tuple(out_specs),
    )(plan, where, own, oth, w_in, w_out, wr)


def unsort_kernel(where_ref, mine_ref, got_ref, unpick_ref, keep_ref, send_ref, y_s):
    count = mine_ref.shape[0]
    cpad, width = y_s.shape
    y_s[0:count, :] = (mine_ref[:, 0:width].astype(F32) + got_ref[:, 0:width].astype(F32)).astype(BF16)
    if cpad > count:
        y_s[count:cpad, :] = jnp.zeros((cpad - count, width), BF16)
    side = where_ref[1]
    send_ref[...] = mm(unpick_ref[1 - side], y_s[...]).astype(BF16)
    keep_ref[...] = mm(unpick_ref[side], y_s[...]).astype(BF16)


def run_unsort(where, mine, got, unpick):
    width = mine.shape[1] // 2
    half, cpad = unpick.shape[1:]
    outs = (sds((half, width), BF16), sds((half, width), BF16))
    return call(
        unsort_kernel, outs, [pltpu.VMEM((cpad, width), BF16)], "unsort", 4, limit=12,
        in_specs=[SMEM_SPEC, VMEM_SPEC, PLAIN_SPEC, VMEM_SPEC], out_specs=(VMEM_SPEC, PLAIN_SPEC),
    )(where, mine, got, unpick)


def unsort_out_kernel(mine_ref, got_ref, pos_ref, ex_ref, y_s):
    count = mine_ref.shape[0]
    half = ex_ref.shape[0] // 2
    columns = jnp.broadcast_to(pos_ref[0:1, :], (LANES, pos_ref.shape[1])).T
    cpad, width = y_s.shape
    y_s[0:count, :] = (mine_ref[:, width:].astype(F32) + got_ref[:, width:].astype(F32)).astype(BF16)
    if cpad > count:
        y_s[count:cpad, :] = jnp.zeros((cpad - count, width), BF16)
    for part in range(2):
        rows = mm(unpick_part(columns, part, half, cpad), y_s[...]).astype(BF16)
        for i in range(half // STRIP):
            at = (2 * i + part) * STRIP
            ex_ref[at : at + STRIP, :] = rows[i * STRIP : (i + 1) * STRIP]


def run_unsort_out(mine, got, pos, own, after):
    count, width = mine.shape[0], mine.shape[1] // 2
    cpad = up(count, LANES)
    return call(
        unsort_out_kernel, sds((own, width), BF16), [pltpu.VMEM((cpad, width), BF16)], "unsort_out", 3, limit=12,
        in_specs=[VMEM_SPEC, PLAIN_SPEC, VMEM_SPEC], out_specs=PLAIN_SPEC, after=after,
    )(mine, got, pos)


def out_kernel(mid_ref, mine_ref, got_ref, out_ref):
    out_ref[...] = (mid_ref[...] + (mine_ref[...].astype(F32) + got_ref[...].astype(F32))).astype(BF16)


def run_out(mid, mine, got, after):
    return call(
        out_kernel, sds(mid.shape, BF16), [], "block_out", 2, limit=12,
        in_specs=[FAR_SPEC, PLAIN_SPEC, PLAIN_SPEC], out_specs=PLAIN_SPEC, after=after,
    )(mid, mine, got)


def join_kernel(where_ref, mine_ref, other_ref, out_ref, sems):
    own = mine_ref.shape[0]
    core = where_ref[0]
    copies = [
        pltpu.make_async_copy(ref, out_ref.at[pl.ds(pl.multiple_of(place * own, GRAIN), own), :], sems.at[i])
        for i, (ref, place) in enumerate(((mine_ref, core), (other_ref, 1 - core)))
    ]
    for copy in copies:
        copy.start()
    for copy in copies:
        copy.wait()


def run_join(where, mine, other, after):
    own, width = mine.shape
    return call(
        join_kernel, sds((2 * own, width), BF16), [pltpu.SemaphoreType.DMA((2,))], "join", 2, limit=4,
        in_specs=[SMEM_SPEC, PLAIN_SPEC, PLAIN_SPEC], out_specs=FAR_ANY, after=after,
    )(where, mine, other)


def mid_back_kernel(where_ref, keep_ref, got_ref, mid_ref, cot_ref, gain2_ref, gmid_ref, ga_ref, part_ref, cot_s, mid_s, sems):
    half = keep_ref.shape[0]
    core, side = where_ref[0], where_ref[1]
    mid_copy = strip_copy(mid_ref, 0, side, mid_s, sems.at[0])
    mid_copy.start()
    copy = strip_copy(cot_ref, core * (half // STRIP), side, cot_s, sems.at[1])
    copy.start()
    grad_h2 = keep_ref[...].astype(F32) + got_ref[...].astype(F32)
    mid_copy.wait()
    normed2, scale2 = normalize_rows(mid_s[...].reshape(half, -1))
    part_ref[...] = jnp.broadcast_to(jnp.sum(grad_h2 * normed2, 0, keepdims=True), part_ref.shape)
    copy.wait()
    grad_final = cot_s[...].reshape(half, -1).astype(F32)
    grad_mid = grad_final + normal_back(grad_h2, normed2, scale2, gain2_ref[...])
    gmid_ref[...] = grad_mid
    ga_ref[...] = grad_mid.astype(BF16)


def run_mid_back(where, keep, got, mid, cot, gain2):
    half, width = keep.shape
    outs = (sds((half, width), F32), sds((half, width), BF16), sds((8, width), F32))
    return call(
        mid_back_kernel, outs, [pltpu.VMEM((half // STRIP, STRIP, width), dtype) for dtype in (BF16, F32)] + [pltpu.SemaphoreType.DMA((2,))],
        "mid_back", 4, limit=12,
        in_specs=[SMEM_SPEC, VMEM_SPEC, PLAIN_SPEC, FAR_ANY, FAR_ANY, VMEM_SPEC],
        out_specs=(FAR_SPEC, PLAIN_SPEC, VMEM_SPEC),
    )(where, keep, got, in_strips(mid), in_strips(cot), gain2)


def back_kernel(
    len_ref, where_ref, ga_ref, gao_ref, ho_any, q_any, lse_any, k_any, kt_any, v_any, hid_any, w3_ref, wproj_ref,
    hkeep_ref, hsend_ref, dqt_ref, dkt_ref, dvt_ref, ga_s, hid_s, ho_s,
    segk_s, qm_s, dm_s, dq_s, dk_s, dv_s, q_s, do_s, lse_s, d_s, gh_s, col_s,
    k_ref, v_ref, kt_ref, hoc_s, lsec_s, qc_s, hidc_s, sems,
):
    half, width = ga_ref.shape
    rows = 4 * half
    own = 2 * half
    kpad = k_ref.shape[0]
    cpad = ga_s.shape[0]
    mine = w3_ref.shape[2]
    heads = mine // 64
    core, side = where_ref[0], where_ref[1]
    ends = seq_ends(len_ref, len_ref.shape[1])
    scale = 1.0 / math.sqrt(width // HEADS)

    strips_of = (hoc_s, lsec_s, qc_s, hidc_s)
    copies = [
        strip_copy(ref, 0, side, dst, sems.at[i])
        for i, (ref, dst) in enumerate(zip((ho_any, lse_any, q_any, hid_any), strips_of))
    ] + [
        pltpu.make_async_copy(ref, dst, sems.at[4 + i])
        for i, (ref, dst) in enumerate(((k_any, k_ref), (v_any, v_ref), (kt_any, kt_ref)))
    ]
    for copy in copies:
        copy.start()
    key_segments(segk_s, ends, kpad)
    at = pl.multiple_of(core * half, GRAIN)
    ga_s[pl.ds(at, half), :] = ga_ref[...]
    at = pl.multiple_of((1 - core) * half, GRAIN)
    ga_s[pl.ds(at, half), :] = gao_ref[...]
    ga_s[own:cpad, :] = jnp.zeros((cpad - own, width), BF16)
    dk_s[...] = jnp.zeros(dk_s.shape, F32)
    dv_s[...] = jnp.zeros(dv_s.shape, F32)
    for copy in copies:
        copy.wait()
    for src, dst in zip(strips_of, (ho_s, col_s, q_s, hid_s)):
        dst[0:own, :] = src[0 : own // STRIP].reshape(own, -1)
        dst[own:cpad, :] = jnp.zeros((cpad - own, dst.shape[1]), dst.dtype)
    lse_s[...] = col_s[...].T[0:8]
    wproj = wproj_ref[pl.ds(pl.multiple_of(core * mine, GRAIN), mine), :]
    do_s[:, 0:mine] = mm(ga_s[...], wproj, COLS_COLS).astype(BF16)
    do_s[:, mine:] = jnp.zeros((cpad, do_s.shape[1] - mine), BF16)
    sub = lax.broadcasted_iota(jnp.int32, (8, do_s.shape[1]), 0)
    lane = lax.broadcasted_iota(jnp.int32, (8, do_s.shape[1]), 1)
    d_s[...] = lax.dot_general(
        (lane // 64 == sub).astype(F32),
        do_s[...].astype(F32) * ho_s[...].astype(F32),
        COLS_COLS,
        precision=lax.Precision.HIGHEST,
        preferred_element_type=F32,
    )

    def place(index):
        return 2 * STRIP * (index // STRIP) + STRIP * side + index % STRIP

    def q_step(qb, carry):
        first = pl.multiple_of(qb * KB, KB)
        last = jnp.minimum(first + KB, own) - 1
        for h in range(heads):
            mask = head_mask(KB, h % 2)
            qm_s[h] = q_s[pl.ds(first, KB), lane_head(h)] * mask
            dm_s[h] = do_s[pl.ds(first, KB), lane_head(h)] * mask
        dq_s[:, pl.ds(first, KB)] = jnp.zeros((mine, KB), F32)
        low, high = seq_bounds(ends, place(first), place(last))
        start, steps = key_steps(low, high)
        index = lax.broadcasted_iota(jnp.int32, (8, KB), 1) + first
        segq = jnp.where(index < own, segment_of(place(index), ends), -1)[0:1]
        lse = [lse_s[h : h + 1, pl.ds(first, KB)] for h in range(heads)]
        dots = [d_s[h : h + 1, pl.ds(first, KB)] for h in range(heads)]

        def k_step(kb, carry):
            at = pl.multiple_of(start + kb * KB, LANES)
            bias = bias_block(segk_s, at, segq)
            s = [mm(k_ref[pl.ds(at, KB), lane_head(h)], qm_s[h], COLS_COLS) for h in range(heads)]
            dp = [mm(v_ref[pl.ds(at, KB), lane_head(h)], dm_s[h], COLS_COLS) for h in range(heads)]
            p = [jnp.exp((s[h] + bias) - lse[h]) for h in range(heads)]
            ds = [(p[h] * (dp[h] - dots[h])).astype(BF16) for h in range(heads)]
            p = [a.astype(BF16) for a in p]
            dv = [mm(p[h], dm_s[h]) for h in range(heads)]
            dk = [mm(ds[h], qm_s[h]) for h in range(heads)]
            dq = [mm(kt_ref[h * 64 : (h + 1) * 64, pl.ds(at, KB)], ds[h]) for h in range(heads)]
            for ref, add in ((dv_s, dv), (dk_s, dk)):
                for j in range(up(heads, 2) // 2):
                    pair = add[2 * j : 2 * j + 2]
                    ref[pl.ds(at, KB), j * LANES : (j + 1) * LANES] += pair[0] if len(pair) == 1 else pair[0] + pair[1]
            for h in range(heads):
                dq_s[h * 64 : (h + 1) * 64, pl.ds(first, KB)] += dq[h]
            return carry

        lax.fori_loop(0, steps, k_step, 0)
        return carry

    lax.fori_loop(0, cpad // KB, q_step, 0)

    wq, wk, wv = w3_ref[0], w3_ref[1], w3_ref[2]
    dqt = (dq_s[...] * scale).astype(BF16)
    dqt_ref[...] = dqt
    step = rows // 8

    def h_body(i, carry):
        at = pl.ds(pl.multiple_of(i * step, GRAIN), step)
        gh_s[at, :] = mm(dk_s[at, 0:mine].astype(BF16), wk, COLS_COLS) + mm(
            dv_s[at, 0:mine].astype(BF16), wv, COLS_COLS
        )
        return carry

    lax.fori_loop(0, 8, h_body, 0)
    dkt_ref[...] = dk_s[...].astype(BF16).T[0:mine]
    dvt_ref[...] = dv_s[...].astype(BF16).T[0:mine]
    grad_q = mm(dqt.T, wq, COLS_COLS)
    for i in range(own // STRIP):
        at = pl.ds(strip_start(0, i, side), STRIP)
        gh_s[at, :] += grad_q[i * STRIP : (i + 1) * STRIP]
    hkeep_ref[...] = gh_s[pl.ds(pl.multiple_of(core * own, GRAIN), own), :].astype(BF16)
    hsend_ref[...] = gh_s[pl.ds(pl.multiple_of((1 - core) * own, GRAIN), own), :].astype(BF16)

def weight_kernel(
    dqt_ref, dkt_ref, dvt_ref, ga_ref, hidc_ref, hoc_ref, hid_any, groute_ref, gain2_ref, pay_ref, hid_ref, sem
):
    mine = dqt_ref.shape[0]
    width = ga_ref.shape[1]
    copy = pltpu.make_async_copy(hid_any, hid_ref, sem)
    copy.start()
    pay_ref[0:mine, :] = mm(dqt_ref[...], hidc_ref[...]).astype(BF16)
    pay_ref[3 * mine : 4 * mine, :] = mm(hoc_ref[...].T[0:mine], ga_ref[...]).astype(BF16)
    copy.wait()
    pay_ref[mine : 2 * mine, :] = mm(dkt_ref[...], hid_ref[...]).astype(BF16)
    pay_ref[2 * mine : 3 * mine, :] = mm(dvt_ref[...], hid_ref[...]).astype(BF16)
    pay_ref[4 * mine : 4 * mine + 8, :] = groute_ref[...].T[0:8].astype(BF16)
    pay_ref[4 * mine + 8 : 4 * mine + 16, :] = gain2_ref[...].astype(BF16)
    pay_ref[4 * mine + 16 :, :] = jnp.zeros((pay_ref.shape[0] - 4 * mine - 16, width), BF16)


def run_weights(pay_rows, dqt, dkt, dvt, ga, hidc, hoc, hid, groute, gain2, after):
    return call(
        weight_kernel, sds((pay_rows, ga.shape[1]), BF16),
        [pltpu.VMEM(hid.shape, BF16), pltpu.SemaphoreType.DMA], "weights", 4, limit=16,
        in_specs=[VMEM_SPEC] * 6 + [FAR_ANY] + [VMEM_SPEC] * 2, out_specs=PLAIN_SPEC, after=after,
    )(dqt, dkt, dvt, ga, hidc, hoc, hid, groute, gain2)


def run_back(lengths, where, ga, gao, ho, q, lse, k, kt, v, hid, w3, wproj, after):
    half, width = ga.shape
    own = 2 * half
    kpad, lanes = k.shape
    mine = w3.shape[2]
    heads = mine // 64
    cpad = up(own, KB)
    outs = (
        sds((own, width), BF16),
        sds((own, width), BF16),
        sds((mine, cpad), BF16),
        sds((mine, kpad), BF16),
        sds((mine, kpad), BF16),
        sds((cpad, width), BF16),
        sds((cpad, width), BF16),
        sds((cpad, lanes), BF16),
    )
    scratch = [
        pltpu.VMEM((kpad, LANES), jnp.int32),
        pltpu.VMEM((heads, KB, LANES), BF16),
        pltpu.VMEM((heads, KB, LANES), BF16),
        pltpu.VMEM((mine, cpad), F32),
        pltpu.VMEM((kpad, lanes), F32),
        pltpu.VMEM((kpad, lanes), F32),
        pltpu.VMEM((cpad, lanes), BF16),
        pltpu.VMEM((cpad, lanes), BF16),
        pltpu.VMEM((8, cpad), F32),
        pltpu.VMEM((8, cpad), F32),
        pltpu.VMEM((4 * half, width), F32),
        pltpu.VMEM((cpad, LANES), F32),
        pltpu.VMEM((kpad, lanes), BF16),
        pltpu.VMEM((kpad, lanes), BF16),
        pltpu.VMEM((mine, kpad), BF16),
        pltpu.VMEM((own // STRIP, STRIP, lanes), BF16),
        pltpu.VMEM((own // STRIP, STRIP, LANES), F32),
        pltpu.VMEM((own // STRIP, STRIP, lanes), BF16),
        pltpu.VMEM((own // STRIP, STRIP, width), BF16),
        pltpu.SemaphoreType.DMA((7,)),
    ]
    return call(
        back_kernel, outs, scratch, "back", 28,
        in_specs=[SMEM_SPEC, SMEM_SPEC, PLAIN_SPEC, PLAIN_SPEC] + [FAR_ANY] * 7 + [VMEM_SPEC] * 2,
        out_specs=(FAR_SPEC, PLAIN_SPEC) + (VMEM_SPEC,) * 6, limit=32, after=after,
    )(lengths, where, ga, gao, in_strips(ho), in_strips(q), in_strips(lse), k, kt, v, in_strips(hid), w3, wproj)


def token_kernel(where_ref, mine_ref, got_ref, gmid_ref, tok_ref, gain1_ref, out_ref, tok_s, sem):
    half = gmid_ref.shape[0]
    copy = strip_copy(tok_ref, where_ref[0] * (half // STRIP), where_ref[1], tok_s, sem)
    copy.start()
    grad_h1 = mine_ref[...].astype(F32) + got_ref[...].astype(F32)
    copy.wait()
    normed1, scale1 = normalize_rows(tok_s[...].reshape(half, -1).astype(F32))
    out_ref[...] = (gmid_ref[...] + normal_back(grad_h1, normed1, scale1, gain1_ref[...])).astype(BF16)


def run_tokens(where, mine, got, gmid, tokens, gain1, after):
    return call(
        token_kernel, sds(gmid.shape, BF16),
        [pltpu.VMEM((gmid.shape[0] // STRIP, STRIP, gmid.shape[1]), BF16), pltpu.SemaphoreType.DMA], "token_grad", 3, limit=12,
        in_specs=[SMEM_SPEC, FAR_SPEC, PLAIN_SPEC, FAR_SPEC, FAR_ANY, VMEM_SPEC], out_specs=PLAIN_SPEC, after=after,
    )(where, mine, got, gmid, in_strips(tokens), gain1)


def split_kernel(where_ref, a_ref, b_ref, keep_ref, send_ref):
    half = keep_ref.shape[0]
    total = (a_ref[...].astype(F32) + b_ref[...].astype(F32)).astype(BF16)
    side = where_ref[1]
    first, second = strips(total, 0, half), strips(total, 1, half)
    keep_ref[...] = jnp.where(side == 0, first, second)
    send_ref[...] = jnp.where(side == 0, second, first)


def run_split(where, a, b, after):
    own, width = a.shape
    outs = (sds((own // 2, width), BF16),) * 2
    return call(
        split_kernel, outs, [], "split", 2, limit=12, in_specs=[SMEM_SPEC, FAR_SPEC, PLAIN_SPEC],
        out_specs=(FAR_SPEC, PLAIN_SPEC), after=after,
    )(where, a, b)


def weave_kernel(where_ref, mine_ref, other_ref, out_ref):
    side = where_ref[1]
    for i in range(mine_ref.shape[0] // STRIP):
        rows = slice(i * STRIP, (i + 1) * STRIP)
        out_ref[pl.ds(strip_start(0, i, side), STRIP), :] = mine_ref[rows, :]
        out_ref[pl.ds(strip_start(0, i, 1 - side), STRIP), :] = other_ref[rows, :]


def run_weave(where, mine, other, after):
    half, width = mine.shape
    return call(
        weave_kernel, sds((2 * half, width), BF16), [], "weave", 2, limit=8,
        in_specs=[SMEM_SPEC] + [PLAIN_SPEC] * 2, out_specs=PLAIN_SPEC, after=after,
    )(where, mine, other)


def summed_end_kernel(total_ref, gin_ref, gout_ref):
    gin_ref[0] = total_ref[0, 0].astype(F32)
    gout_ref[0] = total_ref[0, 1].astype(F32)


def run_summed_end(total, shape_in, shape_out, after):
    size, unused, width, hidden = total.shape
    block = pl.BlockSpec((1, width, hidden), lambda e: (e, 0, 0))
    return call(
        summed_end_kernel,
        (sds(shape_in, F32), sds(shape_out, F32)),
        [],
        "summed_end",
        4, limit=12,
        grid=(size,),
        in_specs=[pl.BlockSpec((1, 2, width, hidden), lambda e: (e, 0, 0, 0))],
        out_specs=(block, block),
        after=after,
    )(total)


def expert_end_kernel(where_ref, mine_ref, other_ref, *refs):
    gin_ref, gout_ref = refs[-2:]
    e = pl.program_id(0)
    mine = mine_ref[e].astype(F32)
    other = other_ref[e].astype(F32)
    first = where_ref[2] == 0
    gin_ref[0] = jnp.where(first, mine, other)
    gout_ref[0] = jnp.where(first, other, mine)


def run_expert_end(at, where, mine, other, shape_in, shape_out, before):
    size, width, hidden = mine.shape
    block = pl.BlockSpec((1, width, hidden), lambda e: (e + at, 0, 0))
    return call(
        expert_end_kernel,
        (sds(shape_in, F32), sds(shape_out, F32)),
        [],
        "expert_end",
        3, limit=12,
        grid=(size,),
        in_specs=[SMEM_SPEC, PLAIN_SPEC, PLAIN_SPEC] + [FAR_ANY] * 2,
        out_specs=(block, block),
        input_output_aliases={3: 0, 4: 1},
    )(where, mine, other, *before)


def total_kernel(parts_ref, out_ref):
    pieces = parts_ref.shape[0]
    total = parts_ref[0].astype(F32)
    for i in range(1, pieces):
        total = total + parts_ref[i].astype(F32)
    total = total.astype(BF16)
    for i in range(pieces):
        out_ref[i] = total


def run_total(parts, after):
    return call(
        total_kernel, sds(parts.shape, BF16), [], "total", 2, limit=8, in_specs=[PLAIN_SPEC], out_specs=PLAIN_SPEC, after=after
    )(parts)


def attn_end_kernel(where_ref, mine_ref, other_ref, wqkv_ref, gain1_ref, gqkv_ref, gproj_ref, g1_ref, g2_ref, groute_ref):
    width = wqkv_ref.shape[1]
    share = width // 2
    first = where_ref[0] == 0
    mine = mine_ref[...].astype(F32)
    other = other_ref[...].astype(F32)
    low = jnp.where(first, mine, other)
    high = jnp.where(first, other, mine)
    product = jnp.zeros((width, width), F32)
    for i in range(3):
        rows = slice(i * share, (i + 1) * share)
        part = jnp.concatenate([low[rows], high[rows]], 0).T
        gqkv_ref[:, i, :] = part
        product = product + part * wqkv_ref[i].astype(F32)
    gproj_ref[...] = jnp.concatenate([low[3 * share : 4 * share], high[3 * share : 4 * share]], 0)
    g1_ref[...] = jnp.sum(product.T, 0, keepdims=True) / gain1_ref[...]
    small = low[4 * share : 4 * share + 16] + high[4 * share : 4 * share + 16]
    groute_ref[...] = small[0:8]
    g2_ref[...] = small[8:9]


def run_attn_end(where, mine, other, wqkv, gain1, after):
    width = wqkv.shape[1]
    outs = (
        sds((width, 3, width), F32),
        sds((width, width), F32),
        sds((1, width), F32),
        sds((1, width), F32),
        sds((8, width), F32),
    )
    return call(
        attn_end_kernel, outs, [], "attn_end", 4, limit=16, in_specs=[SMEM_SPEC, PLAIN_SPEC, PLAIN_SPEC, VMEM_SPEC, VMEM_SPEC],
        out_specs=(FAR_SPEC,) * 5, after=after,
    )(where, mine, other, wqkv, gain1)


def swap(value, axis, mask):
    size = lax.axis_size(axis)
    return lax.ppermute(value, axis, [(i, i ^ mask) for i in range(size)])


def add_kernel(a_ref, b_ref, out_ref):
    out_ref[...] = (a_ref[...].astype(F32) + b_ref[...].astype(F32)).astype(BF16)


def added(a, b, after):
    return call(
        add_kernel, sds(a.shape, BF16), [], "add", 2, limit=8, in_specs=[PLAIN_SPEC] * 2, out_specs=PLAIN_SPEC, after=after
    )(a, b)


def choose_kernel(where_ref, inner_ref, outer_ref, out_ref):
    @pl.when(where_ref[3] == 0)
    def _():
        out_ref[...] = inner_ref[...]

    @pl.when(where_ref[3] != 0)
    def _():
        out_ref[...] = outer_ref[...]


def chosen(where, inner, outer, after):
    return call(
        choose_kernel, sds(inner.shape, BF16), [], "choose", 2, limit=8,
        in_specs=[SMEM_SPEC, PLAIN_SPEC, PLAIN_SPEC], out_specs=PLAIN_SPEC, after=after,
    )(where, inner, outer)


def wide_step(value, step):
    inward = [(w, w + 2) for w in (0, 1)] + [(w, w - 2) for w in (6, 7)]
    if step == 0:
        return lax.ppermute(value, "wide", inward)
    if step == 1:
        return lax.ppermute(value, "wide", [(2, 4), (3, 5), (4, 2), (5, 3)])
    return lax.ppermute(value, "wide", [(b, a) for a, b in inward])


def on_device(
    tokens, w_qkv, w_proj, norm1_gain, norm2_gain, w_route, w_in, w_out, cotangent, routes, kept_mask, lengths
):
    rows, width = tokens.shape
    own, half = rows // 2, rows // 4
    experts = w_in.shape[0]
    core, side = lax.axis_index("lo"), lax.axis_index("hi")
    wide_size, w = lax.axis_size("wide"), lax.axis_index("wide")
    z = w // 2
    outer = ((z == 0) | (z == wide_size // 2 - 1)).astype(jnp.int32)
    where = jnp.stack([core, side, w % 2, outer]).astype(jnp.int32)

    wqkv = w_qkv.transpose(1, 0, 2)
    w3 = lax.dynamic_slice_in_dim(wqkv, core * (width // 2), width // 2, 2)
    wr = jnp.pad(w_route, ((0, 0), (0, LANES - experts)))
    gain1 = norm1_gain.reshape(1, width)
    gain2 = norm2_gain.reshape(1, width)
    code = jnp.where(kept_mask == 1, routes[:, 0], experts).reshape(2, 1, own)
    code = jnp.pad(code, ((0, 0), (0, 0), (0, up(own, LANES) - own)), constant_values=experts)

    hid, k, kt, v, q, ho, lse, keep, send = run_front(lengths, where, tokens, w3, w_proj, gain1)
    got = swap(send, "lo", 1)
    plan, pos = run_plan(where, code, (keep, ANY_SPEC))
    mid, own_x, own_send = run_mid(where, keep, got, tokens, cotangent, gain2, wr, code, pos)
    oth_x = swap(own_send, "lo", 1)

    yown, yoth, groute, grads_a, *pairs = run_experts(plan, where, own_x, oth_x, w_in, w_out, wr)
    got = swap(yoth, "lo", 1)
    total_a = lax.psum(grads_a, "wide")
    pairs = [(pairs[2 * i], pairs[2 * i + 1]) for i in range(len(pairs) // 2)]
    recvs = [swap(give, "wide", 1) for unused, give in pairs]

    unpick = run_unpick(pos, own, own_x.shape[0], (yoth, ANY_SPEC))
    keep, send = run_unsort(where, yown, got, unpick)
    gh2 = swap(send, "hi", 1)
    gmid, ga, gain2_part = run_mid_back(where, keep, gh2, mid, cotangent, gain2)
    gao = swap(ga, "lo", 1)
    ex = run_unsort_out(yown, got, pos, own, (ga, ANY_SPEC))
    ex_got = swap(ex, "hi", 1)

    hkeep, hsend, dqt, dkt, dvt, ga_c, hid_c, ho_c = run_back(
        lengths, where, ga, gao, ho, q, lse, k, kt, v, hid, w3, w_proj, (ex, ANY_SPEC)
    )
    hgot = swap(hsend, "lo", 1)
    last = hsend, ANY_SPEC
    line = wide_size == 8
    sums = []
    for (mine, unused), recv in zip(pairs, recvs):
        mine = added(mine, recv, last)
        if not line:
            for i in range(1, wide_size.bit_length() - 1):
                mine = added(mine, swap(mine, "wide", 1 << i), last)
        last = mine, ANY_SPEC
        sums.append(mine)
    moved = [wide_step(a, 0) for a in sums] if line else sums
    pay_rows = up(2 * width + 16, 8 * lax.axis_size(("wide", "hi")))
    pay = run_weights(pay_rows, dqt, dkt, dvt, ga_c, hid_c, ho_c, hid, groute, gain2_part, last)
    count = pay_rows // lax.axis_size(("wide", "hi"))
    pay_got = lax.all_to_all(pay.reshape(-1, count, width), ("wide", "hi"), 0, 0)
    hk, hs = run_split(where, hkeep, hgot, (pay, ANY_SPEC))
    hs_got = swap(hs, "hi", 1)
    last = hs, ANY_SPEC
    if line:
        for i in range(len(sums)):
            sums[i] = added(sums[i], moved[i], last)
            last = sums[i], ANY_SPEC
            moved[i] = wide_step(sums[i], 1)
    mine = run_out(mid, ex, ex_got, last)
    other = swap(mine, "lo", 1)
    pay_got = run_total(pay_got, (mine, ANY_SPEC))
    last = pay_got, ANY_SPEC
    pay_got = lax.all_to_all(pay_got, ("wide", "hi"), 0, 0).reshape(pay.shape)
    token_rows = run_tokens(where, hk, hs_got, gmid, tokens, gain1, last)
    last = token_rows, ANY_SPEC
    token_got = swap(token_rows, "hi", 1)
    layer_out = run_join(where, mine, other, last)
    last = layer_out, FAR_ANY
    if line:
        for i in range(len(sums)):
            sums[i] = added(sums[i], moved[i], last)
            last = sums[i], ANY_SPEC
            moved[i] = wide_step(sums[i], 2)
    token_own = run_weave(where, token_rows, token_got, last)
    last = token_own, ANY_SPEC
    token_oth = swap(token_own, "lo", 1)
    if line:
        for i in range(len(sums)):
            sums[i] = chosen(where, sums[i], moved[i], last)
            last = sums[i], ANY_SPEC
    others = [swap(a, "wide", 1) for a in sums]
    pay_oth = swap(pay_got, "lo", 1)
    grad_tokens = run_join(where, token_own, token_oth, last)
    last = grad_tokens, FAR_ANY
    grad_qkv, grad_proj, grad_norm1, grad_norm2, route_t = run_attn_end(where, pay_got, pay_oth, wqkv, gain1, last)
    before = run_summed_end(total_a, w_in.shape, w_out.shape, (grad_proj, FAR_ANY))
    at = PARTS[0]
    for mine, other, size in zip(sums, others, PARTS[1:]):
        before = run_expert_end(at, where, mine, other, w_in.shape, w_out.shape, before)
        at += size
    grad_in, grad_out = before

    return (
        layer_out,
        grad_tokens,
        grad_qkv,
        grad_proj,
        grad_norm1.reshape(width),
        grad_norm2.reshape(width),
        route_t.T,
        grad_in,
        grad_out,
    )


def solution(mesh):
    axes = ("wide", ("hi", "lo"))
    split = Mesh(mesh.devices.reshape(mesh.shape["wide"], -1, 2), ("wide", "hi", "lo"))
    wide, narrow = axes
    in_specs = (
        P(wide, None),
        P(),
        P(),
        P(),
        P(),
        P(),
        P(None, None, narrow),
        P(None, narrow, None),
        P(wide, None),
        P(wide, None),
        P(wide),
        P(wide, None),
    )
    out_specs = (
        P(wide, None),
        P(wide, None),
        P(),
        P(),
        P(),
        P(),
        P(),
        P(None, None, narrow),
        P(None, narrow, None),
    )
    return jax.shard_map(on_device, mesh=split, in_specs=in_specs, out_specs=out_specs, check_vma=False)
```

```python
import math

import jax
import jax.numpy as jnp
from jax import lax
from jax.experimental import pallas as pl
from jax.experimental.pallas import tpu as pltpu
from jax.sharding import Mesh, PartitionSpec as P

HEADS = 6
CAP = 408
EPS = 1e-06
NEG = -1e30
F32 = jnp.float32
BF16 = jnp.bfloat16
LANES = 128
KB = 256
GRAIN = 16
STRIP = 32
FLOPS = 10**10
PARTS = (2, 2, 2, 2)
FIRST_TILES = 2
GELU_A = math.sqrt(2.0 / math.pi)
GELU_B = 0.044715

ROWS_COLS = (((1,), (0,)), ((), ()))
COLS_COLS = (((1,), (1,)), ((), ()))
ROWS_ROWS = (((0,), (0,)), ((), ()))


def up(value, grain):
    return -(-value // grain) * grain


def mm(a, b, dims=ROWS_COLS):
    return lax.dot_general(a, b, dims, preferred_element_type=F32)


def normalize_rows(values):
    centre = values - jnp.mean(values, -1, keepdims=True)
    row_scale = lax.rsqrt(jnp.mean(centre * centre, -1, keepdims=True) + EPS)
    return centre * row_scale, row_scale


def normal_back(grad_h, normed, row_scale, gain_row):
    g = grad_h * gain_row
    return row_scale * (
        g - jnp.mean(g, -1, keepdims=True) - normed * jnp.mean(g * normed, -1, keepdims=True)
    )


def lane_head(h):
    return slice((h // 2) * LANES, (h // 2 + 1) * LANES)


def seq_ends(len_ref, count):
    ends = []
    total = jnp.int32(0)
    for j in range(count):
        total = total + len_ref[0, j]
        ends.append(total)
    return ends


def seq_bounds(ends, first_row, last_row):
    low = jnp.int32(0)
    high = ends[-1]
    for end in ends:
        low = jnp.where(end <= first_row, end, low)
    for end in reversed(ends):
        high = jnp.where(end > last_row, end, high)
    return low, high


def segment_of(index, ends):
    seg = jnp.zeros(index.shape, jnp.int32)
    for end in ends:
        seg = seg + (index >= end).astype(jnp.int32)
    return seg


def key_segments(segk_ref, ends, kpad):
    def body(i, carry):
        start = pl.multiple_of(i * LANES, LANES)
        index = lax.broadcasted_iota(jnp.int32, (LANES, LANES), 0) + start
        segk_ref[pl.ds(start, LANES), :] = segment_of(index, ends)
        return carry

    lax.fori_loop(0, kpad // LANES, body, 0)


def bias_block(segk_ref, kstart, segq):
    segk = segk_ref[pl.ds(kstart, KB), :]
    return jnp.where(jnp.concatenate([segk, segk], 1) == segq, 0.0, NEG)


def head_mask(rows, odd):
    lane = lax.broadcasted_iota(jnp.int32, (rows, LANES), 1)
    return ((lane >= 64) if odd else (lane < 64)).astype(BF16)


def plan_of(code_row, experts):
    n = code_row.shape[1]
    sub = lax.broadcasted_iota(jnp.int32, (experts, n), 0)
    lane = lax.broadcasted_iota(jnp.int32, (experts, n), 1)
    member = (code_row == sub).astype(F32)
    rank = member
    shift = 1
    while shift < n:
        rank = rank + jnp.where(lane >= shift, pltpu.roll(rank, shift, 1), 0.0)
        shift *= 2
    counts = jnp.broadcast_to(rank[:, n - 1 : n], (experts, LANES))
    sizes = jnp.floor((counts + (GRAIN - 1)) * (1.0 / GRAIN)) * GRAIN
    row = lax.broadcasted_iota(jnp.int32, (experts, LANES), 0)
    total = sizes
    shift = 1
    while shift < experts:
        total = total + jnp.where(row >= shift, pltpu.roll(total, shift, 0), 0.0)
        shift *= 2
    offsets = total - sizes
    pos = jnp.sum(member * (rank + offsets[:, 0:1]), 0, keepdims=True) - 1.0
    return pos, offsets, sizes


def key_steps(low, high):
    start = low // LANES * LANES
    return start, (high - start + KB - 1) // KB


def plan_kernel(where_ref, code_ref, plan_ref, pos_ref):
    experts = 8
    core = where_ref[0]
    pos, offsets, sizes = plan_of(code_ref[core], experts)
    unused, other_offsets, other_sizes = plan_of(code_ref[1 - core], experts)
    plan_ref[0:8, :] = offsets.astype(jnp.int32)
    plan_ref[8:16, :] = sizes.astype(jnp.int32)
    plan_ref[16:24, :] = other_offsets.astype(jnp.int32)
    plan_ref[24:32, :] = other_sizes.astype(jnp.int32)
    pos_ref[...] = jnp.broadcast_to(pos, pos_ref.shape)


def unpick_part(columns, part, half, cpad):
    lane = lax.broadcasted_iota(jnp.int32, (half, LANES), 1).astype(F32)
    column = strips(columns, part, half)
    return jnp.concatenate(
        [jnp.where(column == lane + float(j * LANES), 1.0, 0.0).astype(BF16) for j in range(cpad // LANES)], 1
    )


def unpick_kernel(pos_ref, unpick_ref):
    half, cpad = unpick_ref.shape[1:]
    columns = jnp.broadcast_to(pos_ref[0:1, :], (LANES, pos_ref.shape[1])).T
    for part in range(2):
        unpick_ref[part] = unpick_part(columns, part, half, cpad)


def run_unpick(pos, own, count, after):
    return call(
        unpick_kernel, sds((2, own // 2, up(count, LANES)), BF16), [], "unpick", 2, limit=12,
        in_specs=[VMEM_SPEC], after=after,
    )(pos)


def strips(value, part, half):
    return jnp.concatenate(
        [value[(2 * i + part) * STRIP : (2 * i + part + 1) * STRIP] for i in range(half // STRIP)], 0
    )


def strip_start(base, i, side):
    return pl.multiple_of(base + 2 * STRIP * i + STRIP * side, STRIP)


def in_strips(array):
    return array.reshape(-1, 2, STRIP, array.shape[-1])


def strip_copy(ref, first, side, dst, sem):
    return pltpu.make_async_copy(ref.at[pl.ds(first, dst.shape[0]), side], dst, sem)


def load_strips(ref, base, side, half):
    return jnp.concatenate([ref[pl.ds(strip_start(base, i, side), STRIP), :] for i in range(half // STRIP)], 0)


def front_kernel(
    len_ref, where_ref, tok_ref, w3_ref, wproj_ref, gain1_ref,
    hid_out, k_out, kt_out, v_out, q_out, ho_out, lse_out, keep_ref, send_ref,
    hid_ref, k_ref, kt_ref, v_ref, q_ref, ho_ref, lse_ref,
    vt_s, segk_s, qm_s, acc_s, m_s, l_s, s_s, st_s, sems,
):
    rows, width = tok_ref.shape
    own = rows // 2
    copies = [
        pltpu.make_async_copy(src, dst, sems.at[i])
        for i, (src, dst) in enumerate(
            (
                (hid_ref, hid_out), (k_ref, k_out), (kt_ref, kt_out), (v_ref, v_out), (q_ref, q_out),
                (ho_ref, ho_out), (lse_ref, lse_out),
            )
        )
    ]
    kpad = hid_ref.shape[0]
    qpad = q_ref.shape[0]
    mine = w3_ref.shape[2]
    heads = mine // 64
    core = where_ref[0]
    ends = seq_ends(len_ref, len_ref.shape[1])
    scale = 1.0 / math.sqrt(width // HEADS)
    key_segments(segk_s, ends, kpad)
    gain1 = gain1_ref[...]
    wq, wk, wv = w3_ref[0], w3_ref[1], w3_ref[2]
    step = rows // 4

    def norm_body(i, carry):
        at = pl.ds(pl.multiple_of(i * step, GRAIN), step)
        normed, unused = normalize_rows(tok_ref[at, :].astype(F32))
        hid = (normed * gain1).astype(BF16)
        hid_ref[at, :] = hid
        k_ref[at, 0:mine] = mm(hid, wk).astype(BF16)
        v_ref[at, 0:mine] = mm(hid, wv).astype(BF16)
        q_ref[at, 0:mine] = (mm(hid, wq).astype(BF16).astype(F32) * scale).astype(BF16)
        return carry

    lax.fori_loop(0, 4, norm_body, 0)
    hid_ref[rows:kpad, :] = jnp.zeros((kpad - rows, width), BF16)
    for ref in (k_ref, v_ref, q_ref):
        size = ref.shape[0]
        ref[rows:size, 0:mine] = jnp.zeros((size - rows, mine), BF16)
        ref[:, mine:] = jnp.zeros((size, ref.shape[1] - mine), BF16)
    wkt = wk.T
    wvt = wv.T

    def key_body(i, carry):
        at = pl.ds(pl.multiple_of(i * 2 * KB, 2 * KB), 2 * KB)
        hid = hid_ref[at, :]
        kt_ref[:, at] = mm(wkt, hid, COLS_COLS).astype(BF16)
        vt_s[:, at] = mm(wvt, hid, COLS_COLS).astype(BF16)
        return carry

    lax.fori_loop(0, kpad // (2 * KB), key_body, 0)
    for copy in copies[:5]:
        copy.start()
    st_s[...] = jnp.zeros(st_s.shape, F32)

    def q_step(qb, carry):
        first = pl.multiple_of(qb * KB, KB)
        last = jnp.minimum(first + KB, rows) - 1
        for h in range(heads):
            qm_s[h] = q_ref[pl.ds(first, KB), lane_head(h)] * head_mask(KB, h % 2)
        for h in range(heads):
            m_s[h : h + 1] = jnp.full((1, KB), NEG, F32)
            l_s[h : h + 1] = jnp.zeros((1, KB), F32)
        acc_s[...] = jnp.zeros(acc_s.shape, F32)
        low, high = seq_bounds(ends, first, last)
        start, steps = key_steps(low, high)
        segq = segment_of(lax.broadcasted_iota(jnp.int32, (8, KB), 1) + first, ends)[0:1]

        def scores(at):
            return [mm(k_ref[pl.ds(at, KB), lane_head(h)], qm_s[h], COLS_COLS) for h in range(heads)]

        for h, s in enumerate(scores(pl.multiple_of(start, LANES))):
            s_s[h] = s

        def k_step(kb, carry):
            at = pl.multiple_of(start + kb * KB, LANES)
            later = pl.multiple_of(start + jnp.minimum(kb + 1, steps - 1) * KB, LANES)
            bias = bias_block(segk_s, at, segq)
            now = [s_s[h] + bias for h in range(heads)]
            nexts = scores(later)
            m_old = [m_s[h : h + 1] for h in range(heads)]
            m_new = [jnp.maximum(m, jnp.max(s, 0, keepdims=True)) for m, s in zip(m_old, now)]
            p = [jnp.exp(s - m) for s, m in zip(now, m_new)]
            alpha = [jnp.exp(a - b) for a, b in zip(m_old, m_new)]
            for h in range(heads):
                m_s[h : h + 1] = m_new[h]
                l_s[h : h + 1] = l_s[h : h + 1] * alpha[h] + jnp.sum(p[h], 0, keepdims=True)
            out = [mm(vt_s[h * 64 : (h + 1) * 64, pl.ds(at, KB)], p[h].astype(BF16)) for h in range(heads)]
            for h in range(heads):
                acc_s[h * 64 : (h + 1) * 64] = acc_s[h * 64 : (h + 1) * 64] * alpha[h] + out[h]
                s_s[h] = nexts[h]
            return carry

        lax.fori_loop(0, steps, k_step, 0)
        parts = []
        for h in range(heads):
            total = l_s[h : h + 1]
            st_s[h : h + 1] = m_s[h : h + 1] + jnp.log(total)
            parts.append(acc_s[h * 64 : (h + 1) * 64] * (1.0 / total))
        lse_ref[pl.ds(first, KB), :] = st_s[...].T
        parts.append(jnp.zeros((ho_ref.shape[1] - mine, KB), F32))
        ho_ref[pl.ds(first, KB), :] = jnp.concatenate(parts, 0).T.astype(BF16)
        return carry

    lax.fori_loop(0, qpad // KB, q_step, 0)
    for copy in copies[5:]:
        copy.start()
    wproj = wproj_ref[pl.ds(pl.multiple_of(core * mine, GRAIN), mine), :]
    keep_ref[...] = mm(ho_ref[pl.ds(pl.multiple_of(core * own, GRAIN), own), 0:mine], wproj).astype(BF16)
    send_ref[...] = mm(ho_ref[pl.ds(pl.multiple_of((1 - core) * own, GRAIN), own), 0:mine], wproj).astype(BF16)
    for copy in copies:
        copy.wait()


def mid_kernel(
    where_ref, keep_ref, got_ref, tok_ref, cot_ref, gain2_ref, wr_ref, code_ref, pos_ref,
    mid_ref, sorted_ref, send_ref, x_s, tok_s, cot_s, mid_s, sems,
):
    own, width = keep_ref.shape
    npad = x_s.shape[0]
    core = where_ref[0]
    at = pl.ds(pl.multiple_of(core * own, GRAIN), own)
    tok_copy = pltpu.make_async_copy(tok_ref.at[at, :], tok_s, sems.at[0])
    cot_copy = pltpu.make_async_copy(cot_ref.at[at, :], cot_s, sems.at[1])
    tok_copy.start()
    cot_copy.start()
    tok_copy.wait()
    mid = tok_s[...].astype(F32) + (keep_ref[...].astype(F32) + got_ref[...].astype(F32))
    mid_s[...] = mid
    mid_copy = pltpu.make_async_copy(mid_s, mid_ref, sems.at[6])
    mid_copy.start()
    normed2, unused = normalize_rows(mid)
    hidden2 = (normed2 * gain2_ref[...]).astype(BF16)
    lane = lax.broadcasted_iota(jnp.int32, (own, LANES), 1)
    gates = router_gates(hidden2, wr_ref[...], lane, 8)
    code_col = jnp.broadcast_to(code_ref[core].astype(F32), (LANES, npad)).T[0:own]
    gate = jnp.sum(jnp.where(code_col == lane.astype(F32), gates, 0.0), -1, keepdims=True)
    x_s[0:own, 0:width] = hidden2
    cot_copy.wait()
    x_s[0:own, width:] = (gate * cot_s[...].astype(F32)).astype(BF16)
    x_s[own:npad, :] = jnp.zeros((npad - own, 2 * width), BF16)
    piece = sorted_ref.shape[0] // 4
    copies = []
    for i in range(4):
        rows = slice(i * piece, (i + 1) * piece)
        sub = lax.broadcasted_iota(jnp.int32, (piece, npad), 0) + i * piece
        pick = jnp.where(sub.astype(F32) == pos_ref[0:1, :], 1.0, 0.0).astype(BF16)
        sorted_ref[rows, :] = mm(pick, x_s[...]).astype(BF16)
        copies.append(pltpu.make_async_copy(sorted_ref.at[rows, :], send_ref.at[rows, :], sems.at[2 + i]))
        copies[-1].start()
    for copy in copies + [mid_copy]:
        copy.wait()


def router_gates(hidden2, wr, lane, experts):
    logits = jnp.where(lane < experts, mm(hidden2, wr), NEG)
    top = jnp.max(logits, -1, keepdims=True)
    e = jnp.exp(logits - top)
    return e / jnp.sum(e, -1, keepdims=True)


def call(kernel, outs, scratch, name, micros, in_specs, limit=24, after=None, **more):
    def out_of(shape, spec):
        if spec is VMEM_SPEC:
            return pltpu.VMEM(shape.shape, shape.dtype)
        return pltpu.HBM(shape.shape, shape.dtype) if is_far(spec) else shape

    out_specs = more.get("out_specs")
    if out_specs is None:
        out_specs = jax.tree.map(lambda o: VMEM_SPEC, outs)
    if isinstance(outs, tuple):
        outs = tuple(out_of(o, spec) for o, spec in zip(outs, out_specs))
    else:
        outs = out_of(outs, out_specs)
    more["out_specs"] = out_specs
    aliases = more.pop("input_output_aliases", {})
    body = kernel
    if after is not None:
        in_specs = [ANY_SPEC] + list(in_specs)
        aliases = {i + 1: o for i, o in aliases.items()}
        body = lambda after_ref, *refs: kernel(*refs)
    run = pl.pallas_call(
        body,
        out_shape=outs,
        in_specs=in_specs,
        scratch_shapes=scratch,
        name=name,
        input_output_aliases=aliases,
        compiler_params=pltpu.CompilerParams(vmem_limit_bytes=limit * 1024 * 1024),
        cost_estimate=pl.CostEstimate(flops=micros * FLOPS, bytes_accessed=10**4, transcendentals=0),
        **more,
    )

    def place(array, spec):
        if spec is VMEM_SPEC:
            return pltpu.with_memory_space_constraint(array, pltpu.VMEM)
        return pltpu.with_memory_space_constraint(array, pltpu.HBM) if is_far(spec) else array

    def run_on(*args):
        placed = [place(a, spec) for a, spec in zip(args, in_specs[len(in_specs) - len(args) :])]
        if after is not None:
            array, spec = after
            placed = [place(array, spec)] + placed
        return run(*placed)

    return run_on


def is_far(spec):
    return spec is FAR_SPEC or spec is FAR_ANY or spec.block_shape is not None


ANY_SPEC = pl.BlockSpec(memory_space=pl.ANY)
FAR_SPEC = pl.BlockSpec(memory_space=pltpu.VMEM)
FAR_ANY = pl.BlockSpec(memory_space=pl.ANY)
PLAIN_SPEC = pl.BlockSpec(memory_space=pltpu.VMEM)
SMEM_SPEC = pl.BlockSpec(memory_space=pltpu.SMEM)
VMEM_SPEC = pl.BlockSpec(memory_space=pltpu.VMEM)


def sds(shape, dtype):
    return jax.ShapeDtypeStruct(shape, dtype)


def run_plan(where, code, after=None):
    npad = code.shape[2]
    outs = (
        sds((32, LANES), jnp.int32),
        sds((8, npad), F32),
    )
    return call(plan_kernel, outs, [], "plan", 5, limit=12, in_specs=[SMEM_SPEC, VMEM_SPEC], after=after)(where, code)


def run_front(lengths, where, tokens, w3, wproj, gain1):
    rows, width = tokens.shape
    own = rows // 2
    mine = w3.shape[2]
    heads = mine // 64
    kpad = up(rows + KB, 2 * KB)
    qpad = up(rows, KB)
    lanes = up(mine, LANES)
    outs = (
        sds((kpad, width), BF16),
        sds((kpad, lanes), BF16),
        sds((mine, kpad), BF16),
        sds((kpad, lanes), BF16),
        sds((qpad, lanes), BF16),
        sds((qpad, lanes), BF16),
        sds((qpad, LANES), F32),
        sds((own, width), BF16),
        sds((own, width), BF16),
    )
    scratch = [pltpu.VMEM(o.shape, o.dtype) for o in outs[:7]] + [
        pltpu.VMEM((mine, kpad), BF16),
        pltpu.VMEM((kpad, LANES), jnp.int32),
        pltpu.VMEM((heads, KB, LANES), BF16),
        pltpu.VMEM((mine, KB), F32),
        pltpu.VMEM((8, KB), F32),
        pltpu.VMEM((8, KB), F32),
        pltpu.VMEM((heads, KB, KB), F32),
        pltpu.VMEM((LANES, KB), F32),
        pltpu.SemaphoreType.DMA((7,)),
    ]
    return call(
        front_kernel, outs, scratch, "front", 33, in_specs=[SMEM_SPEC, SMEM_SPEC, FAR_SPEC, PLAIN_SPEC, FAR_SPEC, PLAIN_SPEC],
        limit=32,
        out_specs=(FAR_ANY,) * 7 + (PLAIN_SPEC,) * 2,
    )(lengths, where, tokens, w3, wproj, gain1)


def run_mid(where, keep, got, tokens, cot, gain2, wr, code, pos):
    own, width = keep.shape
    count = up(own + 8 * (GRAIN - 1), 4 * GRAIN)
    outs = (sds((own, width), F32),) + (sds((count, 2 * width), BF16),) * 2
    scratch = [
        pltpu.VMEM((code.shape[2], 2 * width), BF16),
        pltpu.VMEM((own, width), BF16),
        pltpu.VMEM((own, width), BF16),
        pltpu.VMEM((own, width), F32),
        pltpu.SemaphoreType.DMA((7,)),
    ]
    return call(
        mid_kernel, outs, scratch, "mid", 9, limit=20,
        in_specs=[SMEM_SPEC, PLAIN_SPEC, PLAIN_SPEC, FAR_ANY, FAR_ANY] + [VMEM_SPEC] * 4,
        out_specs=(FAR_ANY, VMEM_SPEC, ANY_SPEC),
    )(where, keep, got, tokens, cot, gain2, wr, code, pos)


def expert_kernel(
    plan_ref, where_ref, own_ref, oth_ref, win_ref, wout_ref, wr_ref,
    yown_ref, yoth_ref, groute_ref, *refs,
):
    *grads, x_s, y_s = refs
    e = pl.program_id(0)
    width = win_ref.shape[1]
    most = x_s.shape[0]

    @pl.when(e == 0)
    def _():
        yown_ref[...] = jnp.zeros(yown_ref.shape, BF16)
        yoth_ref[...] = jnp.zeros(yoth_ref.shape, BF16)
        groute_ref[...] = jnp.zeros(groute_ref.shape, F32)

    own_at, own_size = plan_ref[e, 0], plan_ref[8 + e, 0]
    oth_at, oth_size = plan_ref[16 + e, 0], plan_ref[24 + e, 0]
    total = own_size + oth_size

    def move(dst, dst_at, src, src_at, size):
        def body(i, carry):
            a = pl.multiple_of(dst_at + i * GRAIN, GRAIN)
            b = pl.multiple_of(src_at + i * GRAIN, GRAIN)
            dst[pl.ds(a, GRAIN), :] = src[pl.ds(b, GRAIN), :]
            return carry

        lax.fori_loop(0, size // GRAIN, body, 0)

    move(x_s, 0, own_ref, own_at, own_size)
    move(x_s, own_size, oth_ref, oth_at, oth_size)

    def work(m):
        def zero_body(i, carry):
            x_s[pl.ds(pl.multiple_of(i * GRAIN, GRAIN), GRAIN), :] = jnp.zeros((GRAIN, 2 * width), BF16)
            return carry

        lax.fori_loop(total // GRAIN, m // GRAIN, zero_body, 0)
        h = x_s[0:m, 0:width]
        g = x_s[0:m, width:]
        w_in = win_ref[0]
        w_out = wout_ref[0]
        lane = lax.broadcasted_iota(jnp.int32, (m, LANES), 1)
        gates = router_gates(h, wr_ref[...], lane, 8)
        here = (lane == e).astype(F32)
        pre = mm(h, w_in)
        t = jnp.tanh(GELU_A * (pre + GELU_B * (pre * pre * pre)))
        act = (0.5 * pre * (1.0 + t)).astype(BF16)
        slope = 0.5 * (1.0 + t) + 0.5 * pre * (1.0 - t * t) * (GELU_A * (1.0 + 3.0 * GELU_B * (pre * pre)))
        out = mm(act, w_out)
        grad_pre = (mm(g, w_out, COLS_COLS) * slope).astype(BF16)
        dot = jnp.sum(g.astype(F32) * out, -1, keepdims=True)
        grad_logits = (dot * (here - gates)).astype(BF16)
        gate = jnp.sum(gates * here, -1, keepdims=True)
        y_s[0:m, 0:width] = (mm(grad_pre, w_in, COLS_COLS) + mm(grad_logits, wr_ref[...], COLS_COLS)).astype(BF16)
        y_s[0:m, width:] = (gate * out).astype(BF16)
        ht = h.T
        groute_ref[...] += mm(ht, grad_logits)
        grad_in = mm(ht, grad_pre).astype(BF16)
        grad_out = mm(act.T, g).astype(BF16)

        at = 0
        for i, size in enumerate(PARTS):
            here = (e >= at) & (e < at + size)
            if i == 0:
                put_both(grads[0], grad_in, grad_out, here)
            else:
                put(grads[2 * i - 1 : 2 * i + 1], grad_in, grad_out, here)
            at += size

    def put_both(ref, grad_in, grad_out, here):
        @pl.when(here)
        def _():
            ref[0, 0] = grad_in
            ref[0, 1] = grad_out

    def put(pair, grad_in, grad_out, here):
        keep_ref, send_ref = pair

        @pl.when(here & (where_ref[2] == 0))
        def _():
            keep_ref[0] = grad_in
            send_ref[0] = grad_out

        @pl.when(here & (where_ref[2] != 0))
        def _():
            keep_ref[0] = grad_out
            send_ref[0] = grad_in

    small = up(CAP * 2 // 3, GRAIN)

    @pl.when(total <= small)
    def _():
        work(small)

    @pl.when(total > small)
    def _():
        work(most)

    move(yown_ref, own_at, y_s, 0, own_size)
    move(yoth_ref, oth_at, y_s, own_size, oth_size)


def run_experts(plan, where, own, oth, w_in, w_out, wr):
    experts, width, hidden = w_in.shape
    count = own.shape[0]
    most = (CAP + 2 * (GRAIN - 1)) // GRAIN * GRAIN
    outs = [sds((count, 2 * width), BF16)] * 2 + [sds((width, LANES), F32)]
    out_specs = [PLAIN_SPEC, PLAIN_SPEC, VMEM_SPEC]

    def part(at, size, tail):
        return pl.BlockSpec((1,) + tail, lambda e: (jnp.clip(e - at, 0, size - 1),) + (0,) * len(tail))

    at = 0
    for i, size in enumerate(PARTS):
        tail = (2, width, hidden) if i == 0 else (width, hidden)
        copies = 1 if i == 0 else 2
        outs += [sds((size,) + tail, BF16)] * copies
        out_specs += [part(at, size, tail)] * copies
        at += size
    return call(
        expert_kernel,
        tuple(outs),
        [pltpu.VMEM((most, 2 * width), BF16), pltpu.VMEM((most, 2 * width), BF16)],
        "experts",
        22, limit=28,
        grid=(experts,),
        in_specs=[
            SMEM_SPEC,
            SMEM_SPEC,
            VMEM_SPEC,
            PLAIN_SPEC,
            pl.BlockSpec((1, width, hidden), lambda e: (e, 0, 0)),
            pl.BlockSpec((1, hidden, width), lambda e: (e, 0, 0)),
            VMEM_SPEC,
        ],
        out_specs=tuple(out_specs),
    )(plan, where, own, oth, w_in, w_out, wr)


def unsort_kernel(where_ref, mine_ref, got_ref, unpick_ref, keep_ref, send_ref, y_s):
    count = mine_ref.shape[0]
    cpad, width = y_s.shape
    y_s[0:count, :] = (mine_ref[:, 0:width].astype(F32) + got_ref[:, 0:width].astype(F32)).astype(BF16)
    if cpad > count:
        y_s[count:cpad, :] = jnp.zeros((cpad - count, width), BF16)
    side = where_ref[1]
    send_ref[...] = mm(unpick_ref[1 - side], y_s[...]).astype(BF16)
    keep_ref[...] = mm(unpick_ref[side], y_s[...]).astype(BF16)


def run_unsort(where, mine, got, unpick):
    width = mine.shape[1] // 2
    half, cpad = unpick.shape[1:]
    outs = (sds((half, width), BF16), sds((half, width), BF16))
    return call(
        unsort_kernel, outs, [pltpu.VMEM((cpad, width), BF16)], "unsort", 4, limit=12,
        in_specs=[SMEM_SPEC, PLAIN_SPEC, PLAIN_SPEC, VMEM_SPEC], out_specs=(VMEM_SPEC, PLAIN_SPEC),
    )(where, mine, got, unpick)


def unsort_out_kernel(mine_ref, got_ref, pos_ref, ex_ref, y_s):
    count = mine_ref.shape[0]
    half = ex_ref.shape[0] // 2
    columns = jnp.broadcast_to(pos_ref[0:1, :], (LANES, pos_ref.shape[1])).T
    cpad, width = y_s.shape
    y_s[0:count, :] = (mine_ref[:, width:].astype(F32) + got_ref[:, width:].astype(F32)).astype(BF16)
    if cpad > count:
        y_s[count:cpad, :] = jnp.zeros((cpad - count, width), BF16)
    for part in range(2):
        rows = mm(unpick_part(columns, part, half, cpad), y_s[...]).astype(BF16)
        for i in range(half // STRIP):
            at = (2 * i + part) * STRIP
            ex_ref[at : at + STRIP, :] = rows[i * STRIP : (i + 1) * STRIP]


def run_unsort_out(mine, got, pos, own, after):
    count, width = mine.shape[0], mine.shape[1] // 2
    cpad = up(count, LANES)
    return call(
        unsort_out_kernel, sds((own, width), BF16), [pltpu.VMEM((cpad, width), BF16)], "unsort_out", 3, limit=12,
        in_specs=[PLAIN_SPEC, PLAIN_SPEC, VMEM_SPEC], out_specs=VMEM_SPEC, after=after,
    )(mine, got, pos)


def out_kernel(mid_ref, mine_ref, got_ref, out_ref):
    out_ref[...] = (mid_ref[...] + (mine_ref[...].astype(F32) + got_ref[...].astype(F32))).astype(BF16)


def run_out(mid, mine, got, after):
    return call(
        out_kernel, sds(mid.shape, BF16), [], "block_out", 2, limit=12,
        in_specs=[FAR_SPEC, PLAIN_SPEC, PLAIN_SPEC], out_specs=PLAIN_SPEC, after=after,
    )(mid, mine, got)


def join_kernel(where_ref, mine_ref, other_ref, out_ref, sems):
    own = mine_ref.shape[0]
    core = where_ref[0]
    copies = [
        pltpu.make_async_copy(ref, out_ref.at[pl.ds(pl.multiple_of(place * own, GRAIN), own), :], sems.at[i])
        for i, (ref, place) in enumerate(((mine_ref, core), (other_ref, 1 - core)))
    ]
    for copy in copies:
        copy.start()
    for copy in copies:
        copy.wait()


def run_join(where, mine, other, after):
    own, width = mine.shape
    return call(
        join_kernel, sds((2 * own, width), BF16), [pltpu.SemaphoreType.DMA((2,))], "join", 2, limit=4,
        in_specs=[SMEM_SPEC, PLAIN_SPEC, PLAIN_SPEC], out_specs=FAR_ANY, after=after,
    )(where, mine, other)


def mid_back_kernel(where_ref, keep_ref, got_ref, mid_ref, cot_ref, gain2_ref, ex_ref, gmid_ref, ga_ref, part_ref, ex_out, cot_s, mid_s, sems):
    half = keep_ref.shape[0]
    core, side = where_ref[0], where_ref[1]
    mid_copy = strip_copy(mid_ref, 0, side, mid_s, sems.at[0])
    mid_copy.start()
    copy = strip_copy(cot_ref, core * (half // STRIP), side, cot_s, sems.at[1])
    copy.start()
    grad_h2 = keep_ref[...].astype(F32) + got_ref[...].astype(F32)
    mid_copy.wait()
    normed2, scale2 = normalize_rows(mid_s[...].reshape(half, -1))
    part_ref[...] = jnp.broadcast_to(jnp.sum(grad_h2 * normed2, 0, keepdims=True), part_ref.shape)
    copy.wait()
    grad_final = cot_s[...].reshape(half, -1).astype(F32)
    grad_mid = grad_final + normal_back(grad_h2, normed2, scale2, gain2_ref[...])
    gmid_ref[...] = grad_mid
    ga_ref[...] = grad_mid.astype(BF16)
    ex_out[...] = ex_ref[...]


def run_mid_back(where, keep, got, mid, cot, gain2, ex, after):
    half, width = keep.shape
    outs = (sds((half, width), F32), sds((half, width), BF16), sds((8, width), F32), sds(ex.shape, BF16))
    return call(
        mid_back_kernel, outs, [pltpu.VMEM((half // STRIP, STRIP, width), dtype) for dtype in (BF16, F32)] + [pltpu.SemaphoreType.DMA((2,))],
        "mid_back", 4, limit=12,
        in_specs=[SMEM_SPEC, VMEM_SPEC, PLAIN_SPEC, FAR_ANY, FAR_ANY, VMEM_SPEC, VMEM_SPEC],
        out_specs=(FAR_SPEC, PLAIN_SPEC, VMEM_SPEC, FAR_SPEC), after=after,
    )(where, keep, got, in_strips(mid), in_strips(cot), gain2, ex)


def back_tiles(
    first_tile, last_tile, ends, side, own, q_s, do_s, lse_s, d_s, k_ref, v_ref, kt_ref,
    segk_s, qm_s, dm_s, dq_s, dk_s, dv_s,
):
    mine = kt_ref.shape[0]
    heads = mine // 64

    def place(index):
        return 2 * STRIP * (index // STRIP) + STRIP * side + index % STRIP

    def q_step(qb, carry):
        first = pl.multiple_of(qb * KB, KB)
        last = jnp.minimum(first + KB, own) - 1
        for h in range(heads):
            mask = head_mask(KB, h % 2)
            qm_s[h] = q_s[pl.ds(first, KB), lane_head(h)] * mask
            dm_s[h] = do_s[pl.ds(first, KB), lane_head(h)] * mask
        dq_s[:, pl.ds(first, KB)] = jnp.zeros((mine, KB), F32)
        low, high = seq_bounds(ends, place(first), place(last))
        start, steps = key_steps(low, high)
        index = lax.broadcasted_iota(jnp.int32, (8, KB), 1) + first
        segq = jnp.where(index < own, segment_of(place(index), ends), -1)[0:1]
        lse = [lse_s[h : h + 1, pl.ds(first, KB)] for h in range(heads)]
        dots = [d_s[h : h + 1, pl.ds(first, KB)] for h in range(heads)]

        def k_step(kb, carry):
            at = pl.multiple_of(start + kb * KB, LANES)
            bias = bias_block(segk_s, at, segq)
            s = [mm(k_ref[pl.ds(at, KB), lane_head(h)], qm_s[h], COLS_COLS) for h in range(heads)]
            dp = [mm(v_ref[pl.ds(at, KB), lane_head(h)], dm_s[h], COLS_COLS) for h in range(heads)]
            p = [jnp.exp((s[h] + bias) - lse[h]) for h in range(heads)]
            ds = [(p[h] * (dp[h] - dots[h])).astype(BF16) for h in range(heads)]
            p = [a.astype(BF16) for a in p]
            dv = [mm(p[h], dm_s[h]) for h in range(heads)]
            dk = [mm(ds[h], qm_s[h]) for h in range(heads)]
            dq = [mm(kt_ref[h * 64 : (h + 1) * 64, pl.ds(at, KB)], ds[h]) for h in range(heads)]
            for ref, add in ((dv_s, dv), (dk_s, dk)):
                for j in range(up(heads, 2) // 2):
                    pair = add[2 * j : 2 * j + 2]
                    ref[pl.ds(at, KB), j * LANES : (j + 1) * LANES] += pair[0] if len(pair) == 1 else pair[0] + pair[1]
            for h in range(heads):
                dq_s[h * 64 : (h + 1) * 64, pl.ds(first, KB)] += dq[h]
            return carry

        lax.fori_loop(0, steps, k_step, 0)
        return carry

    lax.fori_loop(first_tile, last_tile, q_step, 0)


def back_first_kernel(
    len_ref, where_ref, ga_ref, gao_ref, ho_any, q_any, lse_any, k_any, kt_any, v_any, hid_any, wproj_ref,
    ga_s, hid_s, ho_s, q_s, do_s, lse_s, d_s, dq_s, dk_s, dv_s,
    segk_s, qm_s, dm_s, col_s, k_ref, v_ref, kt_ref, hoc_s, lsec_s, qc_s, hidc_s, sems,
):
    half, width = ga_ref.shape
    own = 2 * half
    kpad = k_ref.shape[0]
    cpad = ga_s.shape[0]
    mine = kt_ref.shape[0]
    core, side = where_ref[0], where_ref[1]
    ends = seq_ends(len_ref, len_ref.shape[1])

    strips_of = (hoc_s, lsec_s, qc_s, hidc_s)
    copies = [
        strip_copy(ref, 0, side, dst, sems.at[i])
        for i, (ref, dst) in enumerate(zip((ho_any, lse_any, q_any, hid_any), strips_of))
    ] + [
        pltpu.make_async_copy(ref, dst, sems.at[4 + i])
        for i, (ref, dst) in enumerate(((k_any, k_ref), (v_any, v_ref), (kt_any, kt_ref)))
    ]
    for copy in copies:
        copy.start()
    key_segments(segk_s, ends, kpad)
    at = pl.multiple_of(core * half, GRAIN)
    ga_s[pl.ds(at, half), :] = ga_ref[...]
    at = pl.multiple_of((1 - core) * half, GRAIN)
    ga_s[pl.ds(at, half), :] = gao_ref[...]
    ga_s[own:cpad, :] = jnp.zeros((cpad - own, width), BF16)
    dk_s[...] = jnp.zeros(dk_s.shape, F32)
    dv_s[...] = jnp.zeros(dv_s.shape, F32)
    for copy in copies:
        copy.wait()
    for src, dst in zip(strips_of, (ho_s, col_s, q_s, hid_s)):
        dst[0:own, :] = src[0 : own // STRIP].reshape(own, -1)
        dst[own:cpad, :] = jnp.zeros((cpad - own, dst.shape[1]), dst.dtype)
    lse_s[...] = col_s[...].T[0:8]
    wproj = wproj_ref[pl.ds(pl.multiple_of(core * mine, GRAIN), mine), :]
    do_s[:, 0:mine] = mm(ga_s[...], wproj, COLS_COLS).astype(BF16)
    do_s[:, mine:] = jnp.zeros((cpad, do_s.shape[1] - mine), BF16)
    sub = lax.broadcasted_iota(jnp.int32, (8, do_s.shape[1]), 0)
    lane = lax.broadcasted_iota(jnp.int32, (8, do_s.shape[1]), 1)
    d_s[...] = lax.dot_general(
        (lane // 64 == sub).astype(F32),
        do_s[...].astype(F32) * ho_s[...].astype(F32),
        COLS_COLS,
        precision=lax.Precision.HIGHEST,
        preferred_element_type=F32,
    )

    back_tiles(
        0, FIRST_TILES, ends, side, own, q_s, do_s, lse_s, d_s, k_ref, v_ref, kt_ref,
        segk_s, qm_s, dm_s, dq_s, dk_s, dv_s,
    )


def back_second_kernel(
    len_ref, where_ref, k_any, kt_any, v_any, q_s, do_s, lse_s, d_s, dq_ref, dk_ref, dv_ref, w3_ref,
    hkeep_ref, hsend_ref, dqt_ref, dkt_ref, dvt_ref,
    segk_s, qm_s, dm_s, dq_s, dk_s, dv_s, gh_s, k_ref, v_ref, kt_ref, sems,
):
    own, width = hkeep_ref.shape
    rows = 2 * own
    kpad = k_ref.shape[0]
    cpad = q_s.shape[0]
    mine = w3_ref.shape[2]
    core, side = where_ref[0], where_ref[1]
    ends = seq_ends(len_ref, len_ref.shape[1])
    scale = 1.0 / math.sqrt(width // HEADS)
    copies = [
        pltpu.make_async_copy(ref, dst, sems.at[i])
        for i, (ref, dst) in enumerate(((k_any, k_ref), (v_any, v_ref), (kt_any, kt_ref)))
    ]
    for copy in copies:
        copy.start()
    key_segments(segk_s, ends, kpad)
    dq_s[...] = dq_ref[...]
    dk_s[...] = dk_ref[...]
    dv_s[...] = dv_ref[...]
    for copy in copies:
        copy.wait()
    back_tiles(
        FIRST_TILES, cpad // KB, ends, side, own, q_s, do_s, lse_s, d_s, k_ref, v_ref, kt_ref,
        segk_s, qm_s, dm_s, dq_s, dk_s, dv_s,
    )

    wq, wk, wv = w3_ref[0], w3_ref[1], w3_ref[2]
    dqt = (dq_s[...] * scale).astype(BF16)
    dqt_ref[...] = dqt
    step = rows // 8

    def h_body(i, carry):
        at = pl.ds(pl.multiple_of(i * step, GRAIN), step)
        gh_s[at, :] = mm(dk_s[at, 0:mine].astype(BF16), wk, COLS_COLS) + mm(
            dv_s[at, 0:mine].astype(BF16), wv, COLS_COLS
        )
        return carry

    lax.fori_loop(0, 8, h_body, 0)
    dkt_ref[...] = dk_s[...].astype(BF16).T[0:mine]
    dvt_ref[...] = dv_s[...].astype(BF16).T[0:mine]
    grad_q = mm(dqt.T, wq, COLS_COLS)
    for i in range(own // STRIP):
        at = pl.ds(strip_start(0, i, side), STRIP)
        gh_s[at, :] += grad_q[i * STRIP : (i + 1) * STRIP]
    hkeep_ref[...] = gh_s[pl.ds(pl.multiple_of(core * own, GRAIN), own), :].astype(BF16)
    hsend_ref[...] = gh_s[pl.ds(pl.multiple_of((1 - core) * own, GRAIN), own), :].astype(BF16)


def weight_kernel(
    dqt_ref, dkt_ref, dvt_ref, ga_ref, hidc_ref, hoc_ref, hid_any, groute_ref, gain2_ref, pay_ref, hid_ref, sem
):
    mine = dqt_ref.shape[0]
    width = ga_ref.shape[1]
    copy = pltpu.make_async_copy(hid_any, hid_ref, sem)
    copy.start()
    pay_ref[0:mine, :] = mm(dqt_ref[...], hidc_ref[...]).astype(BF16)
    pay_ref[3 * mine : 4 * mine, :] = mm(hoc_ref[...].T[0:mine], ga_ref[...]).astype(BF16)
    copy.wait()
    pay_ref[mine : 2 * mine, :] = mm(dkt_ref[...], hid_ref[...]).astype(BF16)
    pay_ref[2 * mine : 3 * mine, :] = mm(dvt_ref[...], hid_ref[...]).astype(BF16)
    pay_ref[4 * mine : 4 * mine + 8, :] = groute_ref[...].T[0:8].astype(BF16)
    pay_ref[4 * mine + 8 : 4 * mine + 16, :] = gain2_ref[...].astype(BF16)
    pay_ref[4 * mine + 16 :, :] = jnp.zeros((pay_ref.shape[0] - 4 * mine - 16, width), BF16)


def run_weights(pay_rows, dqt, dkt, dvt, ga, hidc, hoc, hid, groute, gain2, after):
    return call(
        weight_kernel, sds((pay_rows, ga.shape[1]), BF16),
        [pltpu.VMEM(hid.shape, BF16), pltpu.SemaphoreType.DMA], "weights", 4, limit=16,
        in_specs=[VMEM_SPEC] * 6 + [FAR_ANY] + [VMEM_SPEC] * 2, out_specs=PLAIN_SPEC, after=after,
    )(dqt, dkt, dvt, ga, hidc, hoc, hid, groute, gain2)


def run_back_first(lengths, where, ga, gao, ho, q, lse, k, kt, v, hid, wproj, after):
    half, width = ga.shape
    own = 2 * half
    kpad, lanes = k.shape
    mine = kt.shape[0]
    heads = mine // 64
    cpad = up(own, KB)
    outs = (
        sds((cpad, width), BF16),
        sds((cpad, width), BF16),
        sds((cpad, lanes), BF16),
        sds((cpad, lanes), BF16),
        sds((cpad, lanes), BF16),
        sds((8, cpad), F32),
        sds((8, cpad), F32),
        sds((mine, cpad), F32),
        sds((kpad, lanes), F32),
        sds((kpad, lanes), F32),
    )
    scratch = [
        pltpu.VMEM((kpad, LANES), jnp.int32),
        pltpu.VMEM((heads, KB, LANES), BF16),
        pltpu.VMEM((heads, KB, LANES), BF16),
        pltpu.VMEM((cpad, LANES), F32),
        pltpu.VMEM((kpad, lanes), BF16),
        pltpu.VMEM((kpad, lanes), BF16),
        pltpu.VMEM((mine, kpad), BF16),
        pltpu.VMEM((own // STRIP, STRIP, lanes), BF16),
        pltpu.VMEM((own // STRIP, STRIP, LANES), F32),
        pltpu.VMEM((own // STRIP, STRIP, lanes), BF16),
        pltpu.VMEM((own // STRIP, STRIP, width), BF16),
        pltpu.SemaphoreType.DMA((7,)),
    ]
    return call(
        back_first_kernel, outs, scratch, "back_first", 14,
        in_specs=[SMEM_SPEC, SMEM_SPEC, PLAIN_SPEC, PLAIN_SPEC] + [FAR_ANY] * 7 + [PLAIN_SPEC],
        out_specs=(VMEM_SPEC,) * 10, limit=24, after=after,
    )(lengths, where, ga, gao, in_strips(ho), in_strips(q), in_strips(lse), k, kt, v, in_strips(hid), wproj)


def run_back_second(own, lengths, where, k, kt, v, q, do, lse, dots, dq, dk, dv, w3, after):
    kpad, lanes = k.shape
    mine = kt.shape[0]
    heads = mine // 64
    cpad = q.shape[0]
    width = w3.shape[1]
    outs = (
        sds((own, width), BF16),
        sds((own, width), BF16),
        sds((mine, cpad), BF16),
        sds((mine, kpad), BF16),
        sds((mine, kpad), BF16),
    )
    scratch = [
        pltpu.VMEM((kpad, LANES), jnp.int32),
        pltpu.VMEM((heads, KB, LANES), BF16),
        pltpu.VMEM((heads, KB, LANES), BF16),
        pltpu.VMEM((mine, cpad), F32),
        pltpu.VMEM((kpad, lanes), F32),
        pltpu.VMEM((kpad, lanes), F32),
        pltpu.VMEM((2 * own, width), F32),
        pltpu.VMEM((kpad, lanes), BF16),
        pltpu.VMEM((kpad, lanes), BF16),
        pltpu.VMEM((mine, kpad), BF16),
        pltpu.SemaphoreType.DMA((3,)),
    ]
    return call(
        back_second_kernel, outs, scratch, "back_second", 14,
        in_specs=[SMEM_SPEC, SMEM_SPEC] + [FAR_ANY] * 3 + [VMEM_SPEC] * 7 + [PLAIN_SPEC],
        out_specs=(FAR_SPEC, PLAIN_SPEC) + (VMEM_SPEC,) * 3, limit=24, after=after,
    )(lengths, where, k, kt, v, q, do, lse, dots, dq, dk, dv, w3)


def token_kernel(where_ref, mine_ref, got_ref, gmid_ref, tok_ref, gain1_ref, out_ref, tok_s, sem):
    half = gmid_ref.shape[0]
    copy = strip_copy(tok_ref, where_ref[0] * (half // STRIP), where_ref[1], tok_s, sem)
    copy.start()
    grad_h1 = mine_ref[...].astype(F32) + got_ref[...].astype(F32)
    copy.wait()
    normed1, scale1 = normalize_rows(tok_s[...].reshape(half, -1).astype(F32))
    out_ref[...] = (gmid_ref[...] + normal_back(grad_h1, normed1, scale1, gain1_ref[...])).astype(BF16)


def run_tokens(where, mine, got, gmid, tokens, gain1, after):
    return call(
        token_kernel, sds(gmid.shape, BF16),
        [pltpu.VMEM((gmid.shape[0] // STRIP, STRIP, gmid.shape[1]), BF16), pltpu.SemaphoreType.DMA], "token_grad", 3, limit=12,
        in_specs=[SMEM_SPEC, FAR_SPEC, PLAIN_SPEC, FAR_SPEC, FAR_ANY, VMEM_SPEC], out_specs=PLAIN_SPEC, after=after,
    )(where, mine, got, gmid, in_strips(tokens), gain1)


def split_kernel(where_ref, a_ref, b_ref, keep_ref, send_ref):
    half = keep_ref.shape[0]
    total = (a_ref[...].astype(F32) + b_ref[...].astype(F32)).astype(BF16)
    side = where_ref[1]
    first, second = strips(total, 0, half), strips(total, 1, half)
    keep_ref[...] = jnp.where(side == 0, first, second)
    send_ref[...] = jnp.where(side == 0, second, first)


def run_split(where, a, b, after):
    own, width = a.shape
    outs = (sds((own // 2, width), BF16),) * 2
    return call(
        split_kernel, outs, [], "split", 2, limit=12, in_specs=[SMEM_SPEC, FAR_SPEC, PLAIN_SPEC],
        out_specs=(FAR_SPEC, PLAIN_SPEC), after=after,
    )(where, a, b)


def weave_kernel(where_ref, mine_ref, other_ref, out_ref):
    side = where_ref[1]
    for i in range(mine_ref.shape[0] // STRIP):
        rows = slice(i * STRIP, (i + 1) * STRIP)
        out_ref[pl.ds(strip_start(0, i, side), STRIP), :] = mine_ref[rows, :]
        out_ref[pl.ds(strip_start(0, i, 1 - side), STRIP), :] = other_ref[rows, :]


def run_weave(where, mine, other, after):
    half, width = mine.shape
    return call(
        weave_kernel, sds((2 * half, width), BF16), [], "weave", 2, limit=8,
        in_specs=[SMEM_SPEC] + [PLAIN_SPEC] * 2, out_specs=PLAIN_SPEC, after=after,
    )(where, mine, other)


def summed_end_kernel(total_ref, gin_ref, gout_ref):
    gin_ref[0] = total_ref[0, 0].astype(F32)
    gout_ref[0] = total_ref[0, 1].astype(F32)


def run_summed_end(total, shape_in, shape_out, after):
    size, unused, width, hidden = total.shape
    block = pl.BlockSpec((1, width, hidden), lambda e: (e, 0, 0))
    return call(
        summed_end_kernel,
        (sds(shape_in, F32), sds(shape_out, F32)),
        [],
        "summed_end",
        4, limit=12,
        grid=(size,),
        in_specs=[pl.BlockSpec((1, 2, width, hidden), lambda e: (e, 0, 0, 0))],
        out_specs=(block, block),
        after=after,
    )(total)


def expert_end_kernel(where_ref, mine_ref, other_ref, *refs):
    gin_ref, gout_ref = refs[-2:]
    e = pl.program_id(0)
    mine = mine_ref[e].astype(F32)
    other = other_ref[e].astype(F32)
    first = where_ref[2] == 0
    gin_ref[0] = jnp.where(first, mine, other)
    gout_ref[0] = jnp.where(first, other, mine)


def run_expert_end(at, where, mine, other, shape_in, shape_out, before):
    size, width, hidden = mine.shape
    block = pl.BlockSpec((1, width, hidden), lambda e: (e + at, 0, 0))
    return call(
        expert_end_kernel,
        (sds(shape_in, F32), sds(shape_out, F32)),
        [],
        "expert_end",
        3, limit=12,
        grid=(size,),
        in_specs=[SMEM_SPEC, PLAIN_SPEC, PLAIN_SPEC] + [FAR_ANY] * 2,
        out_specs=(block, block),
        input_output_aliases={3: 0, 4: 1},
    )(where, mine, other, *before)


def total_kernel(parts_ref, out_ref):
    pieces = parts_ref.shape[0]
    total = parts_ref[0].astype(F32)
    for i in range(1, pieces):
        total = total + parts_ref[i].astype(F32)
    total = total.astype(BF16)
    for i in range(pieces):
        out_ref[i] = total


def run_total(parts, after):
    return call(
        total_kernel, sds(parts.shape, BF16), [], "total", 2, limit=8, in_specs=[PLAIN_SPEC], out_specs=PLAIN_SPEC, after=after
    )(parts)


def attn_end_kernel(where_ref, mine_ref, other_ref, wqkv_ref, gain1_ref, gqkv_ref, gproj_ref, g1_ref, g2_ref, groute_ref):
    width = wqkv_ref.shape[1]
    share = width // 2
    first = where_ref[0] == 0
    mine = mine_ref[...].astype(F32)
    other = other_ref[...].astype(F32)
    low = jnp.where(first, mine, other)
    high = jnp.where(first, other, mine)
    product = jnp.zeros((width, width), F32)
    for i in range(3):
        rows = slice(i * share, (i + 1) * share)
        part = jnp.concatenate([low[rows], high[rows]], 0).T
        gqkv_ref[i] = part
        product = product + part * wqkv_ref[i].astype(F32)
    gproj_ref[...] = jnp.concatenate([low[3 * share : 4 * share], high[3 * share : 4 * share]], 0)
    g1_ref[...] = jnp.sum(product.T, 0, keepdims=True) / gain1_ref[...]
    small = low[4 * share : 4 * share + 16] + high[4 * share : 4 * share + 16]
    groute_ref[...] = small[0:8]
    g2_ref[...] = small[8:9]


def run_attn_end(where, mine, other, wqkv, gain1, after):
    width = wqkv.shape[1]
    outs = (
        sds((3, width, width), F32),
        sds((width, width), F32),
        sds((1, width), F32),
        sds((1, width), F32),
        sds((8, width), F32),
    )
    return call(
        attn_end_kernel, outs, [], "attn_end", 4, limit=16, in_specs=[SMEM_SPEC, PLAIN_SPEC, PLAIN_SPEC, VMEM_SPEC, VMEM_SPEC],
        out_specs=(FAR_SPEC,) * 5, after=after,
    )(where, mine, other, wqkv, gain1)


def swap(value, axis, mask):
    size = lax.axis_size(axis)
    return lax.ppermute(value, axis, [(i, i ^ mask) for i in range(size)])


def add_kernel(a_ref, b_ref, out_ref):
    out_ref[...] = (a_ref[...].astype(F32) + b_ref[...].astype(F32)).astype(BF16)


def added(a, b, after):
    return call(
        add_kernel, sds(a.shape, BF16), [], "add", 2, limit=8, in_specs=[PLAIN_SPEC] * 2, out_specs=PLAIN_SPEC, after=after
    )(a, b)


def choose_kernel(where_ref, inner_ref, outer_ref, out_ref):
    @pl.when(where_ref[3] == 0)
    def _():
        out_ref[...] = inner_ref[...]

    @pl.when(where_ref[3] != 0)
    def _():
        out_ref[...] = outer_ref[...]


def chosen(where, inner, outer, after):
    return call(
        choose_kernel, sds(inner.shape, BF16), [], "choose", 2, limit=8,
        in_specs=[SMEM_SPEC, PLAIN_SPEC, PLAIN_SPEC], out_specs=PLAIN_SPEC, after=after,
    )(where, inner, outer)


def wide_step(value, step):
    inward = [(w, w + 2) for w in (0, 1)] + [(w, w - 2) for w in (6, 7)]
    if step == 0:
        return lax.ppermute(value, "wide", inward)
    if step == 1:
        return lax.ppermute(value, "wide", [(2, 4), (3, 5), (4, 2), (5, 3)])
    return lax.ppermute(value, "wide", [(b, a) for a, b in inward])


def on_device(
    tokens, w_qkv, w_proj, norm1_gain, norm2_gain, w_route, w_in, w_out, cotangent, routes, kept_mask, lengths
):
    rows, width = tokens.shape
    own, half = rows // 2, rows // 4
    experts = w_in.shape[0]
    core, side = lax.axis_index("lo"), lax.axis_index("hi")
    wide_size, w = lax.axis_size("wide"), lax.axis_index("wide")
    z = w // 2
    outer = ((z == 0) | (z == wide_size // 2 - 1)).astype(jnp.int32)
    where = jnp.stack([core, side, w % 2, outer]).astype(jnp.int32)

    wqkv = w_qkv.transpose(1, 0, 2)
    w3 = lax.dynamic_slice_in_dim(wqkv, core * (width // 2), width // 2, 2)
    wr = jnp.pad(w_route, ((0, 0), (0, LANES - experts)))
    gain1 = norm1_gain.reshape(1, width)
    gain2 = norm2_gain.reshape(1, width)
    code = jnp.where(kept_mask == 1, routes[:, 0], experts).reshape(2, 1, own)
    code = jnp.pad(code, ((0, 0), (0, 0), (0, up(own, LANES) - own)), constant_values=experts)

    hid, k, kt, v, q, ho, lse, keep, send = run_front(lengths, where, tokens, w3, w_proj, gain1)
    got = swap(send, "lo", 1)
    plan, pos = run_plan(where, code, (keep, ANY_SPEC))
    mid, own_x, own_send = run_mid(where, keep, got, tokens, cotangent, gain2, wr, code, pos)
    oth_x = swap(own_send, "lo", 1)

    yown, yoth, groute, grads_a, *pairs = run_experts(plan, where, own_x, oth_x, w_in, w_out, wr)
    got = swap(yoth, "lo", 1)
    total_a = lax.psum(grads_a, "wide")
    pairs = [(pairs[2 * i], pairs[2 * i + 1]) for i in range(len(pairs) // 2)]
    recvs = [swap(give, "wide", 1) for unused, give in pairs]

    unpick = run_unpick(pos, own, own_x.shape[0], (yoth, ANY_SPEC))
    keep, send = run_unsort(where, yown, got, unpick)
    gh2 = swap(send, "hi", 1)
    ex = run_unsort_out(yown, got, pos, own, (send, ANY_SPEC))
    sums, moved = [], []
    for mine, unused in pairs:
        sums.append(mine)
    line = wide_size == 8

    def add_step(i, recv, after):
        sums[i] = added(sums[i], recv, after)
        return sums[i], ANY_SPEC

    def first_step(i, after):
        after = add_step(i, recvs[i], after)
        if line:
            moved.append(wide_step(sums[i], 0))
        else:
            for j in range(1, wide_size.bit_length() - 1):
                after = add_step(i, swap(sums[i], "wide", 1 << j), after)
        return after

    def line_step(i, step, after):
        if line:
            after = add_step(i, moved[i], after)
            moved[i] = wide_step(sums[i], step)
        return after

    def last_step(i, after):
        if line:
            sums[i] = chosen(where, sums[i], moved[i], after)
            after = sums[i], ANY_SPEC
        others.append(swap(sums[i], "wide", 1))
        return after

    others = []
    gmid, ga, gain2_part, ex = run_mid_back(where, keep, gh2, mid, cotangent, gain2, ex, (ex, VMEM_SPEC))
    gao = swap(ga, "lo", 1)
    ex_got = swap(ex, "hi", 1)
    last = first_step(0, (ex, FAR_ANY))

    ga_c, hid_c, ho_c, *state = run_back_first(lengths, where, ga, gao, ho, q, lse, k, kt, v, hid, w_proj, last)
    last = ga_c, VMEM_SPEC
    last = first_step(1, last)
    last = line_step(0, 1, last)
    hkeep, hsend, dqt, dkt, dvt = run_back_second(own, lengths, where, k, kt, v, *state, w3, last)
    hgot = swap(hsend, "lo", 1)
    pay_rows = up(2 * width + 16, 8 * lax.axis_size(("wide", "hi")))
    pay = run_weights(pay_rows, dqt, dkt, dvt, ga_c, hid_c, ho_c, hid, groute, gain2_part, (hsend, ANY_SPEC))
    share = pay_rows // lax.axis_size(("wide", "hi"))
    pay_got = lax.all_to_all(pay.reshape(-1, share, width), ("wide", "hi"), 0, 0)
    last = first_step(2, (pay, ANY_SPEC))
    last = line_step(0, 2, last)
    last = line_step(1, 1, last)
    hk, hs = run_split(where, hkeep, hgot, last)
    hs_got = swap(hs, "hi", 1)
    out_own = run_out(mid, ex, ex_got, (hs, ANY_SPEC))
    out_oth = swap(out_own, "lo", 1)
    last = line_step(2, 1, (out_own, ANY_SPEC))
    last = line_step(1, 2, last)
    last = last_step(0, last)
    token_rows = run_tokens(where, hk, hs_got, gmid, tokens, gain1, last)
    token_got = swap(token_rows, "hi", 1)
    last = line_step(2, 2, (token_rows, ANY_SPEC))
    pay_got = run_total(pay_got, last)
    last = pay_got, ANY_SPEC
    pay_got = lax.all_to_all(pay_got, ("wide", "hi"), 0, 0).reshape(pay.shape)
    last = last_step(1, last)
    layer_out = run_join(where, out_own, out_oth, last)
    token_own = run_weave(where, token_rows, token_got, (layer_out, FAR_ANY))
    token_oth = swap(token_own, "lo", 1)
    last = last_step(2, (token_own, ANY_SPEC))
    grad_tokens = run_join(where, token_own, token_oth, last)
    before = run_summed_end(total_a, w_in.shape, w_out.shape, (grad_tokens, FAR_ANY))
    at = PARTS[0]
    for i, size in enumerate(PARTS[1:]):
        if i == len(PARTS) - 2:
            pay_oth = swap(pay_got, "lo", 1)
            grad_qkv, grad_proj, grad_norm1, grad_norm2, route_t = run_attn_end(
                where, pay_got, pay_oth, wqkv, gain1, (before[0], FAR_ANY)
            )
        before = run_expert_end(at, where, sums[i], others[i], w_in.shape, w_out.shape, before)
        at += size
    grad_in, grad_out = before

    return (
        layer_out,
        grad_tokens,
        grad_qkv.transpose(1, 0, 2),
        grad_proj,
        grad_norm1.reshape(width),
        grad_norm2.reshape(width),
        route_t.T,
        grad_in,
        grad_out,
    )


def solution(mesh):
    axes = ("wide", ("hi", "lo"))
    split = Mesh(mesh.devices.reshape(mesh.shape["wide"], -1, 2), ("wide", "hi", "lo"))
    wide, narrow = axes
    in_specs = (
        P(wide, None),
        P(),
        P(),
        P(),
        P(),
        P(),
        P(None, None, narrow),
        P(None, narrow, None),
        P(wide, None),
        P(wide, None),
        P(wide),
        P(wide, None),
    )
    out_specs = (
        P(wide, None),
        P(wide, None),
        P(),
        P(),
        P(),
        P(),
        P(),
        P(None, None, narrow),
        P(None, narrow, None),
    )
    return jax.shard_map(on_device, mesh=split, in_specs=in_specs, out_specs=out_specs, check_vma=False)
```

```python
import math

import jax
import jax.numpy as jnp
from jax import lax
from jax.experimental import pallas as pl
from jax.experimental.pallas import tpu as pltpu
from jax.sharding import Mesh, PartitionSpec as P

HEADS = 6
CAP = 408
EPS = 1e-06
NEG = -1e30
F32 = jnp.float32
BF16 = jnp.bfloat16
LANES = 128
KB = 256
GRAIN = 16
STRIP = 32
FLOPS = 10**10
PARTS = (2, 2, 2, 2)
FIRST_TILES = 2
GELU_A = math.sqrt(2.0 / math.pi)
GELU_B = 0.044715

ROWS_COLS = (((1,), (0,)), ((), ()))
COLS_COLS = (((1,), (1,)), ((), ()))
ROWS_ROWS = (((0,), (0,)), ((), ()))


def up(value, grain):
    return -(-value // grain) * grain


def mm(a, b, dims=ROWS_COLS):
    return lax.dot_general(a, b, dims, preferred_element_type=F32)


def normalize_rows(values):
    centre = values - jnp.mean(values, -1, keepdims=True)
    row_scale = lax.rsqrt(jnp.mean(centre * centre, -1, keepdims=True) + EPS)
    return centre * row_scale, row_scale


def normal_back(grad_h, normed, row_scale, gain_row):
    g = grad_h * gain_row
    return row_scale * (
        g - jnp.mean(g, -1, keepdims=True) - normed * jnp.mean(g * normed, -1, keepdims=True)
    )


def lane_head(h):
    return slice((h // 2) * LANES, (h // 2 + 1) * LANES)


def seq_ends(len_ref, count):
    ends = []
    total = jnp.int32(0)
    for j in range(count):
        total = total + len_ref[0, j]
        ends.append(total)
    return ends


def seq_bounds(ends, first_row, last_row):
    low = jnp.int32(0)
    high = ends[-1]
    for end in ends:
        low = jnp.where(end <= first_row, end, low)
    for end in reversed(ends):
        high = jnp.where(end > last_row, end, high)
    return low, high


def segment_of(index, ends):
    seg = jnp.zeros(index.shape, jnp.int32)
    for end in ends:
        seg = seg + (index >= end).astype(jnp.int32)
    return seg


def key_segments(segk_ref, ends, kpad):
    def body(i, carry):
        start = pl.multiple_of(i * LANES, LANES)
        index = lax.broadcasted_iota(jnp.int32, (LANES, LANES), 0) + start
        segk_ref[pl.ds(start, LANES), :] = segment_of(index, ends)
        return carry

    lax.fori_loop(0, kpad // LANES, body, 0)


def bias_block(segk_ref, kstart, segq):
    segk = segk_ref[pl.ds(kstart, KB), :]
    return jnp.where(jnp.concatenate([segk, segk], 1) == segq, 0.0, NEG)


def head_mask(rows, odd):
    lane = lax.broadcasted_iota(jnp.int32, (rows, LANES), 1)
    return ((lane >= 64) if odd else (lane < 64)).astype(BF16)


def plan_of(code_row, experts):
    n = code_row.shape[1]
    sub = lax.broadcasted_iota(jnp.int32, (experts, n), 0)
    lane = lax.broadcasted_iota(jnp.int32, (experts, n), 1)
    member = (code_row == sub).astype(F32)
    rank = member
    shift = 1
    while shift < n:
        rank = rank + jnp.where(lane >= shift, pltpu.roll(rank, shift, 1), 0.0)
        shift *= 2
    counts = jnp.broadcast_to(rank[:, n - 1 : n], (experts, LANES))
    sizes = jnp.floor((counts + (GRAIN - 1)) * (1.0 / GRAIN)) * GRAIN
    row = lax.broadcasted_iota(jnp.int32, (experts, LANES), 0)
    total = sizes
    shift = 1
    while shift < experts:
        total = total + jnp.where(row >= shift, pltpu.roll(total, shift, 0), 0.0)
        shift *= 2
    offsets = total - sizes
    pos = jnp.sum(member * (rank + offsets[:, 0:1]), 0, keepdims=True) - 1.0
    return pos, offsets, sizes


def key_steps(low, high):
    start = low // LANES * LANES
    return start, (high - start + KB - 1) // KB


def plan_kernel(where_ref, code_ref, plan_ref, pos_ref):
    experts = 8
    core = where_ref[0]
    pos, offsets, sizes = plan_of(code_ref[core], experts)
    unused, other_offsets, other_sizes = plan_of(code_ref[1 - core], experts)
    plan_ref[0:8, :] = offsets.astype(jnp.int32)
    plan_ref[8:16, :] = sizes.astype(jnp.int32)
    plan_ref[16:24, :] = other_offsets.astype(jnp.int32)
    plan_ref[24:32, :] = other_sizes.astype(jnp.int32)
    pos_ref[...] = jnp.broadcast_to(pos, pos_ref.shape)


def unpick_part(columns, part, half, cpad):
    lane = lax.broadcasted_iota(jnp.int32, (half, LANES), 1).astype(F32)
    column = strips(columns, part, half)
    return jnp.concatenate(
        [jnp.where(column == lane + float(j * LANES), 1.0, 0.0).astype(BF16) for j in range(cpad // LANES)], 1
    )


def unpick_kernel(pos_ref, unpick_ref):
    half, cpad = unpick_ref.shape[1:]
    columns = jnp.broadcast_to(pos_ref[0:1, :], (LANES, pos_ref.shape[1])).T
    for part in range(2):
        unpick_ref[part] = unpick_part(columns, part, half, cpad)


def run_unpick(pos, own, count, after):
    return call(
        unpick_kernel, sds((2, own // 2, up(count, LANES)), BF16), [], "unpick", 2, limit=12,
        in_specs=[VMEM_SPEC], after=after,
    )(pos)


def strips(value, part, half):
    return jnp.concatenate(
        [value[(2 * i + part) * STRIP : (2 * i + part + 1) * STRIP] for i in range(half // STRIP)], 0
    )


def strip_start(base, i, side):
    return pl.multiple_of(base + 2 * STRIP * i + STRIP * side, STRIP)


def in_strips(array):
    return array.reshape(-1, 2, STRIP, array.shape[-1])


def strip_copy(ref, first, side, dst, sem):
    return pltpu.make_async_copy(ref.at[pl.ds(first, dst.shape[0]), side], dst, sem)


def load_strips(ref, base, side, half):
    return jnp.concatenate([ref[pl.ds(strip_start(base, i, side), STRIP), :] for i in range(half // STRIP)], 0)


def front_kernel(
    len_ref, where_ref, tok_ref, w3_ref, wproj_ref, gain1_ref,
    hid_out, k_out, kt_out, v_out, q_out, ho_out, lse_out, keep_ref, send_ref,
    hid_ref, k_ref, kt_ref, v_ref, q_ref, ho_ref, lse_ref,
    vt_s, segk_s, qm_s, acc_s, m_s, l_s, s_s, st_s, sems,
):
    rows, width = tok_ref.shape
    own = rows // 2
    copies = [
        pltpu.make_async_copy(src, dst, sems.at[i])
        for i, (src, dst) in enumerate(
            (
                (hid_ref, hid_out), (k_ref, k_out), (kt_ref, kt_out), (v_ref, v_out), (q_ref, q_out),
                (ho_ref, ho_out), (lse_ref, lse_out),
            )
        )
    ]
    kpad = hid_ref.shape[0]
    qpad = q_ref.shape[0]
    mine = w3_ref.shape[2]
    heads = mine // 64
    core = where_ref[0]
    ends = seq_ends(len_ref, len_ref.shape[1])
    scale = 1.0 / math.sqrt(width // HEADS)
    key_segments(segk_s, ends, kpad)
    gain1 = gain1_ref[...]
    wq, wk, wv = w3_ref[0], w3_ref[1], w3_ref[2]
    step = rows // 4

    def norm_body(i, carry):
        at = pl.ds(pl.multiple_of(i * step, GRAIN), step)
        normed, unused = normalize_rows(tok_ref[at, :].astype(F32))
        hid = (normed * gain1).astype(BF16)
        hid_ref[at, :] = hid
        k_ref[at, 0:mine] = mm(hid, wk).astype(BF16)
        v_ref[at, 0:mine] = mm(hid, wv).astype(BF16)
        q_ref[at, 0:mine] = (mm(hid, wq).astype(BF16).astype(F32) * scale).astype(BF16)
        return carry

    lax.fori_loop(0, 4, norm_body, 0)
    hid_ref[rows:kpad, :] = jnp.zeros((kpad - rows, width), BF16)
    for ref in (k_ref, v_ref, q_ref):
        size = ref.shape[0]
        ref[rows:size, 0:mine] = jnp.zeros((size - rows, mine), BF16)
        ref[:, mine:] = jnp.zeros((size, ref.shape[1] - mine), BF16)
    wkt = wk.T
    wvt = wv.T

    def key_body(i, carry):
        at = pl.ds(pl.multiple_of(i * 2 * KB, 2 * KB), 2 * KB)
        hid = hid_ref[at, :]
        kt_ref[:, at] = mm(wkt, hid, COLS_COLS).astype(BF16)
        vt_s[:, at] = mm(wvt, hid, COLS_COLS).astype(BF16)
        return carry

    lax.fori_loop(0, kpad // (2 * KB), key_body, 0)
    for copy in copies[:5]:
        copy.start()
    st_s[...] = jnp.zeros(st_s.shape, F32)

    def q_step(qb, carry):
        first = pl.multiple_of(qb * KB, KB)
        last = jnp.minimum(first + KB, rows) - 1
        for h in range(heads):
            qm_s[h] = q_ref[pl.ds(first, KB), lane_head(h)] * head_mask(KB, h % 2)
        for h in range(heads):
            m_s[h : h + 1] = jnp.full((1, KB), NEG, F32)
            l_s[h : h + 1] = jnp.zeros((1, KB), F32)
        acc_s[...] = jnp.zeros(acc_s.shape, F32)
        low, high = seq_bounds(ends, first, last)
        start, steps = key_steps(low, high)
        segq = segment_of(lax.broadcasted_iota(jnp.int32, (8, KB), 1) + first, ends)[0:1]

        def scores(at):
            return [mm(k_ref[pl.ds(at, KB), lane_head(h)], qm_s[h], COLS_COLS) for h in range(heads)]

        for h, s in enumerate(scores(pl.multiple_of(start, LANES))):
            s_s[h] = s

        def k_step(kb, carry):
            at = pl.multiple_of(start + kb * KB, LANES)
            later = pl.multiple_of(start + jnp.minimum(kb + 1, steps - 1) * KB, LANES)
            bias = bias_block(segk_s, at, segq)
            now = [s_s[h] + bias for h in range(heads)]
            nexts = scores(later)
            m_old = [m_s[h : h + 1] for h in range(heads)]
            m_new = [jnp.maximum(m, jnp.max(s, 0, keepdims=True)) for m, s in zip(m_old, now)]
            p = [jnp.exp(s - m) for s, m in zip(now, m_new)]
            alpha = [jnp.exp(a - b) for a, b in zip(m_old, m_new)]
            for h in range(heads):
                m_s[h : h + 1] = m_new[h]
                l_s[h : h + 1] = l_s[h : h + 1] * alpha[h] + jnp.sum(p[h], 0, keepdims=True)
            out = [mm(vt_s[h * 64 : (h + 1) * 64, pl.ds(at, KB)], p[h].astype(BF16)) for h in range(heads)]
            for h in range(heads):
                acc_s[h * 64 : (h + 1) * 64] = acc_s[h * 64 : (h + 1) * 64] * alpha[h] + out[h]
                s_s[h] = nexts[h]
            return carry

        lax.fori_loop(0, steps, k_step, 0)
        parts = []
        for h in range(heads):
            total = l_s[h : h + 1]
            st_s[h : h + 1] = m_s[h : h + 1] + jnp.log(total)
            parts.append(acc_s[h * 64 : (h + 1) * 64] * (1.0 / total))
        lse_ref[pl.ds(first, KB), :] = st_s[...].T
        parts.append(jnp.zeros((ho_ref.shape[1] - mine, KB), F32))
        ho_ref[pl.ds(first, KB), :] = jnp.concatenate(parts, 0).T.astype(BF16)
        return carry

    lax.fori_loop(0, qpad // KB, q_step, 0)
    for copy in copies[5:]:
        copy.start()
    wproj = wproj_ref[pl.ds(pl.multiple_of(core * mine, GRAIN), mine), :]
    keep_ref[...] = mm(ho_ref[pl.ds(pl.multiple_of(core * own, GRAIN), own), 0:mine], wproj).astype(BF16)
    send_ref[...] = mm(ho_ref[pl.ds(pl.multiple_of((1 - core) * own, GRAIN), own), 0:mine], wproj).astype(BF16)
    for copy in copies:
        copy.wait()


def mid_kernel(
    where_ref, keep_ref, got_ref, tok_ref, cot_ref, gain2_ref, wr_ref, code_ref, pos_ref,
    mid_ref, sorted_ref, send_ref, x_s, tok_s, cot_s, mid_s, sems,
):
    own, width = keep_ref.shape
    npad = x_s.shape[0]
    core = where_ref[0]
    at = pl.ds(pl.multiple_of(core * own, GRAIN), own)
    tok_copy = pltpu.make_async_copy(tok_ref.at[at, :], tok_s, sems.at[0])
    cot_copy = pltpu.make_async_copy(cot_ref.at[at, :], cot_s, sems.at[1])
    tok_copy.start()
    cot_copy.start()
    tok_copy.wait()
    mid = tok_s[...].astype(F32) + (keep_ref[...].astype(F32) + got_ref[...].astype(F32))
    mid_s[...] = mid
    mid_copy = pltpu.make_async_copy(mid_s, mid_ref, sems.at[6])
    mid_copy.start()
    normed2, unused = normalize_rows(mid)
    hidden2 = (normed2 * gain2_ref[...]).astype(BF16)
    lane = lax.broadcasted_iota(jnp.int32, (own, LANES), 1)
    gates = router_gates(hidden2, wr_ref[...], lane, 8)
    code_col = jnp.broadcast_to(code_ref[core].astype(F32), (LANES, npad)).T[0:own]
    gate = jnp.sum(jnp.where(code_col == lane.astype(F32), gates, 0.0), -1, keepdims=True)
    x_s[0:own, 0:width] = hidden2
    cot_copy.wait()
    x_s[0:own, width:] = (gate * cot_s[...].astype(F32)).astype(BF16)
    x_s[own:npad, :] = jnp.zeros((npad - own, 2 * width), BF16)
    piece = sorted_ref.shape[0] // 4
    copies = []
    for i in range(4):
        rows = slice(i * piece, (i + 1) * piece)
        sub = lax.broadcasted_iota(jnp.int32, (piece, npad), 0) + i * piece
        pick = jnp.where(sub.astype(F32) == pos_ref[0:1, :], 1.0, 0.0).astype(BF16)
        sorted_ref[rows, :] = mm(pick, x_s[...]).astype(BF16)
        copies.append(pltpu.make_async_copy(sorted_ref.at[rows, :], send_ref.at[rows, :], sems.at[2 + i]))
        copies[-1].start()
    for copy in copies + [mid_copy]:
        copy.wait()


def router_gates(hidden2, wr, lane, experts):
    logits = jnp.where(lane < experts, mm(hidden2, wr), NEG)
    top = jnp.max(logits, -1, keepdims=True)
    e = jnp.exp(logits - top)
    return e / jnp.sum(e, -1, keepdims=True)


def call(kernel, outs, scratch, name, micros, in_specs, limit=24, after=None, **more):
    def out_of(shape, spec):
        if spec is VMEM_SPEC:
            return pltpu.VMEM(shape.shape, shape.dtype)
        return pltpu.HBM(shape.shape, shape.dtype) if is_far(spec) else shape

    out_specs = more.get("out_specs")
    if out_specs is None:
        out_specs = jax.tree.map(lambda o: VMEM_SPEC, outs)
    if isinstance(outs, tuple):
        outs = tuple(out_of(o, spec) for o, spec in zip(outs, out_specs))
    else:
        outs = out_of(outs, out_specs)
    more["out_specs"] = out_specs
    aliases = more.pop("input_output_aliases", {})
    body = kernel
    if after is not None:
        in_specs = [ANY_SPEC] + list(in_specs)
        aliases = {i + 1: o for i, o in aliases.items()}
        body = lambda after_ref, *refs: kernel(*refs)
    run = pl.pallas_call(
        body,
        out_shape=outs,
        in_specs=in_specs,
        scratch_shapes=scratch,
        name=name,
        input_output_aliases=aliases,
        compiler_params=pltpu.CompilerParams(vmem_limit_bytes=limit * 1024 * 1024),
        cost_estimate=pl.CostEstimate(flops=micros * FLOPS, bytes_accessed=10**4, transcendentals=0),
        **more,
    )

    def place(array, spec):
        if spec is VMEM_SPEC:
            return pltpu.with_memory_space_constraint(array, pltpu.VMEM)
        return pltpu.with_memory_space_constraint(array, pltpu.HBM) if is_far(spec) else array

    def run_on(*args):
        placed = [place(a, spec) for a, spec in zip(args, in_specs[len(in_specs) - len(args) :])]
        if after is not None:
            array, spec = after
            placed = [place(array, spec)] + placed
        return run(*placed)

    return run_on


def is_far(spec):
    return spec is FAR_SPEC or spec is FAR_ANY or spec.block_shape is not None


ANY_SPEC = pl.BlockSpec(memory_space=pl.ANY)
FAR_SPEC = pl.BlockSpec(memory_space=pltpu.VMEM)
FAR_ANY = pl.BlockSpec(memory_space=pl.ANY)
PLAIN_SPEC = pl.BlockSpec(memory_space=pltpu.VMEM)
SMEM_SPEC = pl.BlockSpec(memory_space=pltpu.SMEM)
VMEM_SPEC = pl.BlockSpec(memory_space=pltpu.VMEM)


def sds(shape, dtype):
    return jax.ShapeDtypeStruct(shape, dtype)


def run_plan(where, code, after=None):
    npad = code.shape[2]
    outs = (
        sds((32, LANES), jnp.int32),
        sds((8, npad), F32),
    )
    return call(plan_kernel, outs, [], "plan", 5, limit=12, in_specs=[SMEM_SPEC, VMEM_SPEC], after=after)(where, code)


def run_front(lengths, where, tokens, w3, wproj, gain1):
    rows, width = tokens.shape
    own = rows // 2
    mine = w3.shape[2]
    heads = mine // 64
    kpad = up(rows + KB, 2 * KB)
    qpad = up(rows, KB)
    lanes = up(mine, LANES)
    outs = (
        sds((kpad, width), BF16),
        sds((kpad, lanes), BF16),
        sds((mine, kpad), BF16),
        sds((kpad, lanes), BF16),
        sds((qpad, lanes), BF16),
        sds((qpad, lanes), BF16),
        sds((qpad, LANES), F32),
        sds((own, width), BF16),
        sds((own, width), BF16),
    )
    scratch = [pltpu.VMEM(o.shape, o.dtype) for o in outs[:7]] + [
        pltpu.VMEM((mine, kpad), BF16),
        pltpu.VMEM((kpad, LANES), jnp.int32),
        pltpu.VMEM((heads, KB, LANES), BF16),
        pltpu.VMEM((mine, KB), F32),
        pltpu.VMEM((8, KB), F32),
        pltpu.VMEM((8, KB), F32),
        pltpu.VMEM((heads, KB, KB), F32),
        pltpu.VMEM((LANES, KB), F32),
        pltpu.SemaphoreType.DMA((7,)),
    ]
    return call(
        front_kernel, outs, scratch, "front", 33, in_specs=[SMEM_SPEC, SMEM_SPEC, FAR_SPEC, PLAIN_SPEC, FAR_SPEC, PLAIN_SPEC],
        limit=32,
        out_specs=(FAR_ANY,) * 7 + (PLAIN_SPEC,) * 2,
    )(lengths, where, tokens, w3, wproj, gain1)


def run_mid(where, keep, got, tokens, cot, gain2, wr, code, pos):
    own, width = keep.shape
    count = up(own + 8 * (GRAIN - 1), 4 * GRAIN)
    outs = (sds((own, width), F32),) + (sds((count, 2 * width), BF16),) * 2
    scratch = [
        pltpu.VMEM((code.shape[2], 2 * width), BF16),
        pltpu.VMEM((own, width), BF16),
        pltpu.VMEM((own, width), BF16),
        pltpu.VMEM((own, width), F32),
        pltpu.SemaphoreType.DMA((7,)),
    ]
    return call(
        mid_kernel, outs, scratch, "mid", 9, limit=20,
        in_specs=[SMEM_SPEC, PLAIN_SPEC, PLAIN_SPEC, FAR_ANY, FAR_ANY] + [VMEM_SPEC] * 4,
        out_specs=(FAR_ANY, VMEM_SPEC, ANY_SPEC),
    )(where, keep, got, tokens, cot, gain2, wr, code, pos)


def expert_kernel(
    plan_ref, where_ref, own_ref, oth_ref, win_ref, wout_ref, wr_ref,
    yown_ref, yoth_ref, groute_ref, *refs,
):
    *grads, x_s, y_s = refs
    e = pl.program_id(0)
    width = win_ref.shape[1]
    most = x_s.shape[0]

    @pl.when(e == 0)
    def _():
        yown_ref[...] = jnp.zeros(yown_ref.shape, BF16)
        yoth_ref[...] = jnp.zeros(yoth_ref.shape, BF16)
        groute_ref[...] = jnp.zeros(groute_ref.shape, F32)

    own_at, own_size = plan_ref[e, 0], plan_ref[8 + e, 0]
    oth_at, oth_size = plan_ref[16 + e, 0], plan_ref[24 + e, 0]
    total = own_size + oth_size

    def move(dst, dst_at, src, src_at, size):
        def body(i, carry):
            a = pl.multiple_of(dst_at + i * GRAIN, GRAIN)
            b = pl.multiple_of(src_at + i * GRAIN, GRAIN)
            dst[pl.ds(a, GRAIN), :] = src[pl.ds(b, GRAIN), :]
            return carry

        lax.fori_loop(0, size // GRAIN, body, 0)

    move(x_s, 0, own_ref, own_at, own_size)
    move(x_s, own_size, oth_ref, oth_at, oth_size)

    def work(m):
        def zero_body(i, carry):
            x_s[pl.ds(pl.multiple_of(i * GRAIN, GRAIN), GRAIN), :] = jnp.zeros((GRAIN, 2 * width), BF16)
            return carry

        lax.fori_loop(total // GRAIN, m // GRAIN, zero_body, 0)
        h = x_s[0:m, 0:width]
        g = x_s[0:m, width:]
        w_in = win_ref[0]
        w_out = wout_ref[0]
        lane = lax.broadcasted_iota(jnp.int32, (m, LANES), 1)
        gates = router_gates(h, wr_ref[...], lane, 8)
        here = (lane == e).astype(F32)
        pre = mm(h, w_in)
        t = jnp.tanh(GELU_A * (pre + GELU_B * (pre * pre * pre)))
        act = (0.5 * pre * (1.0 + t)).astype(BF16)
        slope = 0.5 * (1.0 + t) + 0.5 * pre * (1.0 - t * t) * (GELU_A * (1.0 + 3.0 * GELU_B * (pre * pre)))
        out = mm(act, w_out)
        grad_pre = (mm(g, w_out, COLS_COLS) * slope).astype(BF16)
        dot = jnp.sum(g.astype(F32) * out, -1, keepdims=True)
        grad_logits = (dot * (here - gates)).astype(BF16)
        gate = jnp.sum(gates * here, -1, keepdims=True)
        y_s[0:m, 0:width] = (mm(grad_pre, w_in, COLS_COLS) + mm(grad_logits, wr_ref[...], COLS_COLS)).astype(BF16)
        y_s[0:m, width:] = (gate * out).astype(BF16)
        ht = h.T
        groute_ref[...] += mm(ht, grad_logits)
        grad_in = mm(ht, grad_pre).astype(BF16)
        grad_out = mm(act.T, g).astype(BF16)

        at = 0
        for i, size in enumerate(PARTS):
            here = (e >= at) & (e < at + size)
            if i == 0:
                put_both(grads[0], grad_in, grad_out, here)
            else:
                put(grads[2 * i - 1 : 2 * i + 1], grad_in, grad_out, here)
            at += size

    def put_both(ref, grad_in, grad_out, here):
        @pl.when(here)
        def _():
            ref[0, 0] = grad_in
            ref[0, 1] = grad_out

    def put(pair, grad_in, grad_out, here):
        keep_ref, send_ref = pair

        @pl.when(here & (where_ref[2] == 0))
        def _():
            keep_ref[0] = grad_in
            send_ref[0] = grad_out

        @pl.when(here & (where_ref[2] != 0))
        def _():
            keep_ref[0] = grad_out
            send_ref[0] = grad_in

    small = up(CAP * 2 // 3, GRAIN)

    @pl.when(total <= small)
    def _():
        work(small)

    @pl.when(total > small)
    def _():
        work(most)

    move(yown_ref, own_at, y_s, 0, own_size)
    move(yoth_ref, oth_at, y_s, own_size, oth_size)


def run_experts(plan, where, own, oth, w_in, w_out, wr):
    experts, width, hidden = w_in.shape
    count = own.shape[0]
    most = (CAP + 2 * (GRAIN - 1)) // GRAIN * GRAIN
    outs = [sds((count, 2 * width), BF16)] * 2 + [sds((width, LANES), F32)]
    out_specs = [PLAIN_SPEC, PLAIN_SPEC, VMEM_SPEC]

    def part(at, size, tail):
        return pl.BlockSpec((1,) + tail, lambda e: (jnp.clip(e - at, 0, size - 1),) + (0,) * len(tail))

    at = 0
    for i, size in enumerate(PARTS):
        tail = (2, width, hidden) if i == 0 else (width, hidden)
        copies = 1 if i == 0 else 2
        outs += [sds((size,) + tail, BF16)] * copies
        out_specs += [part(at, size, tail)] * copies
        at += size
    return call(
        expert_kernel,
        tuple(outs),
        [pltpu.VMEM((most, 2 * width), BF16), pltpu.VMEM((most, 2 * width), BF16)],
        "experts",
        22, limit=28,
        grid=(experts,),
        in_specs=[
            SMEM_SPEC,
            SMEM_SPEC,
            VMEM_SPEC,
            PLAIN_SPEC,
            pl.BlockSpec((1, width, hidden), lambda e: (e, 0, 0)),
            pl.BlockSpec((1, hidden, width), lambda e: (e, 0, 0)),
            VMEM_SPEC,
        ],
        out_specs=tuple(out_specs),
    )(plan, where, own, oth, w_in, w_out, wr)


def unsort_kernel(where_ref, mine_ref, got_ref, unpick_ref, keep_ref, send_ref, y_s):
    count = mine_ref.shape[0]
    cpad, width = y_s.shape
    y_s[0:count, :] = (mine_ref[:, 0:width].astype(F32) + got_ref[:, 0:width].astype(F32)).astype(BF16)
    if cpad > count:
        y_s[count:cpad, :] = jnp.zeros((cpad - count, width), BF16)
    side = where_ref[1]
    send_ref[...] = mm(unpick_ref[1 - side], y_s[...]).astype(BF16)
    keep_ref[...] = mm(unpick_ref[side], y_s[...]).astype(BF16)


def run_unsort(where, mine, got, unpick):
    width = mine.shape[1] // 2
    half, cpad = unpick.shape[1:]
    outs = (sds((half, width), BF16), sds((half, width), BF16))
    return call(
        unsort_kernel, outs, [pltpu.VMEM((cpad, width), BF16)], "unsort", 4, limit=12,
        in_specs=[SMEM_SPEC, PLAIN_SPEC, PLAIN_SPEC, VMEM_SPEC], out_specs=(VMEM_SPEC, PLAIN_SPEC),
    )(where, mine, got, unpick)


def unsort_out_kernel(mine_ref, got_ref, pos_ref, ex_ref, y_s):
    count = mine_ref.shape[0]
    half = ex_ref.shape[0] // 2
    columns = jnp.broadcast_to(pos_ref[0:1, :], (LANES, pos_ref.shape[1])).T
    cpad, width = y_s.shape
    y_s[0:count, :] = (mine_ref[:, width:].astype(F32) + got_ref[:, width:].astype(F32)).astype(BF16)
    if cpad > count:
        y_s[count:cpad, :] = jnp.zeros((cpad - count, width), BF16)
    for part in range(2):
        rows = mm(unpick_part(columns, part, half, cpad), y_s[...]).astype(BF16)
        for i in range(half // STRIP):
            at = (2 * i + part) * STRIP
            ex_ref[at : at + STRIP, :] = rows[i * STRIP : (i + 1) * STRIP]


def run_unsort_out(mine, got, pos, own, after):
    count, width = mine.shape[0], mine.shape[1] // 2
    cpad = up(count, LANES)
    return call(
        unsort_out_kernel, sds((own, width), BF16), [pltpu.VMEM((cpad, width), BF16)], "unsort_out", 3, limit=12,
        in_specs=[PLAIN_SPEC, PLAIN_SPEC, VMEM_SPEC], out_specs=VMEM_SPEC, after=after,
    )(mine, got, pos)


def out_kernel(mid_ref, mine_ref, got_ref, out_ref):
    out_ref[...] = (mid_ref[...] + (mine_ref[...].astype(F32) + got_ref[...].astype(F32))).astype(BF16)


def run_out(mid, mine, got, after):
    return call(
        out_kernel, sds(mid.shape, BF16), [], "block_out", 2, limit=12,
        in_specs=[FAR_SPEC, PLAIN_SPEC, PLAIN_SPEC], out_specs=PLAIN_SPEC, after=after,
    )(mid, mine, got)


def join_kernel(where_ref, mine_ref, other_ref, out_ref, sems):
    own = mine_ref.shape[0]
    core = where_ref[0]
    copies = [
        pltpu.make_async_copy(ref, out_ref.at[pl.ds(pl.multiple_of(place * own, GRAIN), own), :], sems.at[i])
        for i, (ref, place) in enumerate(((mine_ref, core), (other_ref, 1 - core)))
    ]
    for copy in copies:
        copy.start()
    for copy in copies:
        copy.wait()


def run_join(where, mine, other, after):
    own, width = mine.shape
    return call(
        join_kernel, sds((2 * own, width), BF16), [pltpu.SemaphoreType.DMA((2,))], "join", 2, limit=4,
        in_specs=[SMEM_SPEC, PLAIN_SPEC, PLAIN_SPEC], out_specs=FAR_ANY, after=after,
    )(where, mine, other)


def mid_back_kernel(where_ref, keep_ref, got_ref, mid_ref, cot_ref, gain2_ref, ex_ref, gmid_ref, ga_ref, part_ref, ex_out, cot_s, mid_s, sems):
    half = keep_ref.shape[0]
    core, side = where_ref[0], where_ref[1]
    mid_copy = strip_copy(mid_ref, 0, side, mid_s, sems.at[0])
    mid_copy.start()
    copy = strip_copy(cot_ref, core * (half // STRIP), side, cot_s, sems.at[1])
    copy.start()
    grad_h2 = keep_ref[...].astype(F32) + got_ref[...].astype(F32)
    mid_copy.wait()
    normed2, scale2 = normalize_rows(mid_s[...].reshape(half, -1))
    part_ref[...] = jnp.broadcast_to(jnp.sum(grad_h2 * normed2, 0, keepdims=True), part_ref.shape)
    copy.wait()
    grad_final = cot_s[...].reshape(half, -1).astype(F32)
    grad_mid = grad_final + normal_back(grad_h2, normed2, scale2, gain2_ref[...])
    gmid_ref[...] = grad_mid
    ga_ref[...] = grad_mid.astype(BF16)
    ex_out[...] = ex_ref[...]


def run_mid_back(where, keep, got, mid, cot, gain2, ex, after):
    half, width = keep.shape
    outs = (sds((half, width), F32), sds((half, width), BF16), sds((8, width), F32), sds(ex.shape, BF16))
    return call(
        mid_back_kernel, outs, [pltpu.VMEM((half // STRIP, STRIP, width), dtype) for dtype in (BF16, F32)] + [pltpu.SemaphoreType.DMA((2,))],
        "mid_back", 4, limit=12,
        in_specs=[SMEM_SPEC, VMEM_SPEC, PLAIN_SPEC, FAR_ANY, FAR_ANY, VMEM_SPEC, VMEM_SPEC],
        out_specs=(FAR_SPEC, PLAIN_SPEC, VMEM_SPEC, FAR_SPEC), after=after,
    )(where, keep, got, in_strips(mid), in_strips(cot), gain2, ex)


def back_tiles(
    first_tile, last_tile, ends, side, own, q_s, do_s, lse_s, d_s, k_ref, v_ref, kt_ref,
    segk_s, qm_s, dm_s, dq_s, dk_s, dv_s,
):
    mine = kt_ref.shape[0]
    heads = mine // 64

    def place(index):
        return 2 * STRIP * (index // STRIP) + STRIP * side + index % STRIP

    def q_step(qb, carry):
        first = pl.multiple_of(qb * KB, KB)
        last = jnp.minimum(first + KB, own) - 1
        for h in range(heads):
            mask = head_mask(KB, h % 2)
            qm_s[h] = q_s[pl.ds(first, KB), lane_head(h)] * mask
            dm_s[h] = do_s[pl.ds(first, KB), lane_head(h)] * mask
        dq_s[:, pl.ds(first, KB)] = jnp.zeros((mine, KB), F32)
        low, high = seq_bounds(ends, place(first), place(last))
        start, steps = key_steps(low, high)
        index = lax.broadcasted_iota(jnp.int32, (8, KB), 1) + first
        segq = jnp.where(index < own, segment_of(place(index), ends), -1)[0:1]
        lse = [lse_s[h : h + 1, pl.ds(first, KB)] for h in range(heads)]
        dots = [d_s[h : h + 1, pl.ds(first, KB)] for h in range(heads)]

        def k_step(kb, carry):
            at = pl.multiple_of(start + kb * KB, LANES)
            bias = bias_block(segk_s, at, segq)
            s = [mm(k_ref[pl.ds(at, KB), lane_head(h)], qm_s[h], COLS_COLS) for h in range(heads)]
            dp = [mm(v_ref[pl.ds(at, KB), lane_head(h)], dm_s[h], COLS_COLS) for h in range(heads)]
            p = [jnp.exp((s[h] + bias) - lse[h]) for h in range(heads)]
            ds = [(p[h] * (dp[h] - dots[h])).astype(BF16) for h in range(heads)]
            p = [a.astype(BF16) for a in p]
            dv = [mm(p[h], dm_s[h]) for h in range(heads)]
            dk = [mm(ds[h], qm_s[h]) for h in range(heads)]
            dq = [mm(kt_ref[h * 64 : (h + 1) * 64, pl.ds(at, KB)], ds[h]) for h in range(heads)]
            for ref, add in ((dv_s, dv), (dk_s, dk)):
                for j in range(up(heads, 2) // 2):
                    pair = add[2 * j : 2 * j + 2]
                    ref[pl.ds(at, KB), j * LANES : (j + 1) * LANES] += pair[0] if len(pair) == 1 else pair[0] + pair[1]
            for h in range(heads):
                dq_s[h * 64 : (h + 1) * 64, pl.ds(first, KB)] += dq[h]
            return carry

        lax.fori_loop(0, steps, k_step, 0)
        return carry

    lax.fori_loop(first_tile, last_tile, q_step, 0)


def back_first_kernel(
    len_ref, where_ref, ga_ref, gao_ref, ho_any, q_any, lse_any, k_any, kt_any, v_any, hid_any, wproj_ref,
    ga_s, hid_s, ho_s, q_s, do_s, lse_s, d_s, dq_s, dk_s, dv_s,
    segk_s, qm_s, dm_s, col_s, k_ref, v_ref, kt_ref, hoc_s, lsec_s, qc_s, hidc_s, sems,
):
    half, width = ga_ref.shape
    own = 2 * half
    kpad = k_ref.shape[0]
    cpad = ga_s.shape[0]
    mine = kt_ref.shape[0]
    core, side = where_ref[0], where_ref[1]
    ends = seq_ends(len_ref, len_ref.shape[1])

    strips_of = (hoc_s, lsec_s, qc_s, hidc_s)
    copies = [
        strip_copy(ref, 0, side, dst, sems.at[i])
        for i, (ref, dst) in enumerate(zip((ho_any, lse_any, q_any, hid_any), strips_of))
    ] + [
        pltpu.make_async_copy(ref, dst, sems.at[4 + i])
        for i, (ref, dst) in enumerate(((k_any, k_ref), (v_any, v_ref), (kt_any, kt_ref)))
    ]
    for copy in copies:
        copy.start()
    key_segments(segk_s, ends, kpad)
    at = pl.multiple_of(core * half, GRAIN)
    ga_s[pl.ds(at, half), :] = ga_ref[...]
    at = pl.multiple_of((1 - core) * half, GRAIN)
    ga_s[pl.ds(at, half), :] = gao_ref[...]
    ga_s[own:cpad, :] = jnp.zeros((cpad - own, width), BF16)
    dk_s[...] = jnp.zeros(dk_s.shape, F32)
    dv_s[...] = jnp.zeros(dv_s.shape, F32)
    for copy in copies:
        copy.wait()
    for src, dst in zip(strips_of, (ho_s, col_s, q_s, hid_s)):
        dst[0:own, :] = src[0 : own // STRIP].reshape(own, -1)
        dst[own:cpad, :] = jnp.zeros((cpad - own, dst.shape[1]), dst.dtype)
    lse_s[...] = col_s[...].T[0:8]
    wproj = wproj_ref[pl.ds(pl.multiple_of(core * mine, GRAIN), mine), :]
    do_s[:, 0:mine] = mm(ga_s[...], wproj, COLS_COLS).astype(BF16)
    do_s[:, mine:] = jnp.zeros((cpad, do_s.shape[1] - mine), BF16)
    sub = lax.broadcasted_iota(jnp.int32, (8, do_s.shape[1]), 0)
    lane = lax.broadcasted_iota(jnp.int32, (8, do_s.shape[1]), 1)
    d_s[...] = lax.dot_general(
        (lane // 64 == sub).astype(F32),
        do_s[...].astype(F32) * ho_s[...].astype(F32),
        COLS_COLS,
        precision=lax.Precision.HIGHEST,
        preferred_element_type=F32,
    )

    back_tiles(
        0, FIRST_TILES, ends, side, own, q_s, do_s, lse_s, d_s, k_ref, v_ref, kt_ref,
        segk_s, qm_s, dm_s, dq_s, dk_s, dv_s,
    )


def back_second_kernel(
    len_ref, where_ref, k_any, kt_any, v_any, q_s, do_s, lse_s, d_s, dq_ref, dk_ref, dv_ref, w3_ref,
    hkeep_ref, hsend_ref, dqt_ref, dkt_ref, dvt_ref,
    segk_s, qm_s, dm_s, dq_s, dk_s, dv_s, gh_s, k_ref, v_ref, kt_ref, sems,
):
    own, width = hkeep_ref.shape
    rows = 2 * own
    kpad = k_ref.shape[0]
    cpad = q_s.shape[0]
    mine = w3_ref.shape[2]
    core, side = where_ref[0], where_ref[1]
    ends = seq_ends(len_ref, len_ref.shape[1])
    scale = 1.0 / math.sqrt(width // HEADS)
    copies = [
        pltpu.make_async_copy(ref, dst, sems.at[i])
        for i, (ref, dst) in enumerate(((k_any, k_ref), (v_any, v_ref), (kt_any, kt_ref)))
    ]
    for copy in copies:
        copy.start()
    key_segments(segk_s, ends, kpad)
    dq_s[...] = dq_ref[...]
    dk_s[...] = dk_ref[...]
    dv_s[...] = dv_ref[...]
    for copy in copies:
        copy.wait()
    back_tiles(
        FIRST_TILES, cpad // KB, ends, side, own, q_s, do_s, lse_s, d_s, k_ref, v_ref, kt_ref,
        segk_s, qm_s, dm_s, dq_s, dk_s, dv_s,
    )

    wq, wk, wv = w3_ref[0], w3_ref[1], w3_ref[2]
    dqt = (dq_s[...] * scale).astype(BF16)
    dqt_ref[...] = dqt
    step = rows // 8

    def h_body(i, carry):
        at = pl.ds(pl.multiple_of(i * step, GRAIN), step)
        gh_s[at, :] = mm(dk_s[at, 0:mine].astype(BF16), wk, COLS_COLS) + mm(
            dv_s[at, 0:mine].astype(BF16), wv, COLS_COLS
        )
        return carry

    lax.fori_loop(0, 8, h_body, 0)
    dkt_ref[...] = dk_s[...].astype(BF16).T[0:mine]
    dvt_ref[...] = dv_s[...].astype(BF16).T[0:mine]
    grad_q = mm(dqt.T, wq, COLS_COLS)
    for i in range(own // STRIP):
        at = pl.ds(strip_start(0, i, side), STRIP)
        gh_s[at, :] += grad_q[i * STRIP : (i + 1) * STRIP]
    hkeep_ref[...] = gh_s[pl.ds(pl.multiple_of(core * own, GRAIN), own), :].astype(BF16)
    hsend_ref[...] = gh_s[pl.ds(pl.multiple_of((1 - core) * own, GRAIN), own), :].astype(BF16)


def weight_kernel(
    dqt_ref, dkt_ref, dvt_ref, ga_ref, hidc_ref, hoc_ref, hid_any, groute_ref, gain2_ref, pay_ref, hid_ref, sem
):
    mine = dqt_ref.shape[0]
    width = ga_ref.shape[1]
    copy = pltpu.make_async_copy(hid_any, hid_ref, sem)
    copy.start()
    pay_ref[0:mine, :] = mm(dqt_ref[...], hidc_ref[...]).astype(BF16)
    pay_ref[3 * mine : 4 * mine, :] = mm(hoc_ref[...].T[0:mine], ga_ref[...]).astype(BF16)
    copy.wait()
    pay_ref[mine : 2 * mine, :] = mm(dkt_ref[...], hid_ref[...]).astype(BF16)
    pay_ref[2 * mine : 3 * mine, :] = mm(dvt_ref[...], hid_ref[...]).astype(BF16)
    pay_ref[4 * mine : 4 * mine + 8, :] = groute_ref[...].T[0:8].astype(BF16)
    pay_ref[4 * mine + 8 : 4 * mine + 16, :] = gain2_ref[...].astype(BF16)
    pay_ref[4 * mine + 16 :, :] = jnp.zeros((pay_ref.shape[0] - 4 * mine - 16, width), BF16)


def run_weights(pay_rows, dqt, dkt, dvt, ga, hidc, hoc, hid, groute, gain2, after):
    return call(
        weight_kernel, sds((pay_rows, ga.shape[1]), BF16),
        [pltpu.VMEM(hid.shape, BF16), pltpu.SemaphoreType.DMA], "weights", 4, limit=16,
        in_specs=[VMEM_SPEC] * 6 + [FAR_ANY] + [VMEM_SPEC] * 2, out_specs=PLAIN_SPEC, after=after,
    )(dqt, dkt, dvt, ga, hidc, hoc, hid, groute, gain2)


def run_back_first(lengths, where, ga, gao, ho, q, lse, k, kt, v, hid, wproj, after):
    half, width = ga.shape
    own = 2 * half
    kpad, lanes = k.shape
    mine = kt.shape[0]
    heads = mine // 64
    cpad = up(own, KB)
    outs = (
        sds((cpad, width), BF16),
        sds((cpad, width), BF16),
        sds((cpad, lanes), BF16),
        sds((cpad, lanes), BF16),
        sds((cpad, lanes), BF16),
        sds((8, cpad), F32),
        sds((8, cpad), F32),
        sds((mine, cpad), F32),
        sds((kpad, lanes), F32),
        sds((kpad, lanes), F32),
    )
    scratch = [
        pltpu.VMEM((kpad, LANES), jnp.int32),
        pltpu.VMEM((heads, KB, LANES), BF16),
        pltpu.VMEM((heads, KB, LANES), BF16),
        pltpu.VMEM((cpad, LANES), F32),
        pltpu.VMEM((kpad, lanes), BF16),
        pltpu.VMEM((kpad, lanes), BF16),
        pltpu.VMEM((mine, kpad), BF16),
        pltpu.VMEM((own // STRIP, STRIP, lanes), BF16),
        pltpu.VMEM((own // STRIP, STRIP, LANES), F32),
        pltpu.VMEM((own // STRIP, STRIP, lanes), BF16),
        pltpu.VMEM((own // STRIP, STRIP, width), BF16),
        pltpu.SemaphoreType.DMA((7,)),
    ]
    return call(
        back_first_kernel, outs, scratch, "back_first", 14,
        in_specs=[SMEM_SPEC, SMEM_SPEC, PLAIN_SPEC, PLAIN_SPEC] + [FAR_ANY] * 7 + [PLAIN_SPEC],
        out_specs=(VMEM_SPEC,) * 10, limit=24, after=after,
    )(lengths, where, ga, gao, in_strips(ho), in_strips(q), in_strips(lse), k, kt, v, in_strips(hid), wproj)


def run_back_second(own, lengths, where, k, kt, v, q, do, lse, dots, dq, dk, dv, w3, after):
    kpad, lanes = k.shape
    mine = kt.shape[0]
    heads = mine // 64
    cpad = q.shape[0]
    width = w3.shape[1]
    outs = (
        sds((own, width), BF16),
        sds((own, width), BF16),
        sds((mine, cpad), BF16),
        sds((mine, kpad), BF16),
        sds((mine, kpad), BF16),
    )
    scratch = [
        pltpu.VMEM((kpad, LANES), jnp.int32),
        pltpu.VMEM((heads, KB, LANES), BF16),
        pltpu.VMEM((heads, KB, LANES), BF16),
        pltpu.VMEM((mine, cpad), F32),
        pltpu.VMEM((kpad, lanes), F32),
        pltpu.VMEM((kpad, lanes), F32),
        pltpu.VMEM((2 * own, width), F32),
        pltpu.VMEM((kpad, lanes), BF16),
        pltpu.VMEM((kpad, lanes), BF16),
        pltpu.VMEM((mine, kpad), BF16),
        pltpu.SemaphoreType.DMA((3,)),
    ]
    return call(
        back_second_kernel, outs, scratch, "back_second", 14,
        in_specs=[SMEM_SPEC, SMEM_SPEC] + [FAR_ANY] * 3 + [VMEM_SPEC] * 7 + [PLAIN_SPEC],
        out_specs=(FAR_SPEC, PLAIN_SPEC) + (VMEM_SPEC,) * 3, limit=24, after=after,
    )(lengths, where, k, kt, v, q, do, lse, dots, dq, dk, dv, w3)


def token_kernel(where_ref, mine_ref, got_ref, gmid_ref, tok_ref, gain1_ref, out_ref, tok_s, sem):
    half = gmid_ref.shape[0]
    copy = strip_copy(tok_ref, where_ref[0] * (half // STRIP), where_ref[1], tok_s, sem)
    copy.start()
    grad_h1 = mine_ref[...].astype(F32) + got_ref[...].astype(F32)
    copy.wait()
    normed1, scale1 = normalize_rows(tok_s[...].reshape(half, -1).astype(F32))
    out_ref[...] = (gmid_ref[...] + normal_back(grad_h1, normed1, scale1, gain1_ref[...])).astype(BF16)


def run_tokens(where, mine, got, gmid, tokens, gain1, after):
    return call(
        token_kernel, sds(gmid.shape, BF16),
        [pltpu.VMEM((gmid.shape[0] // STRIP, STRIP, gmid.shape[1]), BF16), pltpu.SemaphoreType.DMA], "token_grad", 3, limit=12,
        in_specs=[SMEM_SPEC, FAR_SPEC, PLAIN_SPEC, FAR_SPEC, FAR_ANY, VMEM_SPEC], out_specs=PLAIN_SPEC, after=after,
    )(where, mine, got, gmid, in_strips(tokens), gain1)


def split_kernel(where_ref, a_ref, b_ref, keep_ref, send_ref):
    half = keep_ref.shape[0]
    total = (a_ref[...].astype(F32) + b_ref[...].astype(F32)).astype(BF16)
    side = where_ref[1]
    first, second = strips(total, 0, half), strips(total, 1, half)
    keep_ref[...] = jnp.where(side == 0, first, second)
    send_ref[...] = jnp.where(side == 0, second, first)


def run_split(where, a, b, after):
    own, width = a.shape
    outs = (sds((own // 2, width), BF16),) * 2
    return call(
        split_kernel, outs, [], "split", 2, limit=12, in_specs=[SMEM_SPEC, FAR_SPEC, PLAIN_SPEC],
        out_specs=(FAR_SPEC, PLAIN_SPEC), after=after,
    )(where, a, b)


def weave_kernel(where_ref, mine_ref, other_ref, out_ref):
    side = where_ref[1]
    for i in range(mine_ref.shape[0] // STRIP):
        rows = slice(i * STRIP, (i + 1) * STRIP)
        out_ref[pl.ds(strip_start(0, i, side), STRIP), :] = mine_ref[rows, :]
        out_ref[pl.ds(strip_start(0, i, 1 - side), STRIP), :] = other_ref[rows, :]


def run_weave(where, mine, other, after):
    half, width = mine.shape
    return call(
        weave_kernel, sds((2 * half, width), BF16), [], "weave", 2, limit=8,
        in_specs=[SMEM_SPEC] + [PLAIN_SPEC] * 2, out_specs=PLAIN_SPEC, after=after,
    )(where, mine, other)


def summed_end_kernel(total_ref, gin_ref, gout_ref):
    gin_ref[0] = total_ref[0, 0].astype(F32)
    gout_ref[0] = total_ref[0, 1].astype(F32)


def run_summed_end(total, shape_in, shape_out, after):
    size, unused, width, hidden = total.shape
    block = pl.BlockSpec((1, width, hidden), lambda e: (e, 0, 0))
    return call(
        summed_end_kernel,
        (sds(shape_in, F32), sds(shape_out, F32)),
        [],
        "summed_end",
        4, limit=12,
        grid=(size,),
        in_specs=[pl.BlockSpec((1, 2, width, hidden), lambda e: (e, 0, 0, 0))],
        out_specs=(block, block),
        after=after,
    )(total)


def expert_end_kernel(where_ref, mine_ref, other_ref, *refs):
    gin_ref, gout_ref = refs[-2:]
    e = pl.program_id(0)
    mine = mine_ref[e].astype(F32)
    other = other_ref[e].astype(F32)
    first = where_ref[2] == 0
    gin_ref[0] = jnp.where(first, mine, other)
    gout_ref[0] = jnp.where(first, other, mine)


def run_expert_end(at, where, mine, other, shape_in, shape_out, before):
    size, width, hidden = mine.shape
    block = pl.BlockSpec((1, width, hidden), lambda e: (e + at, 0, 0))
    return call(
        expert_end_kernel,
        (sds(shape_in, F32), sds(shape_out, F32)),
        [],
        "expert_end",
        3, limit=12,
        grid=(size,),
        in_specs=[SMEM_SPEC, PLAIN_SPEC, PLAIN_SPEC] + [FAR_ANY] * 2,
        out_specs=(block, block),
        input_output_aliases={3: 0, 4: 1},
    )(where, mine, other, *before)


def total_kernel(parts_ref, out_ref):
    pieces = parts_ref.shape[0]
    total = parts_ref[0].astype(F32)
    for i in range(1, pieces):
        total = total + parts_ref[i].astype(F32)
    total = total.astype(BF16)
    for i in range(pieces):
        out_ref[i] = total


def run_total(parts, after):
    return call(
        total_kernel, sds(parts.shape, BF16), [], "total", 2, limit=8, in_specs=[PLAIN_SPEC], out_specs=PLAIN_SPEC, after=after
    )(parts)


def attn_end_kernel(where_ref, mine_ref, other_ref, wqkv_ref, gain1_ref, gqkv_ref, gproj_ref, g1_ref, g2_ref, groute_ref):
    width = wqkv_ref.shape[1]
    share = width // 2
    first = where_ref[0] == 0
    mine = mine_ref[...].astype(F32)
    other = other_ref[...].astype(F32)
    low = jnp.where(first, mine, other)
    high = jnp.where(first, other, mine)
    product = jnp.zeros((width, width), F32)
    for i in range(3):
        rows = slice(i * share, (i + 1) * share)
        part = jnp.concatenate([low[rows], high[rows]], 0).T
        gqkv_ref[i] = part
        product = product + part * wqkv_ref[i].astype(F32)
    gproj_ref[...] = jnp.concatenate([low[3 * share : 4 * share], high[3 * share : 4 * share]], 0)
    g1_ref[...] = (jnp.sum(product.T, 0, keepdims=True) / gain1_ref[...])[0]
    small = low[4 * share : 4 * share + 16] + high[4 * share : 4 * share + 16]
    groute_ref[...] = small[0:8]
    g2_ref[...] = small[8]


def run_attn_end(where, mine, other, wqkv, gain1, after):
    width = wqkv.shape[1]
    outs = (
        sds((3, width, width), F32),
        sds((width, width), F32),
        sds((width,), F32),
        sds((width,), F32),
        sds((8, width), F32),
    )
    return call(
        attn_end_kernel, outs, [], "attn_end", 4, limit=16, in_specs=[SMEM_SPEC, PLAIN_SPEC, PLAIN_SPEC, VMEM_SPEC, VMEM_SPEC],
        out_specs=(FAR_SPEC,) * 5, after=after,
    )(where, mine, other, wqkv, gain1)


def swap(value, axis, mask):
    size = lax.axis_size(axis)
    return lax.ppermute(value, axis, [(i, i ^ mask) for i in range(size)])


def add_kernel(a_ref, b_ref, out_ref):
    out_ref[...] = (a_ref[...].astype(F32) + b_ref[...].astype(F32)).astype(BF16)


def added(a, b, after):
    return call(
        add_kernel, sds(a.shape, BF16), [], "add", 2, limit=8, in_specs=[PLAIN_SPEC] * 2, out_specs=PLAIN_SPEC, after=after
    )(a, b)


def choose_kernel(where_ref, inner_ref, outer_ref, out_ref):
    @pl.when(where_ref[3] == 0)
    def _():
        out_ref[...] = inner_ref[...]

    @pl.when(where_ref[3] != 0)
    def _():
        out_ref[...] = outer_ref[...]


def chosen(where, inner, outer, after):
    return call(
        choose_kernel, sds(inner.shape, BF16), [], "choose", 2, limit=8,
        in_specs=[SMEM_SPEC, PLAIN_SPEC, PLAIN_SPEC], out_specs=PLAIN_SPEC, after=after,
    )(where, inner, outer)


def wide_step(value, step):
    inward = [(w, w + 2) for w in (0, 1)] + [(w, w - 2) for w in (6, 7)]
    if step == 0:
        return lax.ppermute(value, "wide", inward)
    if step == 1:
        return lax.ppermute(value, "wide", [(2, 4), (3, 5), (4, 2), (5, 3)])
    return lax.ppermute(value, "wide", [(b, a) for a, b in inward])


def on_device(
    tokens, w_qkv, w_proj, norm1_gain, norm2_gain, w_route, w_in, w_out, cotangent, routes, kept_mask, lengths
):
    rows, width = tokens.shape
    own, half = rows // 2, rows // 4
    experts = w_in.shape[0]
    core, side = lax.axis_index("lo"), lax.axis_index("hi")
    wide_size, w = lax.axis_size("wide"), lax.axis_index("wide")
    z = w // 2
    outer = ((z == 0) | (z == wide_size // 2 - 1)).astype(jnp.int32)
    where = jnp.stack([core, side, w % 2, outer]).astype(jnp.int32)

    wqkv = w_qkv.transpose(1, 0, 2)
    w3 = lax.dynamic_slice_in_dim(wqkv, core * (width // 2), width // 2, 2)
    wr = jnp.pad(w_route, ((0, 0), (0, LANES - experts)))
    gain1 = norm1_gain.reshape(1, width)
    gain2 = norm2_gain.reshape(1, width)
    code = jnp.where(kept_mask == 1, routes[:, 0], experts).reshape(2, 1, own)
    code = jnp.pad(code, ((0, 0), (0, 0), (0, up(own, LANES) - own)), constant_values=experts)

    hid, k, kt, v, q, ho, lse, keep, send = run_front(lengths, where, tokens, w3, w_proj, gain1)
    got = swap(send, "lo", 1)
    plan, pos = run_plan(where, code, (keep, ANY_SPEC))
    mid, own_x, own_send = run_mid(where, keep, got, tokens, cotangent, gain2, wr, code, pos)
    oth_x = swap(own_send, "lo", 1)

    yown, yoth, groute, grads_a, *pairs = run_experts(plan, where, own_x, oth_x, w_in, w_out, wr)
    got = swap(yoth, "lo", 1)
    total_a = lax.psum(grads_a, "wide")
    pairs = [(pairs[2 * i], pairs[2 * i + 1]) for i in range(len(pairs) // 2)]
    recvs = [swap(give, "wide", 1) for unused, give in pairs]

    unpick = run_unpick(pos, own, own_x.shape[0], (yoth, ANY_SPEC))
    keep, send = run_unsort(where, yown, got, unpick)
    gh2 = swap(send, "hi", 1)
    ex = run_unsort_out(yown, got, pos, own, (send, ANY_SPEC))
    sums, moved = [], []
    for mine, unused in pairs:
        sums.append(mine)
    line = wide_size == 8

    def add_step(i, recv, after):
        sums[i] = added(sums[i], recv, after)
        return sums[i], ANY_SPEC

    def first_step(i, after):
        after = add_step(i, recvs[i], after)
        if line:
            moved.append(wide_step(sums[i], 0))
        else:
            for j in range(1, wide_size.bit_length() - 1):
                after = add_step(i, swap(sums[i], "wide", 1 << j), after)
        return after

    def line_step(i, step, after):
        if line:
            after = add_step(i, moved[i], after)
            moved[i] = wide_step(sums[i], step)
        return after

    def last_step(i, after):
        if line:
            sums[i] = chosen(where, sums[i], moved[i], after)
            after = sums[i], ANY_SPEC
        others.append(swap(sums[i], "wide", 1))
        return after

    others = []
    gmid, ga, gain2_part, ex = run_mid_back(where, keep, gh2, mid, cotangent, gain2, ex, (ex, VMEM_SPEC))
    gao = swap(ga, "lo", 1)
    ex_got = swap(ex, "hi", 1)
    last = first_step(0, (ex, FAR_ANY))

    ga_c, hid_c, ho_c, *state = run_back_first(lengths, where, ga, gao, ho, q, lse, k, kt, v, hid, w_proj, last)
    last = ga_c, VMEM_SPEC
    last = first_step(1, last)
    last = line_step(0, 1, last)
    last = first_step(2, last)
    hkeep, hsend, dqt, dkt, dvt = run_back_second(own, lengths, where, k, kt, v, *state, w3, last)
    hgot = swap(hsend, "lo", 1)
    last = hsend, ANY_SPEC
    last = line_step(0, 2, last)
    last = line_step(1, 1, last)
    last = line_step(2, 1, last)
    pay_rows = up(2 * width + 16, 8 * lax.axis_size(("wide", "hi")))
    pay = run_weights(pay_rows, dqt, dkt, dvt, ga_c, hid_c, ho_c, hid, groute, gain2_part, last)
    share = pay_rows // lax.axis_size(("wide", "hi"))
    pay_got = lax.all_to_all(pay.reshape(-1, share, width), ("wide", "hi"), 0, 0)
    last = pay, ANY_SPEC
    hk, hs = run_split(where, hkeep, hgot, last)
    hs_got = swap(hs, "hi", 1)
    out_own = run_out(mid, ex, ex_got, (hs, ANY_SPEC))
    out_oth = swap(out_own, "lo", 1)
    last = line_step(1, 2, (out_own, ANY_SPEC))
    last = last_step(0, last)
    last = line_step(2, 2, last)
    token_rows = run_tokens(where, hk, hs_got, gmid, tokens, gain1, last)
    token_got = swap(token_rows, "hi", 1)
    last = last_step(1, (token_rows, ANY_SPEC))
    pay_got = run_total(pay_got, last)
    last = pay_got, ANY_SPEC
    pay_got = lax.all_to_all(pay_got, ("wide", "hi"), 0, 0).reshape(pay.shape)
    layer_out = run_join(where, out_own, out_oth, last)
    token_own = run_weave(where, token_rows, token_got, (layer_out, FAR_ANY))
    token_oth = swap(token_own, "lo", 1)
    last = last_step(2, (token_own, ANY_SPEC))
    before = run_summed_end(total_a, w_in.shape, w_out.shape, last)
    at = PARTS[0]
    before = run_expert_end(at, where, sums[0], others[0], w_in.shape, w_out.shape, before)
    grad_tokens = run_join(where, token_own, token_oth, (before[0], FAR_ANY))
    before = run_expert_end(at + PARTS[1], where, sums[1], others[1], w_in.shape, w_out.shape, before)
    pay_oth = swap(pay_got, "lo", 1)
    grad_qkv, grad_proj, grad_norm1, grad_norm2, route_t = run_attn_end(
        where, pay_got, pay_oth, wqkv, gain1, (before[0], FAR_ANY)
    )
    grad_in, grad_out = run_expert_end(
        at + PARTS[1] + PARTS[2], where, sums[2], others[2], w_in.shape, w_out.shape, before
    )

    return (
        layer_out,
        grad_tokens,
        grad_qkv.transpose(1, 0, 2),
        grad_proj,
        grad_norm1,
        grad_norm2,
        route_t.T,
        grad_in,
        grad_out,
    )


def solution(mesh):
    axes = ("wide", ("hi", "lo"))
    split = Mesh(mesh.devices.reshape(mesh.shape["wide"], -1, 2), ("wide", "hi", "lo"))
    wide, narrow = axes
    in_specs = (
        P(wide, None),
        P(),
        P(),
        P(),
        P(),
        P(),
        P(None, None, narrow),
        P(None, narrow, None),
        P(wide, None),
        P(wide, None),
        P(wide),
        P(wide, None),
    )
    out_specs = (
        P(wide, None),
        P(wide, None),
        P(),
        P(),
        P(),
        P(),
        P(),
        P(None, None, narrow),
        P(None, narrow, None),
    )
    return jax.shard_map(on_device, mesh=split, in_specs=in_specs, out_specs=out_specs, check_vma=False)
```

```python
import math

import jax
import jax.numpy as jnp
from jax import lax
from jax.experimental import pallas as pl
from jax.experimental.pallas import tpu as pltpu
from jax.sharding import Mesh, PartitionSpec as P

HEADS = 6
CAP = 408
EPS = 1e-06
NEG = -1e30
F32 = jnp.float32
BF16 = jnp.bfloat16
LANES = 128
KB = 256
GRAIN = 16
STRIP = 32
FLOPS = 10**10
PARTS = (2, 2, 2, 2)
FIRST_TILES = 2
GELU_A = math.sqrt(2.0 / math.pi)
GELU_B = 0.044715

ROWS_COLS = (((1,), (0,)), ((), ()))
COLS_COLS = (((1,), (1,)), ((), ()))
ROWS_ROWS = (((0,), (0,)), ((), ()))


def up(value, grain):
    return -(-value // grain) * grain


def mm(a, b, dims=ROWS_COLS):
    return lax.dot_general(a, b, dims, preferred_element_type=F32)


def normalize_rows(values):
    centre = values - jnp.mean(values, -1, keepdims=True)
    row_scale = lax.rsqrt(jnp.mean(centre * centre, -1, keepdims=True) + EPS)
    return centre * row_scale, row_scale


def normal_back(grad_h, normed, row_scale, gain_row):
    g = grad_h * gain_row
    return row_scale * (
        g - jnp.mean(g, -1, keepdims=True) - normed * jnp.mean(g * normed, -1, keepdims=True)
    )


def lane_head(h):
    return slice((h // 2) * LANES, (h // 2 + 1) * LANES)


def seq_ends(len_ref, count):
    ends = []
    total = jnp.int32(0)
    for j in range(count):
        total = total + len_ref[0, j]
        ends.append(total)
    return ends


def seq_bounds(ends, first_row, last_row):
    low = jnp.int32(0)
    high = ends[-1]
    for end in ends:
        low = jnp.where(end <= first_row, end, low)
    for end in reversed(ends):
        high = jnp.where(end > last_row, end, high)
    return low, high


def segment_of(index, ends):
    seg = jnp.zeros(index.shape, jnp.int32)
    for end in ends:
        seg = seg + (index >= end).astype(jnp.int32)
    return seg


def key_segments(segk_ref, ends, kpad):
    def body(i, carry):
        start = pl.multiple_of(i * LANES, LANES)
        index = lax.broadcasted_iota(jnp.int32, (LANES, LANES), 0) + start
        segk_ref[pl.ds(start, LANES), :] = segment_of(index, ends)
        return carry

    lax.fori_loop(0, kpad // LANES, body, 0)


def bias_block(segk_ref, kstart, segq):
    segk = segk_ref[pl.ds(kstart, KB), :]
    return jnp.where(jnp.concatenate([segk, segk], 1) == segq, 0.0, NEG)


def head_mask(rows, odd):
    lane = lax.broadcasted_iota(jnp.int32, (rows, LANES), 1)
    return ((lane >= 64) if odd else (lane < 64)).astype(BF16)


def plan_of(code_row, experts):
    n = code_row.shape[1]
    sub = lax.broadcasted_iota(jnp.int32, (experts, n), 0)
    lane = lax.broadcasted_iota(jnp.int32, (experts, n), 1)
    member = (code_row == sub).astype(F32)
    rank = member
    shift = 1
    while shift < n:
        rank = rank + jnp.where(lane >= shift, pltpu.roll(rank, shift, 1), 0.0)
        shift *= 2
    counts = jnp.broadcast_to(rank[:, n - 1 : n], (experts, LANES))
    sizes = jnp.floor((counts + (GRAIN - 1)) * (1.0 / GRAIN)) * GRAIN
    row = lax.broadcasted_iota(jnp.int32, (experts, LANES), 0)
    total = sizes
    shift = 1
    while shift < experts:
        total = total + jnp.where(row >= shift, pltpu.roll(total, shift, 0), 0.0)
        shift *= 2
    offsets = total - sizes
    pos = jnp.sum(member * (rank + offsets[:, 0:1]), 0, keepdims=True) - 1.0
    return pos, offsets, sizes


def key_steps(low, high):
    start = low // LANES * LANES
    return start, (high - start + KB - 1) // KB


def plan_kernel(where_ref, code_ref, plan_ref, pos_ref):
    experts = 8
    core = where_ref[0]
    pos, offsets, sizes = plan_of(code_ref[core], experts)
    unused, other_offsets, other_sizes = plan_of(code_ref[1 - core], experts)
    plan_ref[0:8, :] = offsets.astype(jnp.int32)
    plan_ref[8:16, :] = sizes.astype(jnp.int32)
    plan_ref[16:24, :] = other_offsets.astype(jnp.int32)
    plan_ref[24:32, :] = other_sizes.astype(jnp.int32)
    pos_ref[...] = jnp.broadcast_to(pos, pos_ref.shape)


def unpick_part(columns, part, half, cpad):
    lane = lax.broadcasted_iota(jnp.int32, (half, LANES), 1).astype(F32)
    column = strips(columns, part, half)
    return jnp.concatenate(
        [jnp.where(column == lane + float(j * LANES), 1.0, 0.0).astype(BF16) for j in range(cpad // LANES)], 1
    )


def unpick_kernel(pos_ref, unpick_ref):
    half, cpad = unpick_ref.shape[1:]
    columns = jnp.broadcast_to(pos_ref[0:1, :], (LANES, pos_ref.shape[1])).T
    for part in range(2):
        unpick_ref[part] = unpick_part(columns, part, half, cpad)


def run_unpick(pos, own, count, after):
    return call(
        unpick_kernel, sds((2, own // 2, up(count, LANES)), BF16), [], "unpick", 2, limit=12,
        in_specs=[VMEM_SPEC], after=after,
    )(pos)


def strips(value, part, half):
    return jnp.concatenate(
        [value[(2 * i + part) * STRIP : (2 * i + part + 1) * STRIP] for i in range(half // STRIP)], 0
    )


def strip_start(base, i, side):
    return pl.multiple_of(base + 2 * STRIP * i + STRIP * side, STRIP)


def in_strips(array):
    return array.reshape(-1, 2, STRIP, array.shape[-1])


def strip_copy(ref, first, side, dst, sem):
    return pltpu.make_async_copy(ref.at[pl.ds(first, dst.shape[0]), side], dst, sem)


def load_strips(ref, base, side, half):
    return jnp.concatenate([ref[pl.ds(strip_start(base, i, side), STRIP), :] for i in range(half // STRIP)], 0)


def front_kernel(
    len_ref, where_ref, tok_ref, w3_ref, wproj_ref, gain1_ref,
    hid_out, k_out, kt_out, v_out, q_out, ho_out, lse_out, keep_ref, send_ref,
    hid_ref, k_ref, kt_ref, v_ref, q_ref, ho_ref, lse_ref,
    vt_s, segk_s, qm_s, acc_s, m_s, l_s, s_s, st_s, sems,
):
    rows, width = tok_ref.shape
    own = rows // 2
    copies = [
        pltpu.make_async_copy(src, dst, sems.at[i])
        for i, (src, dst) in enumerate(
            (
                (hid_ref, hid_out), (k_ref, k_out), (kt_ref, kt_out), (v_ref, v_out), (q_ref, q_out),
                (ho_ref, ho_out), (lse_ref, lse_out),
            )
        )
    ]
    kpad = hid_ref.shape[0]
    qpad = q_ref.shape[0]
    mine = w3_ref.shape[2]
    heads = mine // 64
    core = where_ref[0]
    ends = seq_ends(len_ref, len_ref.shape[1])
    scale = 1.0 / math.sqrt(width // HEADS)
    key_segments(segk_s, ends, kpad)
    gain1 = gain1_ref[...]
    wq, wk, wv = w3_ref[0], w3_ref[1], w3_ref[2]
    step = rows // 4

    def norm_body(i, carry):
        at = pl.ds(pl.multiple_of(i * step, GRAIN), step)
        normed, unused = normalize_rows(tok_ref[at, :].astype(F32))
        hid = (normed * gain1).astype(BF16)
        hid_ref[at, :] = hid
        k_ref[at, 0:mine] = mm(hid, wk).astype(BF16)
        v_ref[at, 0:mine] = mm(hid, wv).astype(BF16)
        q_ref[at, 0:mine] = (mm(hid, wq).astype(BF16).astype(F32) * scale).astype(BF16)
        return carry

    lax.fori_loop(0, 4, norm_body, 0)
    hid_ref[rows:kpad, :] = jnp.zeros((kpad - rows, width), BF16)
    for ref in (k_ref, v_ref, q_ref):
        size = ref.shape[0]
        ref[rows:size, 0:mine] = jnp.zeros((size - rows, mine), BF16)
        ref[:, mine:] = jnp.zeros((size, ref.shape[1] - mine), BF16)
    wkt = wk.T
    wvt = wv.T

    def key_body(i, carry):
        at = pl.ds(pl.multiple_of(i * 2 * KB, 2 * KB), 2 * KB)
        hid = hid_ref[at, :]
        kt_ref[:, at] = mm(wkt, hid, COLS_COLS).astype(BF16)
        vt_s[:, at] = mm(wvt, hid, COLS_COLS).astype(BF16)
        return carry

    lax.fori_loop(0, kpad // (2 * KB), key_body, 0)
    for copy in copies[:5]:
        copy.start()
    st_s[...] = jnp.zeros(st_s.shape, F32)

    def q_step(qb, carry):
        first = pl.multiple_of(qb * KB, KB)
        last = jnp.minimum(first + KB, rows) - 1
        for h in range(heads):
            qm_s[h] = q_ref[pl.ds(first, KB), lane_head(h)] * head_mask(KB, h % 2)
        for h in range(heads):
            m_s[h : h + 1] = jnp.full((1, KB), NEG, F32)
            l_s[h : h + 1] = jnp.zeros((1, KB), F32)
        acc_s[...] = jnp.zeros(acc_s.shape, F32)
        low, high = seq_bounds(ends, first, last)
        start, steps = key_steps(low, high)
        segq = segment_of(lax.broadcasted_iota(jnp.int32, (8, KB), 1) + first, ends)[0:1]

        def scores(at):
            return [mm(k_ref[pl.ds(at, KB), lane_head(h)], qm_s[h], COLS_COLS) for h in range(heads)]

        for h, s in enumerate(scores(pl.multiple_of(start, LANES))):
            s_s[h] = s

        def k_step(kb, carry):
            at = pl.multiple_of(start + kb * KB, LANES)
            later = pl.multiple_of(start + jnp.minimum(kb + 1, steps - 1) * KB, LANES)
            bias = bias_block(segk_s, at, segq)
            now = [s_s[h] + bias for h in range(heads)]
            nexts = scores(later)
            m_old = [m_s[h : h + 1] for h in range(heads)]
            m_new = [jnp.maximum(m, jnp.max(s, 0, keepdims=True)) for m, s in zip(m_old, now)]
            p = [jnp.exp(s - m) for s, m in zip(now, m_new)]
            alpha = [jnp.exp(a - b) for a, b in zip(m_old, m_new)]
            for h in range(heads):
                m_s[h : h + 1] = m_new[h]
                l_s[h : h + 1] = l_s[h : h + 1] * alpha[h] + jnp.sum(p[h], 0, keepdims=True)
            out = [mm(vt_s[h * 64 : (h + 1) * 64, pl.ds(at, KB)], p[h].astype(BF16)) for h in range(heads)]
            for h in range(heads):
                acc_s[h * 64 : (h + 1) * 64] = acc_s[h * 64 : (h + 1) * 64] * alpha[h] + out[h]
                s_s[h] = nexts[h]
            return carry

        lax.fori_loop(0, steps, k_step, 0)
        parts = []
        for h in range(heads):
            total = l_s[h : h + 1]
            st_s[h : h + 1] = m_s[h : h + 1] + jnp.log(total)
            parts.append(acc_s[h * 64 : (h + 1) * 64] * (1.0 / total))
        lse_ref[pl.ds(first, KB), :] = st_s[...].T
        parts.append(jnp.zeros((ho_ref.shape[1] - mine, KB), F32))
        ho_ref[pl.ds(first, KB), :] = jnp.concatenate(parts, 0).T.astype(BF16)
        return carry

    lax.fori_loop(0, qpad // KB, q_step, 0)
    for copy in copies[5:]:
        copy.start()
    wproj = wproj_ref[pl.ds(pl.multiple_of(core * mine, GRAIN), mine), :]
    keep_ref[...] = mm(ho_ref[pl.ds(pl.multiple_of(core * own, GRAIN), own), 0:mine], wproj).astype(BF16)
    send_ref[...] = mm(ho_ref[pl.ds(pl.multiple_of((1 - core) * own, GRAIN), own), 0:mine], wproj).astype(BF16)
    for copy in copies:
        copy.wait()


def mid_kernel(
    where_ref, keep_ref, got_ref, tok_ref, cot_ref, gain2_ref, wr_ref, code_ref, pos_ref,
    mid_ref, sorted_ref, send_ref, x_s, tok_s, cot_s, mid_s, sems,
):
    own, width = keep_ref.shape
    npad = x_s.shape[0]
    core = where_ref[0]
    at = pl.ds(pl.multiple_of(core * own, GRAIN), own)
    tok_copy = pltpu.make_async_copy(tok_ref.at[at, :], tok_s, sems.at[0])
    cot_copy = pltpu.make_async_copy(cot_ref.at[at, :], cot_s, sems.at[1])
    tok_copy.start()
    cot_copy.start()
    tok_copy.wait()
    mid = tok_s[...].astype(F32) + (keep_ref[...].astype(F32) + got_ref[...].astype(F32))
    mid_s[...] = mid
    mid_copy = pltpu.make_async_copy(mid_s, mid_ref, sems.at[6])
    mid_copy.start()
    normed2, unused = normalize_rows(mid)
    hidden2 = (normed2 * gain2_ref[...]).astype(BF16)
    lane = lax.broadcasted_iota(jnp.int32, (own, LANES), 1)
    gates = router_gates(hidden2, wr_ref[...], lane, 8)
    code_col = jnp.broadcast_to(code_ref[core].astype(F32), (LANES, npad)).T[0:own]
    gate = jnp.sum(jnp.where(code_col == lane.astype(F32), gates, 0.0), -1, keepdims=True)
    x_s[0:own, 0:width] = hidden2
    cot_copy.wait()
    x_s[0:own, width:] = (gate * cot_s[...].astype(F32)).astype(BF16)
    x_s[own:npad, :] = jnp.zeros((npad - own, 2 * width), BF16)
    piece = sorted_ref.shape[0] // 4
    copies = []
    for i in range(4):
        rows = slice(i * piece, (i + 1) * piece)
        sub = lax.broadcasted_iota(jnp.int32, (piece, npad), 0) + i * piece
        pick = jnp.where(sub.astype(F32) == pos_ref[0:1, :], 1.0, 0.0).astype(BF16)
        sorted_ref[rows, :] = mm(pick, x_s[...]).astype(BF16)
        copies.append(pltpu.make_async_copy(sorted_ref.at[rows, :], send_ref.at[rows, :], sems.at[2 + i]))
        copies[-1].start()
    for copy in copies + [mid_copy]:
        copy.wait()


def router_gates(hidden2, wr, lane, experts):
    logits = jnp.where(lane < experts, mm(hidden2, wr), NEG)
    top = jnp.max(logits, -1, keepdims=True)
    e = jnp.exp(logits - top)
    return e / jnp.sum(e, -1, keepdims=True)


def call(kernel, outs, scratch, name, micros, in_specs, limit=24, after=None, **more):
    def out_of(shape, spec):
        if spec is VMEM_SPEC:
            return pltpu.VMEM(shape.shape, shape.dtype)
        return pltpu.HBM(shape.shape, shape.dtype) if is_far(spec) else shape

    out_specs = more.get("out_specs")
    if out_specs is None:
        out_specs = jax.tree.map(lambda o: VMEM_SPEC, outs)
    if isinstance(outs, tuple):
        outs = tuple(out_of(o, spec) for o, spec in zip(outs, out_specs))
    else:
        outs = out_of(outs, out_specs)
    more["out_specs"] = out_specs
    aliases = more.pop("input_output_aliases", {})
    body = kernel
    if after is not None:
        in_specs = [ANY_SPEC] + list(in_specs)
        aliases = {i + 1: o for i, o in aliases.items()}
        body = lambda after_ref, *refs: kernel(*refs)
    run = pl.pallas_call(
        body,
        out_shape=outs,
        in_specs=in_specs,
        scratch_shapes=scratch,
        name=name,
        input_output_aliases=aliases,
        compiler_params=pltpu.CompilerParams(vmem_limit_bytes=limit * 1024 * 1024),
        cost_estimate=pl.CostEstimate(flops=micros * FLOPS, bytes_accessed=10**4, transcendentals=0),
        **more,
    )

    def place(array, spec):
        if spec is VMEM_SPEC:
            return pltpu.with_memory_space_constraint(array, pltpu.VMEM)
        return pltpu.with_memory_space_constraint(array, pltpu.HBM) if is_far(spec) else array

    def run_on(*args):
        placed = [place(a, spec) for a, spec in zip(args, in_specs[len(in_specs) - len(args) :])]
        if after is not None:
            array, spec = after
            placed = [place(array, spec)] + placed
        return run(*placed)

    return run_on


def is_far(spec):
    return spec is FAR_SPEC or spec is FAR_ANY or spec.block_shape is not None


ANY_SPEC = pl.BlockSpec(memory_space=pl.ANY)
FAR_SPEC = pl.BlockSpec(memory_space=pltpu.VMEM)
FAR_ANY = pl.BlockSpec(memory_space=pl.ANY)
PLAIN_SPEC = pl.BlockSpec(memory_space=pltpu.VMEM)
SMEM_SPEC = pl.BlockSpec(memory_space=pltpu.SMEM)
VMEM_SPEC = pl.BlockSpec(memory_space=pltpu.VMEM)


def sds(shape, dtype):
    return jax.ShapeDtypeStruct(shape, dtype)


def run_plan(where, code, after=None):
    npad = code.shape[2]
    outs = (
        sds((32, LANES), jnp.int32),
        sds((8, npad), F32),
    )
    return call(plan_kernel, outs, [], "plan", 5, limit=12, in_specs=[SMEM_SPEC, VMEM_SPEC], after=after)(where, code)


def run_front(lengths, where, tokens, w3, wproj, gain1):
    rows, width = tokens.shape
    own = rows // 2
    mine = w3.shape[2]
    heads = mine // 64
    kpad = up(rows + KB, 2 * KB)
    qpad = up(rows, KB)
    lanes = up(mine, LANES)
    outs = (
        sds((kpad, width), BF16),
        sds((kpad, lanes), BF16),
        sds((mine, kpad), BF16),
        sds((kpad, lanes), BF16),
        sds((qpad, lanes), BF16),
        sds((qpad, lanes), BF16),
        sds((qpad, LANES), F32),
        sds((own, width), BF16),
        sds((own, width), BF16),
    )
    scratch = [pltpu.VMEM(o.shape, o.dtype) for o in outs[:7]] + [
        pltpu.VMEM((mine, kpad), BF16),
        pltpu.VMEM((kpad, LANES), jnp.int32),
        pltpu.VMEM((heads, KB, LANES), BF16),
        pltpu.VMEM((mine, KB), F32),
        pltpu.VMEM((8, KB), F32),
        pltpu.VMEM((8, KB), F32),
        pltpu.VMEM((heads, KB, KB), F32),
        pltpu.VMEM((LANES, KB), F32),
        pltpu.SemaphoreType.DMA((7,)),
    ]
    return call(
        front_kernel, outs, scratch, "front", 33, in_specs=[SMEM_SPEC, SMEM_SPEC, FAR_SPEC, PLAIN_SPEC, FAR_SPEC, PLAIN_SPEC],
        limit=32,
        out_specs=(FAR_ANY,) * 7 + (PLAIN_SPEC,) * 2,
    )(lengths, where, tokens, w3, wproj, gain1)


def run_mid(where, keep, got, tokens, cot, gain2, wr, code, pos):
    own, width = keep.shape
    count = up(own + 8 * (GRAIN - 1), 4 * GRAIN)
    outs = (sds((own, width), F32),) + (sds((count, 2 * width), BF16),) * 2
    scratch = [
        pltpu.VMEM((code.shape[2], 2 * width), BF16),
        pltpu.VMEM((own, width), BF16),
        pltpu.VMEM((own, width), BF16),
        pltpu.VMEM((own, width), F32),
        pltpu.SemaphoreType.DMA((7,)),
    ]
    return call(
        mid_kernel, outs, scratch, "mid", 9, limit=20,
        in_specs=[SMEM_SPEC, PLAIN_SPEC, PLAIN_SPEC, FAR_ANY, FAR_ANY] + [VMEM_SPEC] * 4,
        out_specs=(FAR_ANY, VMEM_SPEC, ANY_SPEC),
    )(where, keep, got, tokens, cot, gain2, wr, code, pos)


def expert_kernel(
    plan_ref, where_ref, own_ref, oth_ref, win_ref, wout_ref, wr_ref,
    yown_ref, yoth_ref, groute_ref, *refs,
):
    *grads, x_s, y_s = refs
    e = pl.program_id(0)
    width = win_ref.shape[1]
    most = x_s.shape[0]

    @pl.when(e == 0)
    def _():
        yown_ref[...] = jnp.zeros(yown_ref.shape, BF16)
        yoth_ref[...] = jnp.zeros(yoth_ref.shape, BF16)
        groute_ref[...] = jnp.zeros(groute_ref.shape, F32)

    own_at, own_size = plan_ref[e, 0], plan_ref[8 + e, 0]
    oth_at, oth_size = plan_ref[16 + e, 0], plan_ref[24 + e, 0]
    total = own_size + oth_size

    def move(dst, dst_at, src, src_at, size):
        def body(i, carry):
            a = pl.multiple_of(dst_at + i * GRAIN, GRAIN)
            b = pl.multiple_of(src_at + i * GRAIN, GRAIN)
            dst[pl.ds(a, GRAIN), :] = src[pl.ds(b, GRAIN), :]
            return carry

        lax.fori_loop(0, size // GRAIN, body, 0)

    move(x_s, 0, own_ref, own_at, own_size)
    move(x_s, own_size, oth_ref, oth_at, oth_size)

    def work(m):
        def zero_body(i, carry):
            x_s[pl.ds(pl.multiple_of(i * GRAIN, GRAIN), GRAIN), :] = jnp.zeros((GRAIN, 2 * width), BF16)
            return carry

        lax.fori_loop(total // GRAIN, m // GRAIN, zero_body, 0)
        h = x_s[0:m, 0:width]
        g = x_s[0:m, width:]
        w_in = win_ref[0]
        w_out = wout_ref[0]
        lane = lax.broadcasted_iota(jnp.int32, (m, LANES), 1)
        gates = router_gates(h, wr_ref[...], lane, 8)
        here = (lane == e).astype(F32)
        pre = mm(h, w_in)
        t = jnp.tanh(GELU_A * (pre + GELU_B * (pre * pre * pre)))
        act = (0.5 * pre * (1.0 + t)).astype(BF16)
        slope = 0.5 * (1.0 + t) + 0.5 * pre * (1.0 - t * t) * (GELU_A * (1.0 + 3.0 * GELU_B * (pre * pre)))
        out = mm(act, w_out)
        grad_pre = (mm(g, w_out, COLS_COLS) * slope).astype(BF16)
        dot = jnp.sum(g.astype(F32) * out, -1, keepdims=True)
        grad_logits = (dot * (here - gates)).astype(BF16)
        gate = jnp.sum(gates * here, -1, keepdims=True)
        y_s[0:m, 0:width] = (mm(grad_pre, w_in, COLS_COLS) + mm(grad_logits, wr_ref[...], COLS_COLS)).astype(BF16)
        y_s[0:m, width:] = (gate * out).astype(BF16)
        ht = h.T
        groute_ref[...] += mm(ht, grad_logits)
        grad_in = mm(ht, grad_pre).astype(BF16)
        grad_out = mm(act.T, g).astype(BF16)

        at = 0
        for i, size in enumerate(PARTS):
            here = (e >= at) & (e < at + size)
            if i == 0:
                put_both(grads[0], grad_in, grad_out, here)
            else:
                put(grads[2 * i - 1 : 2 * i + 1], grad_in, grad_out, here)
            at += size

    def put_both(ref, grad_in, grad_out, here):
        @pl.when(here)
        def _():
            ref[0, 0] = grad_in
            ref[0, 1] = grad_out

    def put(pair, grad_in, grad_out, here):
        keep_ref, send_ref = pair

        @pl.when(here & (where_ref[2] == 0))
        def _():
            keep_ref[0] = grad_in
            send_ref[0] = grad_out

        @pl.when(here & (where_ref[2] != 0))
        def _():
            keep_ref[0] = grad_out
            send_ref[0] = grad_in

    small = up(CAP * 2 // 3, GRAIN)

    @pl.when(total <= small)
    def _():
        work(small)

    @pl.when(total > small)
    def _():
        work(most)

    move(yown_ref, own_at, y_s, 0, own_size)
    move(yoth_ref, oth_at, y_s, own_size, oth_size)


def run_experts(plan, where, own, oth, w_in, w_out, wr):
    experts, width, hidden = w_in.shape
    count = own.shape[0]
    most = (CAP + 2 * (GRAIN - 1)) // GRAIN * GRAIN
    outs = [sds((count, 2 * width), BF16)] * 2 + [sds((width, LANES), F32)]
    out_specs = [PLAIN_SPEC, PLAIN_SPEC, VMEM_SPEC]

    def part(at, size, tail):
        return pl.BlockSpec((1,) + tail, lambda e: (jnp.clip(e - at, 0, size - 1),) + (0,) * len(tail))

    at = 0
    for i, size in enumerate(PARTS):
        tail = (2, width, hidden) if i == 0 else (width, hidden)
        copies = 1 if i == 0 else 2
        outs += [sds((size,) + tail, BF16)] * copies
        out_specs += [part(at, size, tail)] * copies
        at += size
    return call(
        expert_kernel,
        tuple(outs),
        [pltpu.VMEM((most, 2 * width), BF16), pltpu.VMEM((most, 2 * width), BF16)],
        "experts",
        22, limit=28,
        grid=(experts,),
        in_specs=[
            SMEM_SPEC,
            SMEM_SPEC,
            VMEM_SPEC,
            PLAIN_SPEC,
            pl.BlockSpec((1, width, hidden), lambda e: (e, 0, 0)),
            pl.BlockSpec((1, hidden, width), lambda e: (e, 0, 0)),
            VMEM_SPEC,
        ],
        out_specs=tuple(out_specs),
    )(plan, where, own, oth, w_in, w_out, wr)


def unsort_kernel(where_ref, mine_ref, got_ref, unpick_ref, keep_ref, send_ref, y_s):
    count = mine_ref.shape[0]
    cpad, width = y_s.shape
    y_s[0:count, :] = (mine_ref[:, 0:width].astype(F32) + got_ref[:, 0:width].astype(F32)).astype(BF16)
    if cpad > count:
        y_s[count:cpad, :] = jnp.zeros((cpad - count, width), BF16)
    side = where_ref[1]
    send_ref[...] = mm(unpick_ref[1 - side], y_s[...]).astype(BF16)
    keep_ref[...] = mm(unpick_ref[side], y_s[...]).astype(BF16)


def run_unsort(where, mine, got, unpick):
    width = mine.shape[1] // 2
    half, cpad = unpick.shape[1:]
    outs = (sds((half, width), BF16), sds((half, width), BF16))
    return call(
        unsort_kernel, outs, [pltpu.VMEM((cpad, width), BF16)], "unsort", 4, limit=12,
        in_specs=[SMEM_SPEC, PLAIN_SPEC, PLAIN_SPEC, VMEM_SPEC], out_specs=(VMEM_SPEC, PLAIN_SPEC),
    )(where, mine, got, unpick)


def unsort_out_kernel(mine_ref, got_ref, pos_ref, ex_ref, y_s):
    count = mine_ref.shape[0]
    half = ex_ref.shape[0] // 2
    columns = jnp.broadcast_to(pos_ref[0:1, :], (LANES, pos_ref.shape[1])).T
    cpad, width = y_s.shape
    y_s[0:count, :] = (mine_ref[:, width:].astype(F32) + got_ref[:, width:].astype(F32)).astype(BF16)
    if cpad > count:
        y_s[count:cpad, :] = jnp.zeros((cpad - count, width), BF16)
    for part in range(2):
        rows = mm(unpick_part(columns, part, half, cpad), y_s[...]).astype(BF16)
        for i in range(half // STRIP):
            at = (2 * i + part) * STRIP
            ex_ref[at : at + STRIP, :] = rows[i * STRIP : (i + 1) * STRIP]


def run_unsort_out(mine, got, pos, own, after):
    count, width = mine.shape[0], mine.shape[1] // 2
    cpad = up(count, LANES)
    return call(
        unsort_out_kernel, sds((own, width), BF16), [pltpu.VMEM((cpad, width), BF16)], "unsort_out", 3, limit=12,
        in_specs=[PLAIN_SPEC, PLAIN_SPEC, VMEM_SPEC], out_specs=VMEM_SPEC, after=after,
    )(mine, got, pos)


def out_kernel(mid_ref, mine_ref, got_ref, out_ref):
    out_ref[...] = (mid_ref[...] + (mine_ref[...].astype(F32) + got_ref[...].astype(F32))).astype(BF16)


def run_out(mid, mine, got, after):
    return call(
        out_kernel, sds(mid.shape, BF16), [], "block_out", 2, limit=12,
        in_specs=[FAR_SPEC, PLAIN_SPEC, PLAIN_SPEC], out_specs=PLAIN_SPEC, after=after,
    )(mid, mine, got)


def join_kernel(where_ref, mine_ref, other_ref, out_ref, sems):
    own = mine_ref.shape[0]
    core = where_ref[0]
    copies = [
        pltpu.make_async_copy(ref, out_ref.at[pl.ds(pl.multiple_of(place * own, GRAIN), own), :], sems.at[i])
        for i, (ref, place) in enumerate(((mine_ref, core), (other_ref, 1 - core)))
    ]
    for copy in copies:
        copy.start()
    for copy in copies:
        copy.wait()


def run_join(where, mine, other, after):
    own, width = mine.shape
    return call(
        join_kernel, sds((2 * own, width), BF16), [pltpu.SemaphoreType.DMA((2,))], "join", 2, limit=4,
        in_specs=[SMEM_SPEC, PLAIN_SPEC, PLAIN_SPEC], out_specs=FAR_ANY, after=after,
    )(where, mine, other)


def mid_back_kernel(where_ref, keep_ref, got_ref, mid_ref, cot_ref, gain2_ref, ex_ref, gmid_ref, ga_ref, part_ref, ex_out, cot_s, mid_s, sems):
    half = keep_ref.shape[0]
    core, side = where_ref[0], where_ref[1]
    mid_copy = strip_copy(mid_ref, 0, side, mid_s, sems.at[0])
    mid_copy.start()
    copy = strip_copy(cot_ref, core * (half // STRIP), side, cot_s, sems.at[1])
    copy.start()
    grad_h2 = keep_ref[...].astype(F32) + got_ref[...].astype(F32)
    mid_copy.wait()
    normed2, scale2 = normalize_rows(mid_s[...].reshape(half, -1))
    part_ref[...] = jnp.broadcast_to(jnp.sum(grad_h2 * normed2, 0, keepdims=True), part_ref.shape)
    copy.wait()
    grad_final = cot_s[...].reshape(half, -1).astype(F32)
    grad_mid = grad_final + normal_back(grad_h2, normed2, scale2, gain2_ref[...])
    gmid_ref[...] = grad_mid
    ga_ref[...] = grad_mid.astype(BF16)
    ex_out[...] = ex_ref[...]


def run_mid_back(where, keep, got, mid, cot, gain2, ex, after):
    half, width = keep.shape
    outs = (sds((half, width), F32), sds((half, width), BF16), sds((8, width), F32), sds(ex.shape, BF16))
    return call(
        mid_back_kernel, outs, [pltpu.VMEM((half // STRIP, STRIP, width), dtype) for dtype in (BF16, F32)] + [pltpu.SemaphoreType.DMA((2,))],
        "mid_back", 4, limit=12,
        in_specs=[SMEM_SPEC, VMEM_SPEC, PLAIN_SPEC, FAR_ANY, FAR_ANY, VMEM_SPEC, VMEM_SPEC],
        out_specs=(FAR_SPEC, PLAIN_SPEC, VMEM_SPEC, FAR_SPEC), after=after,
    )(where, keep, got, in_strips(mid), in_strips(cot), gain2, ex)


def back_tiles(
    first_tile, last_tile, ends, side, own, q_s, do_s, lse_s, d_s, k_ref, v_ref, kt_ref,
    segk_s, qm_s, dm_s, dq_s, dk_s, dv_s,
):
    mine = kt_ref.shape[0]
    heads = mine // 64

    def place(index):
        return 2 * STRIP * (index // STRIP) + STRIP * side + index % STRIP

    def q_step(qb, carry):
        first = pl.multiple_of(qb * KB, KB)
        last = jnp.minimum(first + KB, own) - 1
        for h in range(heads):
            mask = head_mask(KB, h % 2)
            qm_s[h] = q_s[pl.ds(first, KB), lane_head(h)] * mask
            dm_s[h] = do_s[pl.ds(first, KB), lane_head(h)] * mask
        dq_s[:, pl.ds(first, KB)] = jnp.zeros((mine, KB), F32)
        low, high = seq_bounds(ends, place(first), place(last))
        start, steps = key_steps(low, high)
        index = lax.broadcasted_iota(jnp.int32, (8, KB), 1) + first
        segq = jnp.where(index < own, segment_of(place(index), ends), -1)[0:1]
        lse = [lse_s[h : h + 1, pl.ds(first, KB)] for h in range(heads)]
        dots = [d_s[h : h + 1, pl.ds(first, KB)] for h in range(heads)]

        def k_step(kb, carry):
            at = pl.multiple_of(start + kb * KB, LANES)
            bias = bias_block(segk_s, at, segq)
            s = [mm(k_ref[pl.ds(at, KB), lane_head(h)], qm_s[h], COLS_COLS) for h in range(heads)]
            dp = [mm(v_ref[pl.ds(at, KB), lane_head(h)], dm_s[h], COLS_COLS) for h in range(heads)]
            p = [jnp.exp((s[h] + bias) - lse[h]) for h in range(heads)]
            ds = [(p[h] * (dp[h] - dots[h])).astype(BF16) for h in range(heads)]
            p = [a.astype(BF16) for a in p]
            dv = [mm(p[h], dm_s[h]) for h in range(heads)]
            dk = [mm(ds[h], qm_s[h]) for h in range(heads)]
            dq = [mm(kt_ref[h * 64 : (h + 1) * 64, pl.ds(at, KB)], ds[h]) for h in range(heads)]
            for ref, add in ((dv_s, dv), (dk_s, dk)):
                for j in range(up(heads, 2) // 2):
                    pair = add[2 * j : 2 * j + 2]
                    ref[pl.ds(at, KB), j * LANES : (j + 1) * LANES] += pair[0] if len(pair) == 1 else pair[0] + pair[1]
            for h in range(heads):
                dq_s[h * 64 : (h + 1) * 64, pl.ds(first, KB)] += dq[h]
            return carry

        lax.fori_loop(0, steps, k_step, 0)
        return carry

    lax.fori_loop(first_tile, last_tile, q_step, 0)


def back_first_kernel(
    len_ref, where_ref, ga_ref, gao_ref, ho_any, q_any, lse_any, k_any, kt_any, v_any, hid_any, wproj_ref,
    ga_s, hid_s, ho_s, q_s, do_s, lse_s, d_s, dq_s, dk_s, dv_s,
    segk_s, qm_s, dm_s, col_s, k_ref, v_ref, kt_ref, hoc_s, lsec_s, qc_s, hidc_s, sems,
):
    half, width = ga_ref.shape
    own = 2 * half
    kpad = k_ref.shape[0]
    cpad = ga_s.shape[0]
    mine = kt_ref.shape[0]
    core, side = where_ref[0], where_ref[1]
    ends = seq_ends(len_ref, len_ref.shape[1])

    strips_of = (hoc_s, lsec_s, qc_s, hidc_s)
    copies = [
        strip_copy(ref, 0, side, dst, sems.at[i])
        for i, (ref, dst) in enumerate(zip((ho_any, lse_any, q_any, hid_any), strips_of))
    ] + [
        pltpu.make_async_copy(ref, dst, sems.at[4 + i])
        for i, (ref, dst) in enumerate(((k_any, k_ref), (v_any, v_ref), (kt_any, kt_ref)))
    ]
    for copy in copies:
        copy.start()
    key_segments(segk_s, ends, kpad)
    at = pl.multiple_of(core * half, GRAIN)
    ga_s[pl.ds(at, half), :] = ga_ref[...]
    at = pl.multiple_of((1 - core) * half, GRAIN)
    ga_s[pl.ds(at, half), :] = gao_ref[...]
    ga_s[own:cpad, :] = jnp.zeros((cpad - own, width), BF16)
    dk_s[...] = jnp.zeros(dk_s.shape, F32)
    dv_s[...] = jnp.zeros(dv_s.shape, F32)
    for copy in copies:
        copy.wait()
    for src, dst in zip(strips_of, (ho_s, col_s, q_s, hid_s)):
        dst[0:own, :] = src[0 : own // STRIP].reshape(own, -1)
        dst[own:cpad, :] = jnp.zeros((cpad - own, dst.shape[1]), dst.dtype)
    lse_s[...] = col_s[...].T[0:8]
    wproj = wproj_ref[pl.ds(pl.multiple_of(core * mine, GRAIN), mine), :]
    do_s[:, 0:mine] = mm(ga_s[...], wproj, COLS_COLS).astype(BF16)
    do_s[:, mine:] = jnp.zeros((cpad, do_s.shape[1] - mine), BF16)
    sub = lax.broadcasted_iota(jnp.int32, (8, do_s.shape[1]), 0)
    lane = lax.broadcasted_iota(jnp.int32, (8, do_s.shape[1]), 1)
    d_s[...] = lax.dot_general(
        (lane // 64 == sub).astype(F32),
        do_s[...].astype(F32) * ho_s[...].astype(F32),
        COLS_COLS,
        precision=lax.Precision.HIGHEST,
        preferred_element_type=F32,
    )

    back_tiles(
        0, FIRST_TILES, ends, side, own, q_s, do_s, lse_s, d_s, k_ref, v_ref, kt_ref,
        segk_s, qm_s, dm_s, dq_s, dk_s, dv_s,
    )


def back_second_kernel(
    len_ref, where_ref, k_any, kt_any, v_any, q_s, do_s, lse_s, d_s, dq_ref, dk_ref, dv_ref, w3_ref,
    hkeep_ref, hsend_ref, dqt_ref, dkt_ref, dvt_ref,
    segk_s, qm_s, dm_s, dq_s, dk_s, dv_s, gh_s, k_ref, v_ref, kt_ref, sems,
):
    own, width = hkeep_ref.shape
    rows = 2 * own
    kpad = k_ref.shape[0]
    cpad = q_s.shape[0]
    mine = w3_ref.shape[2]
    core, side = where_ref[0], where_ref[1]
    ends = seq_ends(len_ref, len_ref.shape[1])
    scale = 1.0 / math.sqrt(width // HEADS)
    copies = [
        pltpu.make_async_copy(ref, dst, sems.at[i])
        for i, (ref, dst) in enumerate(((k_any, k_ref), (v_any, v_ref), (kt_any, kt_ref)))
    ]
    for copy in copies:
        copy.start()
    key_segments(segk_s, ends, kpad)
    dq_s[...] = dq_ref[...]
    dk_s[...] = dk_ref[...]
    dv_s[...] = dv_ref[...]
    for copy in copies:
        copy.wait()
    back_tiles(
        FIRST_TILES, cpad // KB, ends, side, own, q_s, do_s, lse_s, d_s, k_ref, v_ref, kt_ref,
        segk_s, qm_s, dm_s, dq_s, dk_s, dv_s,
    )

    wq, wk, wv = w3_ref[0], w3_ref[1], w3_ref[2]
    dqt = (dq_s[...] * scale).astype(BF16)
    dqt_ref[...] = dqt
    step = rows // 8

    def h_body(i, carry):
        at = pl.ds(pl.multiple_of(i * step, GRAIN), step)
        gh_s[at, :] = mm(dk_s[at, 0:mine].astype(BF16), wk, COLS_COLS) + mm(
            dv_s[at, 0:mine].astype(BF16), wv, COLS_COLS
        )
        return carry

    lax.fori_loop(0, 8, h_body, 0)
    dkt_ref[...] = dk_s[...].astype(BF16).T[0:mine]
    dvt_ref[...] = dv_s[...].astype(BF16).T[0:mine]
    grad_q = mm(dqt.T, wq, COLS_COLS)
    for i in range(own // STRIP):
        at = pl.ds(strip_start(0, i, side), STRIP)
        gh_s[at, :] += grad_q[i * STRIP : (i + 1) * STRIP]
    hkeep_ref[...] = gh_s[pl.ds(pl.multiple_of(core * own, GRAIN), own), :].astype(BF16)
    hsend_ref[...] = gh_s[pl.ds(pl.multiple_of((1 - core) * own, GRAIN), own), :].astype(BF16)


def weight_kernel(
    dqt_ref, dkt_ref, dvt_ref, ga_ref, hidc_ref, hoc_ref, hid_any, groute_ref, gain2_ref, pay_ref, hid_ref, sem
):
    mine = dqt_ref.shape[0]
    width = ga_ref.shape[1]
    copy = pltpu.make_async_copy(hid_any, hid_ref, sem)
    copy.start()
    pay_ref[0:mine, :] = mm(dqt_ref[...], hidc_ref[...]).astype(BF16)
    pay_ref[3 * mine : 4 * mine, :] = mm(hoc_ref[...].T[0:mine], ga_ref[...]).astype(BF16)
    copy.wait()
    pay_ref[mine : 2 * mine, :] = mm(dkt_ref[...], hid_ref[...]).astype(BF16)
    pay_ref[2 * mine : 3 * mine, :] = mm(dvt_ref[...], hid_ref[...]).astype(BF16)
    pay_ref[4 * mine : 4 * mine + 8, :] = groute_ref[...].T[0:8].astype(BF16)
    pay_ref[4 * mine + 8 : 4 * mine + 16, :] = gain2_ref[...].astype(BF16)
    pay_ref[4 * mine + 16 :, :] = jnp.zeros((pay_ref.shape[0] - 4 * mine - 16, width), BF16)


def run_weights(pay_rows, dqt, dkt, dvt, ga, hidc, hoc, hid, groute, gain2, after):
    return call(
        weight_kernel, sds((pay_rows, ga.shape[1]), BF16),
        [pltpu.VMEM(hid.shape, BF16), pltpu.SemaphoreType.DMA], "weights", 4, limit=16,
        in_specs=[VMEM_SPEC] * 6 + [FAR_ANY] + [VMEM_SPEC] * 2, out_specs=PLAIN_SPEC, after=after,
    )(dqt, dkt, dvt, ga, hidc, hoc, hid, groute, gain2)


def run_back_first(lengths, where, ga, gao, ho, q, lse, k, kt, v, hid, wproj, after):
    half, width = ga.shape
    own = 2 * half
    kpad, lanes = k.shape
    mine = kt.shape[0]
    heads = mine // 64
    cpad = up(own, KB)
    outs = (
        sds((cpad, width), BF16),
        sds((cpad, width), BF16),
        sds((cpad, lanes), BF16),
        sds((cpad, lanes), BF16),
        sds((cpad, lanes), BF16),
        sds((8, cpad), F32),
        sds((8, cpad), F32),
        sds((mine, cpad), F32),
        sds((kpad, lanes), F32),
        sds((kpad, lanes), F32),
    )
    scratch = [
        pltpu.VMEM((kpad, LANES), jnp.int32),
        pltpu.VMEM((heads, KB, LANES), BF16),
        pltpu.VMEM((heads, KB, LANES), BF16),
        pltpu.VMEM((cpad, LANES), F32),
        pltpu.VMEM((kpad, lanes), BF16),
        pltpu.VMEM((kpad, lanes), BF16),
        pltpu.VMEM((mine, kpad), BF16),
        pltpu.VMEM((own // STRIP, STRIP, lanes), BF16),
        pltpu.VMEM((own // STRIP, STRIP, LANES), F32),
        pltpu.VMEM((own // STRIP, STRIP, lanes), BF16),
        pltpu.VMEM((own // STRIP, STRIP, width), BF16),
        pltpu.SemaphoreType.DMA((7,)),
    ]
    return call(
        back_first_kernel, outs, scratch, "back_first", 14,
        in_specs=[SMEM_SPEC, SMEM_SPEC, PLAIN_SPEC, PLAIN_SPEC] + [FAR_ANY] * 7 + [PLAIN_SPEC],
        out_specs=(VMEM_SPEC,) * 10, limit=24, after=after,
    )(lengths, where, ga, gao, in_strips(ho), in_strips(q), in_strips(lse), k, kt, v, in_strips(hid), wproj)


def run_back_second(own, lengths, where, k, kt, v, q, do, lse, dots, dq, dk, dv, w3, after):
    kpad, lanes = k.shape
    mine = kt.shape[0]
    heads = mine // 64
    cpad = q.shape[0]
    width = w3.shape[1]
    outs = (
        sds((own, width), BF16),
        sds((own, width), BF16),
        sds((mine, cpad), BF16),
        sds((mine, kpad), BF16),
        sds((mine, kpad), BF16),
    )
    scratch = [
        pltpu.VMEM((kpad, LANES), jnp.int32),
        pltpu.VMEM((heads, KB, LANES), BF16),
        pltpu.VMEM((heads, KB, LANES), BF16),
        pltpu.VMEM((mine, cpad), F32),
        pltpu.VMEM((kpad, lanes), F32),
        pltpu.VMEM((kpad, lanes), F32),
        pltpu.VMEM((2 * own, width), F32),
        pltpu.VMEM((kpad, lanes), BF16),
        pltpu.VMEM((kpad, lanes), BF16),
        pltpu.VMEM((mine, kpad), BF16),
        pltpu.SemaphoreType.DMA((3,)),
    ]
    return call(
        back_second_kernel, outs, scratch, "back_second", 14,
        in_specs=[SMEM_SPEC, SMEM_SPEC] + [FAR_ANY] * 3 + [VMEM_SPEC] * 7 + [PLAIN_SPEC],
        out_specs=(FAR_SPEC, PLAIN_SPEC) + (VMEM_SPEC,) * 3, limit=24, after=after,
    )(lengths, where, k, kt, v, q, do, lse, dots, dq, dk, dv, w3)


def token_kernel(where_ref, mine_ref, got_ref, gmid_ref, tok_ref, gain1_ref, out_ref, tok_s, sem):
    half = gmid_ref.shape[0]
    copy = strip_copy(tok_ref, where_ref[0] * (half // STRIP), where_ref[1], tok_s, sem)
    copy.start()
    grad_h1 = mine_ref[...].astype(F32) + got_ref[...].astype(F32)
    copy.wait()
    normed1, scale1 = normalize_rows(tok_s[...].reshape(half, -1).astype(F32))
    out_ref[...] = (gmid_ref[...] + normal_back(grad_h1, normed1, scale1, gain1_ref[...])).astype(BF16)


def run_tokens(where, mine, got, gmid, tokens, gain1, after):
    return call(
        token_kernel, sds(gmid.shape, BF16),
        [pltpu.VMEM((gmid.shape[0] // STRIP, STRIP, gmid.shape[1]), BF16), pltpu.SemaphoreType.DMA], "token_grad", 3, limit=12,
        in_specs=[SMEM_SPEC, FAR_SPEC, PLAIN_SPEC, FAR_SPEC, FAR_ANY, VMEM_SPEC], out_specs=PLAIN_SPEC, after=after,
    )(where, mine, got, gmid, in_strips(tokens), gain1)


def split_kernel(where_ref, a_ref, b_ref, keep_ref, send_ref):
    half = keep_ref.shape[0]
    total = (a_ref[...].astype(F32) + b_ref[...].astype(F32)).astype(BF16)
    side = where_ref[1]
    first, second = strips(total, 0, half), strips(total, 1, half)
    keep_ref[...] = jnp.where(side == 0, first, second)
    send_ref[...] = jnp.where(side == 0, second, first)


def run_split(where, a, b, after):
    own, width = a.shape
    outs = (sds((own // 2, width), BF16),) * 2
    return call(
        split_kernel, outs, [], "split", 2, limit=12, in_specs=[SMEM_SPEC, FAR_SPEC, PLAIN_SPEC],
        out_specs=(FAR_SPEC, PLAIN_SPEC), after=after,
    )(where, a, b)


def weave_kernel(where_ref, mine_ref, other_ref, out_ref):
    side = where_ref[1]
    for i in range(mine_ref.shape[0] // STRIP):
        rows = slice(i * STRIP, (i + 1) * STRIP)
        out_ref[pl.ds(strip_start(0, i, side), STRIP), :] = mine_ref[rows, :]
        out_ref[pl.ds(strip_start(0, i, 1 - side), STRIP), :] = other_ref[rows, :]


def run_weave(where, mine, other, after):
    half, width = mine.shape
    return call(
        weave_kernel, sds((2 * half, width), BF16), [], "weave", 2, limit=8,
        in_specs=[SMEM_SPEC] + [PLAIN_SPEC] * 2, out_specs=PLAIN_SPEC, after=after,
    )(where, mine, other)


def summed_end_kernel(total_ref, gin_ref, gout_ref):
    gin_ref[0] = total_ref[0, 0].astype(F32)
    gout_ref[0] = total_ref[0, 1].astype(F32)


def run_summed_end(total, shape_in, shape_out, after):
    size, unused, width, hidden = total.shape
    block = pl.BlockSpec((1, width, hidden), lambda e: (e, 0, 0))
    return call(
        summed_end_kernel,
        (sds(shape_in, F32), sds(shape_out, F32)),
        [],
        "summed_end",
        4, limit=12,
        grid=(size,),
        in_specs=[pl.BlockSpec((1, 2, width, hidden), lambda e: (e, 0, 0, 0))],
        out_specs=(block, block),
        after=after,
    )(total)


def expert_end_kernel(where_ref, mine_ref, other_ref, *refs):
    gin_ref, gout_ref = refs[-2:]
    e = pl.program_id(0)
    mine = mine_ref[e].astype(F32)
    other = other_ref[e].astype(F32)
    first = where_ref[2] == 0
    gin_ref[0] = jnp.where(first, mine, other)
    gout_ref[0] = jnp.where(first, other, mine)


def run_expert_end(at, where, mine, other, shape_in, shape_out, before):
    size, width, hidden = mine.shape
    block = pl.BlockSpec((1, width, hidden), lambda e: (e + at, 0, 0))
    return call(
        expert_end_kernel,
        (sds(shape_in, F32), sds(shape_out, F32)),
        [],
        "expert_end",
        3, limit=12,
        grid=(size,),
        in_specs=[SMEM_SPEC, PLAIN_SPEC, PLAIN_SPEC] + [FAR_ANY] * 2,
        out_specs=(block, block),
        input_output_aliases={3: 0, 4: 1},
    )(where, mine, other, *before)


def total_kernel(parts_ref, out_ref):
    pieces = parts_ref.shape[0]
    total = parts_ref[0].astype(F32)
    for i in range(1, pieces):
        total = total + parts_ref[i].astype(F32)
    total = total.astype(BF16)
    for i in range(pieces):
        out_ref[i] = total


def run_total(parts, after):
    return call(
        total_kernel, sds(parts.shape, BF16), [], "total", 2, limit=8, in_specs=[PLAIN_SPEC], out_specs=PLAIN_SPEC, after=after
    )(parts)


def attn_end_kernel(where_ref, mine_ref, other_ref, wqkv_ref, gain1_ref, gqkv_ref, gproj_ref, g1_ref, g2_ref, groute_ref):
    width = wqkv_ref.shape[1]
    share = width // 2
    first = where_ref[0] == 0
    mine = mine_ref[...].astype(F32)
    other = other_ref[...].astype(F32)
    low = jnp.where(first, mine, other)
    high = jnp.where(first, other, mine)
    product = jnp.zeros((width, width), F32)
    for i in range(3):
        rows = slice(i * share, (i + 1) * share)
        part = jnp.concatenate([low[rows], high[rows]], 0).T
        gqkv_ref[i] = part
        product = product + part * wqkv_ref[i].astype(F32)
    gproj_ref[...] = jnp.concatenate([low[3 * share : 4 * share], high[3 * share : 4 * share]], 0)
    g1_ref[...] = (jnp.sum(product.T, 0, keepdims=True) / gain1_ref[...])[0]
    small = low[4 * share : 4 * share + 16] + high[4 * share : 4 * share + 16]
    groute_ref[...] = small[0:8]
    g2_ref[...] = small[8]


def run_attn_end(where, mine, other, wqkv, gain1, after):
    width = wqkv.shape[1]
    outs = (
        sds((3, width, width), F32),
        sds((width, width), F32),
        sds((width,), F32),
        sds((width,), F32),
        sds((8, width), F32),
    )
    return call(
        attn_end_kernel, outs, [], "attn_end", 4, limit=16, in_specs=[SMEM_SPEC, PLAIN_SPEC, PLAIN_SPEC, VMEM_SPEC, VMEM_SPEC],
        out_specs=(FAR_SPEC,) * 5, after=after,
    )(where, mine, other, wqkv, gain1)


def swap(value, axis, mask):
    size = lax.axis_size(axis)
    return lax.ppermute(value, axis, [(i, i ^ mask) for i in range(size)])


def add_kernel(a_ref, b_ref, out_ref):
    out_ref[...] = (a_ref[...].astype(F32) + b_ref[...].astype(F32)).astype(BF16)


def added(a, b, after):
    return call(
        add_kernel, sds(a.shape, BF16), [], "add", 2, limit=8, in_specs=[PLAIN_SPEC] * 2, out_specs=PLAIN_SPEC, after=after
    )(a, b)


def choose_kernel(where_ref, inner_ref, outer_ref, out_ref):
    @pl.when(where_ref[3] == 0)
    def _():
        out_ref[...] = inner_ref[...]

    @pl.when(where_ref[3] != 0)
    def _():
        out_ref[...] = outer_ref[...]


def chosen(where, inner, outer, after):
    return call(
        choose_kernel, sds(inner.shape, BF16), [], "choose", 2, limit=8,
        in_specs=[SMEM_SPEC, PLAIN_SPEC, PLAIN_SPEC], out_specs=PLAIN_SPEC, after=after,
    )(where, inner, outer)


def wide_step(value, step):
    inward = [(w, w + 2) for w in (0, 1)] + [(w, w - 2) for w in (6, 7)]
    if step == 0:
        return lax.ppermute(value, "wide", inward)
    if step == 1:
        return lax.ppermute(value, "wide", [(2, 4), (3, 5), (4, 2), (5, 3)])
    return lax.ppermute(value, "wide", [(b, a) for a, b in inward])


def on_device(
    tokens, w_qkv, w_proj, norm1_gain, norm2_gain, w_route, w_in, w_out, cotangent, routes, kept_mask, lengths
):
    rows, width = tokens.shape
    own, half = rows // 2, rows // 4
    experts = w_in.shape[0]
    core, side = lax.axis_index("lo"), lax.axis_index("hi")
    wide_size, w = lax.axis_size("wide"), lax.axis_index("wide")
    z = w // 2
    outer = ((z == 0) | (z == wide_size // 2 - 1)).astype(jnp.int32)
    where = jnp.stack([core, side, w % 2, outer]).astype(jnp.int32)

    wqkv = w_qkv.transpose(1, 0, 2)
    w3 = lax.dynamic_slice_in_dim(wqkv, core * (width // 2), width // 2, 2)
    wr = jnp.pad(w_route, ((0, 0), (0, LANES - experts)))
    gain1 = norm1_gain.reshape(1, width)
    gain2 = norm2_gain.reshape(1, width)
    code = jnp.where(kept_mask == 1, routes[:, 0], experts).reshape(2, 1, own)
    code = jnp.pad(code, ((0, 0), (0, 0), (0, up(own, LANES) - own)), constant_values=experts)

    hid, k, kt, v, q, ho, lse, keep, send = run_front(lengths, where, tokens, w3, w_proj, gain1)
    got = swap(send, "lo", 1)
    plan, pos = run_plan(where, code, (keep, ANY_SPEC))
    mid, own_x, own_send = run_mid(where, keep, got, tokens, cotangent, gain2, wr, code, pos)
    oth_x = swap(own_send, "lo", 1)

    yown, yoth, groute, grads_a, *pairs = run_experts(plan, where, own_x, oth_x, w_in, w_out, wr)
    got = swap(yoth, "lo", 1)
    total_a = lax.psum(grads_a, "wide")
    pairs = [(pairs[2 * i], pairs[2 * i + 1]) for i in range(len(pairs) // 2)]
    recvs = [swap(give, "wide", 1) for unused, give in pairs]

    unpick = run_unpick(pos, own, own_x.shape[0], (yoth, ANY_SPEC))
    keep, send = run_unsort(where, yown, got, unpick)
    gh2 = swap(send, "hi", 1)
    ex = run_unsort_out(yown, got, pos, own, (send, ANY_SPEC))
    sums, moved = [], []
    for mine, unused in pairs:
        sums.append(mine)
    line = wide_size == 8

    def add_step(i, recv, after):
        sums[i] = added(sums[i], recv, after)
        return sums[i], ANY_SPEC

    def first_step(i, after):
        after = add_step(i, recvs[i], after)
        if line:
            moved.append(wide_step(sums[i], 0))
        else:
            for j in range(1, wide_size.bit_length() - 1):
                after = add_step(i, swap(sums[i], "wide", 1 << j), after)
        return after

    def line_step(i, step, after):
        if line:
            after = add_step(i, moved[i], after)
            moved[i] = wide_step(sums[i], step)
        return after

    def last_step(i, after):
        if line:
            sums[i] = chosen(where, sums[i], moved[i], after)
            after = sums[i], ANY_SPEC
        others.append(swap(sums[i], "wide", 1))
        return after

    others = []
    gmid, ga, gain2_part, ex = run_mid_back(where, keep, gh2, mid, cotangent, gain2, ex, (ex, VMEM_SPEC))
    gao = swap(ga, "lo", 1)
    ex_got = swap(ex, "hi", 1)
    last = first_step(0, (ex, FAR_ANY))

    ga_c, hid_c, ho_c, *state = run_back_first(lengths, where, ga, gao, ho, q, lse, k, kt, v, hid, w_proj, last)
    last = ga_c, VMEM_SPEC
    last = first_step(1, last)
    last = line_step(0, 1, last)
    last = first_step(2, last)
    hkeep, hsend, dqt, dkt, dvt = run_back_second(own, lengths, where, k, kt, v, *state, w3, last)
    hgot = swap(hsend, "lo", 1)
    last = hsend, ANY_SPEC
    last = line_step(0, 2, last)
    last = line_step(1, 1, last)
    last = line_step(2, 1, last)
    pay_rows = up(2 * width + 16, 8 * lax.axis_size(("wide", "hi")))
    pay = run_weights(pay_rows, dqt, dkt, dvt, ga_c, hid_c, ho_c, hid, groute, gain2_part, last)
    share = pay_rows // lax.axis_size(("wide", "hi"))
    pay_got = lax.all_to_all(pay.reshape(-1, share, width), ("wide", "hi"), 0, 0)
    last = pay, ANY_SPEC
    last = line_step(1, 2, last)
    hk, hs = run_split(where, hkeep, hgot, last)
    hs_got = swap(hs, "hi", 1)
    out_own = run_out(mid, ex, ex_got, (hs, ANY_SPEC))
    out_oth = swap(out_own, "lo", 1)
    last = last_step(0, (out_own, ANY_SPEC))
    last = line_step(2, 2, last)
    token_rows = run_tokens(where, hk, hs_got, gmid, tokens, gain1, last)
    token_got = swap(token_rows, "hi", 1)
    last = last_step(1, (token_rows, ANY_SPEC))
    pay_got = run_total(pay_got, last)
    last = pay_got, ANY_SPEC
    pay_got = lax.all_to_all(pay_got, ("wide", "hi"), 0, 0).reshape(pay.shape)
    layer_out = run_join(where, out_own, out_oth, last)
    token_own = run_weave(where, token_rows, token_got, (layer_out, FAR_ANY))
    token_oth = swap(token_own, "lo", 1)
    last = last_step(2, (token_own, ANY_SPEC))
    before = run_summed_end(total_a, w_in.shape, w_out.shape, last)
    at = PARTS[0]
    before = run_expert_end(at, where, sums[0], others[0], w_in.shape, w_out.shape, before)
    grad_tokens = run_join(where, token_own, token_oth, (before[0], FAR_ANY))
    before = run_expert_end(at + PARTS[1], where, sums[1], others[1], w_in.shape, w_out.shape, before)
    pay_oth = swap(pay_got, "lo", 1)
    grad_qkv, grad_proj, grad_norm1, grad_norm2, route_t = run_attn_end(
        where, pay_got, pay_oth, wqkv, gain1, (before[0], FAR_ANY)
    )
    grad_in, grad_out = run_expert_end(
        at + PARTS[1] + PARTS[2], where, sums[2], others[2], w_in.shape, w_out.shape, before
    )

    return (
        layer_out,
        grad_tokens,
        grad_qkv.transpose(1, 0, 2),
        grad_proj,
        grad_norm1,
        grad_norm2,
        route_t.T,
        grad_in,
        grad_out,
    )


def solution(mesh):
    axes = ("wide", ("hi", "lo"))
    split = Mesh(mesh.devices.reshape(mesh.shape["wide"], -1, 2), ("wide", "hi", "lo"))
    wide, narrow = axes
    in_specs = (
        P(wide, None),
        P(),
        P(),
        P(),
        P(),
        P(),
        P(None, None, narrow),
        P(None, narrow, None),
        P(wide, None),
        P(wide, None),
        P(wide),
        P(wide, None),
    )
    out_specs = (
        P(wide, None),
        P(wide, None),
        P(),
        P(),
        P(),
        P(),
        P(),
        P(None, None, narrow),
        P(None, narrow, None),
    )
    return jax.shard_map(on_device, mesh=split, in_specs=in_specs, out_specs=out_specs, check_vma=False)
```
